32 devices in a mesh: dp: 16 (over z, y, core), mp: 2 (over x).
Axes of the slice: x: 2, y: 2, z: 4, core: 2. Of those that a mesh axis runs over, the one named last changes fastest.
Arguments:
- tokens: bfloat16 [8192, 1536], P(('dp', 'mp')), may hold values from -6 to 6
- seq_lengths: int32 [16, 3], P('dp'), may hold values from 0 to 512, as said below
- norm_attn: bfloat16 [1536], replicated, may hold values from 0.5 to 1.5
- w_query: bfloat16 [1536, 1536], P('dp', 'mp'), may hold values from -0.15625 to 0.15625
- key_weight: bfloat16 [1536, 768], P('dp', 'mp'), may hold values from -0.15625 to 0.15625
- value_weight: bfloat16 [1536, 768], P('dp', 'mp'), may hold values from -0.15625 to 0.15625
- w_out: bfloat16 [1536, 1536], P('mp', 'dp'), may hold values from -2.5 to 2.5
- norm_mlp: bfloat16 [1536], replicated, may hold values from 0.5 to 1.5
- w_gate: bfloat16 [1536, 4096], P('dp', 'mp'), may hold values from -0.15625 to 0.15625
- w_up: bfloat16 [1536, 4096], P('dp', 'mp'), may hold values from -0.15625 to 0.15625
- w_down: bfloat16 [4096, 1536], P('mp', 'dp'), may hold values from -0.09375 to 0.09375
- cotangent: bfloat16 [8192, 1536], P(('dp', 'mp')), may hold values from -6 to 6
Outputs:
- block_out: bfloat16 [8192, 1536], P(('dp', 'mp'))
- grad_tokens: bfloat16 [8192, 1536], P(('dp', 'mp'))
- grad_norm_attn: float32 [1536], replicated
- grad_w_query: float32 [1536, 1536], P('dp', 'mp')
- grad_w_key: float32 [1536, 768], P('dp', 'mp')
- grad_w_value: float32 [1536, 768], P('dp', 'mp')
- grad_w_out: float32 [1536, 1536], P('mp', 'dp')
- grad_norm_mlp: float32 [1536], replicated
- grad_w_gate: float32 [1536, 4096], P('dp', 'mp')
- grad_w_up: float32 [1536, 4096], P('dp', 'mp')
- grad_w_down: float32 [4096, 1536], P('mp', 'dp')
The draws below stay inside these ranges and needn't reach their ends.
Inputs may be any that keep to these rules, and one draw needn't show every extreme that they name: `seq_lengths`: row g lists three sequences packed in that order at the start of token group g; the rest of the group is padding. A zero length means that sequence is absent. The middle sequence starts in the first 256 rows of the group and ends in its last 256 rows; some group is one sequence of 512 tokens.
All inputs are finite; a program needn't handle non-finite values.
Results may differ from the reference program's by a relative error of at most 0.02.
Values may be sent and summed in bfloat16 or wider, within the bound.
A program may use at most 192 MiB of HBM per device.

```python
import jax
import jax.numpy as jnp
from jax import lax

MODEL_WIDTH = 1536
FF = 4096
QUERY_HEADS = 16
KEY_VALUE_HEADS = 8
HEAD_SIZE = 96
TOK_DEV = 256
GROUP = 512
TOKENS = 8192
N_DP = 16


def draw_seq_lengths(key, part):
    key = jax.random.fold_in(key, 7)
    key_head, key_tail, key_pad, key_pick = jax.random.split(key, 4)
    head_len = jax.random.randint(key_head, (N_DP,), 0, TOK_DEV // 2 + 1)
    tail_len = jax.random.randint(key_tail, (N_DP,), 0, TOK_DEV // 2 + 1)
    pad_len = jax.random.randint(key_pick, (N_DP,), 0, TOK_DEV // 4 + 1)
    chosen = jax.random.randint(key_pad, (), 0, N_DP)
    single = jnp.arange(N_DP) == chosen
    head_len = jnp.where(single, 0, head_len)
    tail_len = jnp.where(single, 0, tail_len)
    pad_len = jnp.where(single, 0, pad_len)
    middle_len = GROUP - head_len - tail_len - pad_len
    return jnp.stack([head_len, middle_len, tail_len], axis=1).astype(jnp.int32)


def level_of(stream_key, shape, pieces, smallest, top_value):
    def one(axis_at, blocks):
        heights = jax.random.uniform(jax.random.fold_in(jax.random.fold_in(stream_key, 6), axis_at), (blocks,), jnp.float32, smallest / len(pieces), top_value / len(pieces))
        return jnp.repeat(jnp.exp(heights), shape[axis_at] // blocks).reshape((-1,) + (1,) * (len(shape) - axis_at - 1))

    gain = one(*pieces[0])
    for cut in pieces[1:]:
        gain = gain * one(*cut)
    return gain


def centred(own_key, dims, spread, reach, pieces=(), kind=jnp.bfloat16):
    array = jax.random.normal(own_key, dims, jnp.float32) * spread
    if len(pieces) > 0:
        array = level_of(own_key, dims, pieces, -0.22, 0.18) * array
    return jnp.clip(array, min=-reach, max=reach).astype(kind)


def setup_inputs(seed: int = 0) -> dict:
    arg_keys = jax.random.split(jax.random.key(seed), 13)
    return {
        "tokens": centred(arg_keys[0], (TOKENS, MODEL_WIDTH), 1.0, 6.0, ((0, 32),)),
        "seq_lengths": draw_seq_lengths(jax.random.fold_in(arg_keys[12], 71), 0),
        "norm_attn": jnp.clip(1.0 + 0.1 * jax.random.normal(arg_keys[2], (MODEL_WIDTH,), jnp.float32), 0.5, 1.5).astype(jnp.bfloat16),
        "w_query": centred(arg_keys[3], (MODEL_WIDTH, MODEL_WIDTH), MODEL_WIDTH ** -0.5, 0.15625, ((0, 16), (1, 2))),
        "key_weight": centred(arg_keys[4], (MODEL_WIDTH, KEY_VALUE_HEADS * HEAD_SIZE), MODEL_WIDTH ** -0.5, 0.15625, ((0, 16), (1, 2))),
        "value_weight": centred(arg_keys[5], (MODEL_WIDTH, KEY_VALUE_HEADS * HEAD_SIZE), MODEL_WIDTH ** -0.5, 0.15625, ((0, 16), (1, 2))),
        "w_out": centred(arg_keys[6], (MODEL_WIDTH, MODEL_WIDTH), (MODEL_WIDTH // 256) ** -0.5, 2.5, ((0, 2), (1, 16))),
        "norm_mlp": jnp.clip(1.0 + 0.1 * jax.random.normal(arg_keys[7], (MODEL_WIDTH,), jnp.float32), 0.5, 1.5).astype(jnp.bfloat16),
        "w_gate": centred(arg_keys[8], (MODEL_WIDTH, FF), MODEL_WIDTH ** -0.5, 0.15625, ((0, 16), (1, 2))),
        "w_up": centred(arg_keys[9], (MODEL_WIDTH, FF), MODEL_WIDTH ** -0.5, 0.15625, ((0, 16), (1, 2))),
        "w_down": centred(arg_keys[10], (FF, MODEL_WIDTH), FF ** -0.5, 0.09375, ((0, 2), (1, 16))),
        "cotangent": centred(arg_keys[11], (TOKENS, MODEL_WIDTH), 1.0, 6.0, ((0, 32),)),
    }


EPSILON = 1e-05
ROPE_BASE = 100000.0
MASKED = -1e+30

@jax.custom_vjp
def precision_cast(v):
    return lax.optimization_barrier(v.astype(jnp.bfloat16)).astype(jnp.float32)

@jax.custom_vjp
def precision_cast_backward(v):
    return v

def low_keep(v):
    return (precision_cast(v), None)

def low_pass(kept, grad):
    return (grad,)

def back_keep(v):
    return (v, None)

def back_low(kept, grad):
    return (precision_cast(grad),)
precision_cast.defvjp(low_keep, low_pass)
precision_cast_backward.defvjp(back_keep, back_low)

def matrix_product(left_op, right_op):
    return jnp.dot(left_op, right_op, precision=lax.Precision.HIGHEST)

def layout(lengths, rows_total):
    places = jnp.arange(rows_total, dtype=jnp.int32)
    first_end = lengths[0]
    middle_end = lengths[0] + lengths[1]
    last_end = middle_end + lengths[2]
    segment = jnp.where(places < first_end, 0, jnp.where(places < middle_end, 1, jnp.where(places < last_end, 2, -1))).astype(jnp.int32)
    offset = jnp.where(places < first_end, 0, jnp.where(places < middle_end, first_end, middle_end))
    position = jnp.where(segment >= 0, places - offset, 0).astype(jnp.int32)
    return (segment, position)

def rotation(position):
    half_dim = HEAD_SIZE // 2
    inverse = ROPE_BASE ** (-jnp.arange(half_dim, dtype=jnp.float32) * 2.0 / HEAD_SIZE)
    angles = position.astype(jnp.float32)[:, None] * inverse[None, :]
    return (jnp.cos(angles)[:, None, :], jnp.sin(angles)[:, None, :])

def apply_rotary(tensor, cosine_table, sine_lookup_table):
    half_dim = tensor.shape[-1] // 2
    lead_half = tensor[..., :half_dim]
    tail_half = tensor[..., half_dim:]
    return jnp.concatenate([lead_half * cosine_table - tail_half * sine_lookup_table, tail_half * cosine_table + lead_half * sine_lookup_table], axis=-1)

def rms_norm(inputs, gain_vec):
    factor = lax.rsqrt(lax.optimization_barrier(jnp.mean(inputs * inputs, axis=-1, keepdims=True)) + EPSILON)
    return inputs * factor * gain_vec

def forward(block_x, gain_one, query_w, key_matrix, value_matrix, out_w, gain_two, gate_w, up_w, down_w, segment, position):
    row_total_count = block_x.shape[0]
    group_member_count = QUERY_HEADS // KEY_VALUE_HEADS
    first_normed_rows = precision_cast(rms_norm(block_x, gain_one))
    query_unrotated = precision_cast_backward(matrix_product(first_normed_rows, query_w)).reshape(row_total_count, QUERY_HEADS, HEAD_SIZE)
    key_unrotated = precision_cast_backward(matrix_product(first_normed_rows, key_matrix)).reshape(row_total_count, KEY_VALUE_HEADS, HEAD_SIZE)
    value_activation = precision_cast(precision_cast_backward(matrix_product(first_normed_rows, value_matrix))).reshape(row_total_count, KEY_VALUE_HEADS, HEAD_SIZE)
    cosine_table, sine_lookup_table = rotation(position)
    query_rotated = precision_cast(apply_rotary(query_unrotated, cosine_table, sine_lookup_table)).reshape(row_total_count, KEY_VALUE_HEADS, group_member_count, HEAD_SIZE)
    key_rot = precision_cast(apply_rotary(key_unrotated, cosine_table, sine_lookup_table))
    places = jnp.arange(row_total_count, dtype=jnp.int32)
    allowed = (places[:, None] >= places[None, :]) & (segment[:, None] == segment[None, :]) & ((segment[None, :] >= 0) | (places[:, None] == places[None, :]))
    raw_scores = jnp.einsum('qhgd,khd->hgqk', query_rotated, key_rot, precision=lax.Precision.HIGHEST) * HEAD_SIZE ** (-0.5)
    scores = jnp.where(allowed[None, None], precision_cast_backward(raw_scores), MASKED)
    row_max = lax.optimization_barrier(jnp.max(scores, axis=-1, keepdims=True))
    exp_scores = jnp.exp(scores - row_max)
    attn_probs = precision_cast(exp_scores / lax.optimization_barrier(jnp.sum(exp_scores, axis=-1, keepdims=True)))
    mixed_out = jnp.einsum('hgqk,khd->qhgd', attn_probs, value_activation, precision=lax.Precision.HIGHEST).reshape(row_total_count, MODEL_WIDTH)
    attended = precision_cast(precision_cast_backward(mixed_out))
    residual = block_x + precision_cast_backward(matrix_product(attended, out_w))
    normed_two = precision_cast(rms_norm(residual, gain_two))
    gate_act = precision_cast_backward(matrix_product(normed_two, gate_w))
    up_act = precision_cast_backward(matrix_product(normed_two, up_w))
    hidden = precision_cast(jax.nn.silu(gate_act) * up_act)
    return residual + matrix_product(hidden, down_w)

def reference(tokens, seq_lengths, norm_attn, w_query, key_weight, value_weight, w_out, norm_mlp, w_gate, w_up, w_down, cotangent):
    weights = tuple((element.astype(jnp.float32) for element in (norm_attn, w_query, key_weight, value_weight, w_out, norm_mlp, w_gate, w_up, w_down)))
    inputs = tokens.astype(jnp.float32).reshape(N_DP, GROUP, MODEL_WIDTH)
    grads_in = cotangent.astype(jnp.float32).reshape(N_DP, GROUP, MODEL_WIDTH)

    def group_step(totals, element):
        block_in, block_grad, lengths = element
        segment, position = layout(lengths, GROUP)

        def apply_block(block_x, *params):
            return forward(block_x, *params, segment, position)
        result, pullback = jax.vjp(apply_block, block_in, *weights)
        gradients = pullback(block_grad)
        totals = tuple((running + fresh for running, fresh in zip(totals, gradients[1:])))
        return (totals, (result.astype(jnp.bfloat16), gradients[0].astype(jnp.bfloat16)))
    initial = tuple((jnp.zeros_like(element) for element in weights))
    totals, (outputs, grad_input) = lax.scan(group_step, initial, (inputs, grads_in, seq_lengths))
    return (outputs.reshape(TOKENS, MODEL_WIDTH), grad_input.reshape(TOKENS, MODEL_WIDTH), totals[0], totals[1], totals[2], totals[3], totals[4], totals[5], totals[6], totals[7], totals[8])
```

```python
import jax
import jax.numpy as jnp
from jax import lax
from jax.sharding import PartitionSpec as P

HEAD_SIZE = 96
EPSILON = 1e-05
ROPE_BASE = 100000.0
MASKED = -1e30
F32 = jnp.float32
BF16 = jnp.bfloat16


def layout(lengths, rows_total):
    places = jnp.arange(rows_total, dtype=jnp.int32)
    first_end = lengths[0]
    middle_end = lengths[0] + lengths[1]
    last_end = middle_end + lengths[2]
    segment = jnp.where(
        places < first_end,
        0,
        jnp.where(places < middle_end, 1, jnp.where(places < last_end, 2, -1)),
    ).astype(jnp.int32)
    offset = jnp.where(places < first_end, 0, jnp.where(places < middle_end, first_end, middle_end))
    position = jnp.where(segment >= 0, places - offset, 0)
    return segment, position


def rotation(position):
    half_dim = HEAD_SIZE // 2
    inverse = ROPE_BASE ** (-jnp.arange(half_dim, dtype=F32) * 2.0 / HEAD_SIZE)
    angles = position.astype(F32)[:, None] * inverse[None, :]
    return jnp.cos(angles)[:, None, :], jnp.sin(angles)[:, None, :]


def rotate(tensor, cosine, sine):
    half_dim = tensor.shape[-1] // 2
    lead, tail = tensor[..., :half_dim], tensor[..., half_dim:]
    return jnp.concatenate([lead * cosine - tail * sine, tail * cosine + lead * sine], axis=-1)


def rms_parts(inputs):
    factor = lax.rsqrt(jnp.mean(inputs * inputs, axis=-1, keepdims=True) + EPSILON)
    return factor, inputs * factor


def rms_back(inputs, gain, gradient):
    factor, normed = rms_parts(inputs)
    gain_grad = jnp.sum(gradient * normed, axis=0)
    scaled = gradient * gain
    return (
        factor * (scaled - normed * jnp.mean(scaled * normed, axis=-1, keepdims=True)),
        gain_grad,
    )


def mul(left, right):
    return jnp.dot(left, right, preferred_element_type=F32)


def mul_t(left, right):
    return lax.dot_general(left, right, (((1,), (1,)), ((), ())), preferred_element_type=F32)


def outer_sum(left, right):
    return lax.dot_general(left, right, (((0,), (0,)), ((), ())), preferred_element_type=F32)


def mp_shift(block, step, parts):
    return lax.ppermute(block, "mp", [(i, (i + step) % parts) for i in range(parts)])


def mp_gather(block, parts):
    me = lax.axis_index("mp")
    rows = block.shape[0]
    whole = jnp.zeros((parts * rows,) + block.shape[1:], block.dtype)
    for step in range(parts):
        piece = block if step == 0 else mp_shift(block, step, parts)
        owner = lax.rem(me - step + parts, parts)
        whole = lax.dynamic_update_slice_in_dim(whole, piece, owner * rows, 0)
    return whole


def mp_sum_rows(whole, parts):
    me = lax.axis_index("mp")
    rows = whole.shape[0] // parts
    total = lax.dynamic_slice_in_dim(whole, me * rows, rows, 0)
    for step in range(1, parts):
        owner = lax.rem(me + step, parts)
        piece = lax.dynamic_slice_in_dim(whole, owner * rows, rows, 0).astype(BF16)
        total = total + mp_shift(piece, step, parts).astype(F32)
    return total


def shards(
    tokens,
    seq_lengths,
    norm_attn,
    w_query,
    key_weight,
    value_weight,
    w_out,
    norm_mlp,
    w_gate,
    w_up,
    w_down,
    cotangent,
):
    parts = lax.axis_size("mp")
    rows = tokens.shape[0]
    group = rows * parts
    q_width, kv_width, hidden_width = w_query.shape[1], key_weight.shape[1], w_gate.shape[1]
    heads, kv_heads = q_width // HEAD_SIZE, kv_width // HEAD_SIZE
    members = heads // kv_heads
    factor = HEAD_SIZE ** (-0.5)

    attn_w = lax.all_gather(
        jnp.concatenate([w_query, key_weight, value_weight, w_out.T], axis=1),
        "dp", axis=0, tiled=True,
    )
    mlp_w = lax.all_gather(
        jnp.concatenate([w_gate, w_up, w_down.T], axis=1), "dp", axis=0, tiled=True
    )
    cuts = (q_width, q_width + kv_width, q_width + 2 * kv_width)
    query_w, key_w, value_w, out_wt = jnp.split(attn_w, cuts, axis=1)
    gate_w, up_w, down_wt = jnp.split(mlp_w, 3, axis=1)

    inputs = tokens.astype(F32)
    gain_one, gain_two = norm_attn.astype(F32), norm_mlp.astype(F32)
    normed_one = mp_gather((rms_parts(inputs)[1] * gain_one).astype(BF16), parts)
    grad_rows = mp_gather(cotangent, parts)

    segment, position = layout(seq_lengths[0], group)
    cosine, sine = rotation(position)
    places = jnp.arange(group, dtype=jnp.int32)
    allowed = (
        (places[:, None] >= places[None, :])
        & (segment[:, None] == segment[None, :])
        & ((segment[None, :] >= 0) | (places[:, None] == places[None, :]))
    )

    query = rotate(mul(normed_one, query_w).reshape(group, heads, HEAD_SIZE), cosine, sine)
    key = rotate(mul(normed_one, key_w).reshape(group, kv_heads, HEAD_SIZE), cosine, sine)
    value = mul(normed_one, value_w).astype(BF16).reshape(group, kv_heads, HEAD_SIZE)
    query = query.astype(BF16).reshape(group, kv_heads, members, HEAD_SIZE)
    key = key.astype(BF16)
    scores = jnp.einsum("qhgd,khd->hgqk", query, key, preferred_element_type=F32) * factor
    scores = jnp.where(allowed[None, None], scores, MASKED)
    peak = jnp.max(scores, axis=-1, keepdims=True)
    grown = jnp.exp(scores - peak)
    probs = grown / jnp.sum(grown, axis=-1, keepdims=True)
    probs_low = probs.astype(BF16)
    attended = (
        jnp.einsum("hgqk,khd->qhgd", probs_low, value, preferred_element_type=F32)
        .astype(BF16)
        .reshape(group, q_width)
    )
    residual = inputs + mp_sum_rows(mul_t(attended, out_wt), parts)
    normed_two = mp_gather((rms_parts(residual)[1] * gain_two).astype(BF16), parts)

    gate_act, up_act = mul(normed_two, gate_w), mul(normed_two, up_w)
    sigmoid_g = jax.nn.sigmoid(gate_act)
    swish = gate_act * sigmoid_g
    hidden = (swish * up_act).astype(BF16)
    branch = mul_t(hidden, down_wt)
    grad_hidden = mul(grad_rows, down_wt)
    grad_gate = (grad_hidden * up_act * sigmoid_g * (1.0 + gate_act * (1.0 - sigmoid_g))).astype(
        BF16
    )
    grad_up = (grad_hidden * swish).astype(BF16)
    grad_mlp = jnp.concatenate(
        [
            outer_sum(normed_two, grad_gate).astype(BF16),
            outer_sum(normed_two, grad_up).astype(BF16),
            outer_sum(grad_rows, hidden).astype(BF16),
        ],
        axis=1,
    )
    grad_mlp = lax.psum_scatter(grad_mlp, "dp", scatter_dimension=0, tiled=True)
    grad_two = mp_sum_rows(mul_t(grad_gate, gate_w) + mul_t(grad_up, up_w), parts)
    block_out = (residual + mp_sum_rows(branch, parts)).astype(BF16)

    from_two, gain_two_grad = rms_back(residual, gain_two, grad_two)
    grad_residual = cotangent.astype(F32) + from_two
    grad_branch = mp_gather(grad_residual.astype(BF16), parts)
    grad_attended = (
        mul(grad_branch, out_wt).astype(BF16).reshape(group, kv_heads, members, HEAD_SIZE)
    )
    dprob = jnp.einsum("qhgd,khd->hgqk", grad_attended, value, preferred_element_type=F32)
    inner = jnp.sum(probs * dprob, axis=-1, keepdims=True)
    dscore = (probs * (dprob - inner)).astype(BF16)
    grad_query = jnp.einsum("hgqk,khd->qhgd", dscore, key, preferred_element_type=F32) * factor
    grad_key = jnp.einsum("hgqk,qhgd->khd", dscore, query, preferred_element_type=F32) * factor
    grad_value = jnp.einsum(
        "hgqk,qhgd->khd", probs_low, grad_attended, preferred_element_type=F32
    )
    grad_query = rotate(grad_query.reshape(group, heads, HEAD_SIZE), cosine, -sine)
    grad_query = grad_query.astype(BF16).reshape(group, q_width)
    grad_key = rotate(grad_key, cosine, -sine).astype(BF16).reshape(group, kv_width)
    grad_value = grad_value.astype(BF16).reshape(group, kv_width)
    grad_attn = jnp.concatenate(
        [
            outer_sum(normed_one, grad_query).astype(BF16),
            outer_sum(normed_one, grad_key).astype(BF16),
            outer_sum(normed_one, grad_value).astype(BF16),
            outer_sum(grad_branch, attended).astype(BF16),
        ],
        axis=1,
    )
    grad_attn = lax.psum_scatter(grad_attn, "dp", scatter_dimension=0, tiled=True)
    grad_one = mp_sum_rows(
        mul_t(grad_query, query_w) + mul_t(grad_key, key_w) + mul_t(grad_value, value_w), parts
    )
    from_one, gain_one_grad = rms_back(inputs, gain_one, grad_one)
    grad_tokens = (grad_residual + from_one).astype(BF16)
    gains = lax.psum(jnp.stack([gain_one_grad, gain_two_grad]), ("dp", "mp"))

    attn_parts = jnp.split(grad_attn.astype(F32), cuts, axis=1)
    mlp_parts = jnp.split(grad_mlp.astype(F32), 3, axis=1)
    return (
        block_out,
        grad_tokens,
        gains[0],
        attn_parts[0],
        attn_parts[1],
        attn_parts[2],
        attn_parts[3].T,
        gains[1],
        mlp_parts[0],
        mlp_parts[1],
        mlp_parts[2].T,
    )


def solution(mesh):
    rows, whole = P(("dp", "mp"), None), P()
    split, turned = P("dp", "mp"), P("mp", "dp")
    return jax.shard_map(
        shards,
        mesh=mesh,
        in_specs=(
            rows, P("dp", None), whole, split, split, split, turned, whole, split, split, turned, rows,
        ),
        out_specs=(
            rows, rows, whole, split, split, split, turned, whole, split, split, turned,
        ),
        check_vma=False,
    )
```

```python
import functools

import jax
import jax.numpy as jnp
from jax import lax
from jax.experimental import pallas as pl
from jax.experimental.pallas import tpu as pltpu
from jax.sharding import PartitionSpec as P

HEAD_SIZE = 96
EPSILON = 1e-05
ROPE_BASE = 100000.0
MASKED = -1e30
F32 = jnp.float32
BF16 = jnp.bfloat16


def layout(lengths, rows_total):
    places = jnp.arange(rows_total, dtype=jnp.int32)
    first_end = lengths[0]
    middle_end = lengths[0] + lengths[1]
    last_end = middle_end + lengths[2]
    segment = jnp.where(
        places < first_end,
        0,
        jnp.where(places < middle_end, 1, jnp.where(places < last_end, 2, -1)),
    ).astype(jnp.int32)
    offset = jnp.where(places < first_end, 0, jnp.where(places < middle_end, first_end, middle_end))
    position = jnp.where(segment >= 0, places - offset, 0)
    return segment, position


def rotation(position):
    half_dim = HEAD_SIZE // 2
    inverse = ROPE_BASE ** (-jnp.arange(half_dim, dtype=F32) * 2.0 / HEAD_SIZE)
    angles = position.astype(F32)[:, None] * inverse[None, :]
    return jnp.cos(angles)[:, None, :], jnp.sin(angles)[:, None, :]


def rotate(tensor, cosine, sine):
    half_dim = tensor.shape[-1] // 2
    lead, tail = tensor[..., :half_dim], tensor[..., half_dim:]
    return jnp.concatenate([lead * cosine - tail * sine, tail * cosine + lead * sine], axis=-1)


def rms_parts(inputs):
    factor = lax.rsqrt(jnp.mean(inputs * inputs, axis=-1, keepdims=True) + EPSILON)
    return factor, inputs * factor


def mul(left, right):
    return jnp.dot(left, right, preferred_element_type=F32)


def mul_t(left, right):
    return lax.dot_general(left, right, (((1,), (1,)), ((), ())), preferred_element_type=F32)


def outer_sum(left, right):
    return lax.dot_general(left, right, (((0,), (0,)), ((), ())), preferred_element_type=F32)


def mp_shift(block, step, parts):
    return lax.ppermute(block, "mp", [(i, (i + step) % parts) for i in range(parts)])


def mp_gather(block, parts):
    me = lax.axis_index("mp")
    rows = block.shape[0]
    whole = jnp.zeros((parts * rows,) + block.shape[1:], block.dtype)
    for step in range(parts):
        piece = block if step == 0 else mp_shift(block, step, parts)
        owner = lax.rem(me - step + parts, parts)
        whole = lax.dynamic_update_slice_in_dim(whole, piece, owner * rows, 0)
    return whole


def mp_sum_rows(whole, parts):
    me = lax.axis_index("mp")
    rows = whole.shape[0] // parts
    total = lax.dynamic_slice_in_dim(whole, me * rows, rows, 0)
    for step in range(1, parts):
        owner = lax.rem(me + step, parts)
        piece = lax.dynamic_slice_in_dim(whole, owner * rows, rows, 0).astype(BF16)
        total = total + mp_shift(piece, step, parts).astype(F32)
    return total


MESH = pl.DeviceIdType.MESH
VMEM_SPEC = pl.BlockSpec(memory_space=pltpu.VMEM)
ANY_SPEC = pl.BlockSpec(memory_space=pl.ANY)
DMA = pltpu.SemaphoreType.DMA


def place(depth, parts):
    me, part = lax.axis_index("dp"), lax.axis_index("mp")
    z, y, core = me // 4, lax.rem(me // 2, 2), lax.rem(me, 2)

    def dp_of(step, at_y, at_core):
        return lax.rem(z + step, depth) * 4 + at_y * 2 + at_core

    def mp_of(step):
        return lax.rem(part + step, parts)

    return me, part, z, y, core, dp_of, mp_of


def greet(depth, parts):
    me, part, z, y, core, dp_of, mp_of = place(depth, parts)
    near = [(dp_of(0, y, 1 - core), part), (dp_of(0, 1 - y, core), part)]
    near += [(dp_of(step, y, core), part) for step in range(1, depth)]
    near += [(me, mp_of(step)) for step in range(1, parts)]
    barrier = pltpu.get_barrier_semaphore()
    for device in near:
        pl.semaphore_signal(barrier, inc=1, device_id=device, device_id_type=MESH)
    pl.semaphore_wait(barrier, len(near))


def send(source, target, sems, at, device):
    sent, landed = sems
    copy = pltpu.make_async_remote_copy(
        src_ref=source,
        dst_ref=target,
        send_sem=sent.at[at],
        recv_sem=landed.at[at],
        device_id=device,
        device_id_type=MESH,
    )
    return copy


def gather_kernel(depth, parts, shard, normed, cot, weights, normed_all, cot_all,
                  z_sent, z_got, y_sent, y_got, c_sent, c_got, x_sent, x_got, kept):
    me, part, z, y, core, dp_of, mp_of = place(depth, parts)
    own = [
        pltpu.make_async_copy(shard, weights.at[me], kept.at[0]),
        pltpu.make_async_copy(normed, normed_all.at[part], kept.at[1]),
        pltpu.make_async_copy(cot, cot_all.at[part], kept.at[2]),
    ]
    for copy in own:
        copy.start()
    greet(depth, parts)
    other_y, other_core = (dp_of(0, 1 - y, core), part), (dp_of(0, y, 1 - core), part)

    along_z = [
        send(shard, weights.at[me], (z_sent, z_got), step - 1, (dp_of(step, y, core), part))
        for step in range(1, depth)
    ]
    along_x = [
        send(source, target.at[part], (x_sent, x_got), 2 * (step - 1) + i, (me, mp_of(step)))
        for i, (source, target) in enumerate(((normed, normed_all), (cot, cot_all)))
        for step in range(1, parts)
    ]

    def block_from(step, at_y):
        return weights.at[dp_of(depth - step, at_y, core)]

    def to_y(step):
        block = shard if step == 0 else block_from(step, y)
        return send(block, block_from(step, y), (y_sent, y_got), step, other_y)

    def to_core(step, at_y, slot):
        block = block_from(step, at_y)
        source = shard if step == 0 and slot == 0 else block
        return send(source, block, (c_sent, c_got), 2 * step + slot, other_core)

    along_y = [to_y(step) for step in range(depth)]
    across = [[to_core(step, y, 0), to_core(step, 1 - y, 1)] for step in range(depth)]
    for copy in along_z:
        copy.start()
    along_y[0].start()
    across[0][0].start()
    for copy in along_x:
        copy.start()
    for step in range(1, depth):
        along_z[step - 1].wait_recv()
        along_y[step].start()
        across[step][0].start()
    for step in range(depth):
        along_y[step].wait_recv()
        across[step][1].start()
    for copy in along_x:
        copy.wait()
    for copy in along_z + along_y:
        copy.wait_send()
    for pair in across:
        for copy in pair:
            copy.wait()
    for copy in own:
        copy.wait()


def gather_attn(shard, normed, cot):
    depth, parts = lax.axis_size("dp") // 4, lax.axis_size("mp")
    size = depth * 4
    return pl.pallas_call(
        functools.partial(gather_kernel, depth, parts),
        out_shape=(
            jax.ShapeDtypeStruct((size,) + shard.shape, shard.dtype),
            jax.ShapeDtypeStruct((parts,) + normed.shape, normed.dtype),
            jax.ShapeDtypeStruct((parts,) + cot.shape, cot.dtype),
        ),
        in_specs=[ANY_SPEC] * 3,
        out_specs=(ANY_SPEC,) * 3,
        scratch_shapes=[DMA((depth - 1,))] * 2 + [DMA((depth,))] * 2 + [DMA((2 * depth,))] * 2
        + [DMA((2 * (parts - 1),))] * 2 + [DMA((3,))],
        compiler_params=pltpu.CompilerParams(collective_id=0, has_side_effects=True),
        name="gather_attn",
    )(shard, normed, cot)


def add_rows(target, sources):
    def body(i, carry):
        here = pl.ds(pl.multiple_of(i * 16, 16), 16)
        total = sources[0][here, :].astype(F32)
        for source in sources[1:]:
            total = total + source[here, :].astype(F32)
        target[here, :] = total.astype(target.dtype)
        return carry

    lax.fori_loop(0, target.shape[0] // 16, body, 0)


class Sums:
    CORE_AHEAD = 3
    Y_AHEAD = 3

    def __init__(self, depth, parts, pieces, wholes, outs, scratch):
        self.depth, self.parts, self.wholes, self.outs = depth, parts, wholes, outs
        count = len(wholes)
        self.mine, self.core_in, self.y_in, self.z_in = (
            scratch[i * count : (i + 1) * count] for i in range(4)
        )
        self.sems = scratch[4 * count :]
        self.order = [
            (step, k, piece)
            for step in range(1, depth + 1)
            for k in range(count)
            for piece in range(pieces)
        ]
        self.pieces = pieces
        self.where = place(depth, parts)
        self.items = [self.parts_of(n) for n in range(len(self.order))]

    @staticmethod
    def scratch(depth, pieces, wholes):
        kinds = ((depth, 2), (depth, 2), (depth,), (depth - 1,))
        buffers = [
            pltpu.VMEM(lead + whole.shape[3:], BF16) for lead in kinds for whole in wholes
        ]
        count = depth * len(wholes) * pieces
        return buffers + [DMA((count,))] * 7

    def parts_of(self, n):
        step, k, piece = self.order[n]
        me, part, z, y, core, dp_of, mp_of = self.where
        at = lax.rem(z + step, self.depth)
        kept, c_sent, c_got, y_sent, y_got, z_sent, z_got = self.sems
        whole, mine = self.wholes[k], self.mine[k]
        width = mine.shape[3] // self.pieces
        cols = pl.ds(piece * width, width)
        own = pltpu.make_async_copy(
            whole.at[at, :, core, :, cols], mine.at[at, :, :, cols], kept.at[n]
        )
        across = send(
            whole.at[at, :, 1 - core, :, cols], self.core_in[k].at[at, :, :, cols],
            (c_sent, c_got), n, (dp_of(0, y, 1 - core), part),
        )
        along_y = send(
            mine.at[at, 1 - y, :, cols], self.y_in[k].at[at, :, cols], (y_sent, y_got), n,
            (dp_of(0, 1 - y, core), part),
        )
        along_z = None
        if step < self.depth:
            along_z = send(
                mine.at[at, y, :, cols], self.z_in[k].at[step - 1, :, cols], (z_sent, z_got), n,
                (dp_of(step, y, core), part),
            )
        return at, k, cols, own, across, along_y, along_z

    def begin(self):
        for n in range(min(self.CORE_AHEAD, len(self.items))):
            self.load(n)

    def load(self, n):
        self.items[n][3].start()
        self.items[n][4].start()

    def cross(self, n):
        at, k, cols, own, across, along_y, along_z = self.items[n]
        own.wait()
        across.wait_recv()
        if n + self.CORE_AHEAD < len(self.items):
            self.load(n + self.CORE_AHEAD)
        for at_y in range(2):
            mine = self.mine[k].at[at, at_y, :, cols]
            add_rows(mine, (mine, self.core_in[k].at[at, at_y, :, cols]))
        along_y.start()

    def onward(self, n):
        y = self.where[3]
        at, k, cols, own, across, along_y, along_z = self.items[n]
        along_y.wait_recv()
        mine = self.mine[k].at[at, y, :, cols]
        add_rows(mine, (mine, self.y_in[k].at[at, :, cols]))
        if along_z is not None:
            along_z.start()

    def advance(self, n):
        if n < len(self.items):
            self.cross(n)
        if n >= self.Y_AHEAD:
            self.onward(n - self.Y_AHEAD)

    def steps(self):
        return len(self.items) + self.Y_AHEAD

    def end(self):
        z, y = self.where[2:4]
        for at, k, cols, own, across, along_y, along_z in self.items:
            if along_z is not None:
                along_z.wait_recv()
        for k, out in enumerate(self.outs):
            add_rows(
                out, [self.mine[k].at[z, y]] + [self.z_in[k].at[i] for i in range(self.depth - 1)]
            )
        for at, k, cols, own, across, along_y, along_z in self.items:
            across.wait_send()
            along_y.wait_send()
            if along_z is not None:
                along_z.wait_send()


def pieces_of(width, wanted):
    return wanted if width % (128 * wanted) == 0 else 1


def norm_back(rows_in, gain, gradient):
    factor = lax.rsqrt(jnp.mean(rows_in * rows_in, axis=-1, keepdims=True) + EPSILON)
    normed = rows_in * factor
    scaled = gradient * gain
    back = factor * (scaled - normed * jnp.mean(scaled * normed, axis=-1, keepdims=True))
    return back, gradient * normed


TILE = 16


def fold(terms):
    total = terms[0:8]
    for at in range(8, terms.shape[0], 8):
        total = total + terms[at : at + 8]
    return total


def sum_mlp_kernel(depth, parts, *refs):
    (gate, up, down, own_two, give_two, own_out, give_out, residual, cot, gain,
     gate_out, up_out, down_out, block_out, grad_residual, branch_all, gain_grad,
     in_two, in_out, branch, two_sent, two_got, out_sent, out_got, b_sent, b_got, kept) = refs[:27]
    me, part, z, y, core, dp_of, mp_of = place(depth, parts)
    rows = own_two.shape[0]
    sums = Sums(depth, parts, 1, (gate, up, down), (gate_out, up_out, down_out), refs[27:])
    greet(depth, parts)

    def along_x(source, target, sems):
        return [
            send(source(step), target(step), sems, step - 1, (me, mp_of(step)))
            for step in range(1, parts)
        ]

    to_two = along_x(
        lambda s: give_two.at[s - 1], lambda s: in_two.at[s - 1], (two_sent, two_got)
    )
    to_out = along_x(
        lambda s: give_out.at[s - 1], lambda s: in_out.at[s - 1], (out_sent, out_got)
    )
    to_branch = along_x(lambda s: branch, lambda s: branch_all.at[part], (b_sent, b_got))
    for copy in to_two:
        copy.start()
    sums.begin()
    at = 0
    while at < sums.Y_AHEAD:
        sums.advance(at)
        at += 1
    for copy in to_two:
        copy.wait_recv()
    gain_grad[...] = jnp.zeros_like(gain_grad)

    def body(i, carry):
        here = pl.ds(pl.multiple_of(i * TILE, TILE), TILE)
        total = own_two[here, :]
        for step in range(parts - 1):
            total = total + in_two[step, here, :].astype(F32)
        back, terms = norm_back(residual[here, :], gain[...], total)
        gain_grad[...] += fold(terms)
        result = cot[here, :].astype(F32) + back
        grad_residual[here, :] = result
        branch[here, :] = result.astype(BF16)
        return carry

    lax.fori_loop(0, rows // TILE, body, 0)
    mine = pltpu.make_async_copy(branch, branch_all.at[part], kept.at[0])
    mine.start()
    for copy in to_branch + to_out:
        copy.start()
    while at < sums.steps():
        sums.advance(at)
        at += 1
    for copy in to_out:
        copy.wait_recv()

    def finish(i, carry):
        here = pl.ds(pl.multiple_of(i * TILE, TILE), TILE)
        total = own_out[here, :]
        for step in range(parts - 1):
            total = total + in_out[step, here, :].astype(F32)
        block_out[here, :] = (residual[here, :] + total).astype(BF16)
        return carry

    lax.fori_loop(0, rows // TILE, finish, 0)
    sums.end()
    mine.wait()
    for copy in to_branch:
        copy.wait()
    for copy in to_two + to_out:
        copy.wait_send()


def sum_mlp(grads, own_two, give_two, own_out, give_out, residual, cot, gain):
    depth, parts = lax.axis_size("dp") // 4, lax.axis_size("mp")
    rows, width = residual.shape
    wholes = [grad.reshape(depth, 2, 2, grad.shape[0] // (4 * depth), -1) for grad in grads]
    return pl.pallas_call(
        functools.partial(sum_mlp_kernel, depth, parts),
        out_shape=[jax.ShapeDtypeStruct(whole.shape[3:], F32) for whole in wholes]
        + [
            jax.ShapeDtypeStruct((rows, width), BF16),
            jax.ShapeDtypeStruct((rows, width), F32),
            jax.ShapeDtypeStruct((parts, rows, width), BF16),
            jax.ShapeDtypeStruct((8, width), F32),
        ],
        in_specs=[ANY_SPEC] * 3 + [VMEM_SPEC, ANY_SPEC, VMEM_SPEC, ANY_SPEC] + [VMEM_SPEC] * 3,
        out_specs=[VMEM_SPEC] * 5 + [ANY_SPEC, VMEM_SPEC],
        scratch_shapes=[pltpu.VMEM((parts - 1, rows, width), BF16)] * 2
        + [pltpu.VMEM((rows, width), BF16)]
        + [DMA((parts - 1,))] * 6 + [DMA((1,))]
        + Sums.scratch(depth, 1, wholes),
        compiler_params=pltpu.CompilerParams(
            collective_id=1, has_side_effects=True, vmem_limit_bytes=56 * 2**20
        ),
        name="sum_mlp",
    )(*wholes, own_two, give_two, own_out, give_out, residual, cot, gain)


def sum_attn_kernel(depth, parts, *refs):
    (grad, own_one, give_one, tokens, grad_residual, gain, gain_two_grad,
     grad_out, grad_tokens, gains,
     in_one, held, around, one_sent, one_got, g_sent, g_got) = refs[:17]
    me, part, z, y, core, dp_of, mp_of = place(depth, parts)
    rows = own_one.shape[0]
    pieces = pieces_of(grad.shape[4], 3)
    sums = Sums(depth, parts, pieces, (grad,), (grad_out,), refs[17:])
    greet(depth, parts)
    to_one = [
        send(give_one.at[step - 1], in_one.at[step - 1], (one_sent, one_got), step - 1,
             (me, mp_of(step)))
        for step in range(1, parts)
    ]
    for copy in to_one:
        copy.start()
    sums.begin()
    at = 0
    while at < sums.Y_AHEAD:
        sums.advance(at)
        at += 1
    for copy in to_one:
        copy.wait_recv()
    held[0:8] = jnp.zeros((8, held.shape[1]), F32)
    held[8:16] = gain_two_grad[...]

    def body(i, carry):
        here = pl.ds(pl.multiple_of(i * TILE, TILE), TILE)
        total = own_one[here, :]
        for step in range(parts - 1):
            total = total + in_one[step, here, :].astype(F32)
        back, terms = norm_back(tokens[here, :].astype(F32), gain[...], total)
        held[0:8] += fold(terms)
        grad_tokens[here, :] = (grad_residual[here, :] + back).astype(BF16)
        return carry

    lax.fori_loop(0, rows // TILE, body, 0)
    stages = [
        [(dp_of(0, y, 1 - core), part)],
        [(me, mp_of(step)) for step in range(1, parts)],
        [(dp_of(step, y, core), part) for step in range(1, depth)],
        [(dp_of(0, 1 - y, core), part)],
    ]
    levels, slot = [], 0
    for number, stage in enumerate(stages):
        copies = []
        for device in stage:
            landing = around.at[pl.ds(16 * slot, 16)]
            copies.append(
                (send(held.at[pl.ds(16 * number, 16)], landing, (g_sent, g_got), slot, device),
                 landing)
            )
            slot += 1
        levels.append(copies)

    def begin_level(number):
        for copy, landing in levels[number]:
            copy.start()

    def end_level(number):
        total = held[16 * number : 16 * number + 16]
        for copy, landing in levels[number]:
            copy.wait_recv()
            total = total + landing[...]
        held[16 * (number + 1) : 16 * (number + 2)] = total

    number = 0
    begin_level(0)
    while at < sums.steps():
        sums.advance(at)
        at += 1
        if number < len(levels):
            end_level(number)
            number += 1
            if number < len(levels):
                begin_level(number)
    while number < len(levels):
        end_level(number)
        number += 1
        if number < len(levels):
            begin_level(number)
    gains[...] = held[64:80]
    sums.end()
    for copy in to_one + [copy for copies in levels for copy, landing in copies]:
        copy.wait_send()


def sum_attn(grad, own_one, give_one, tokens, grad_residual, gain, gain_two_grad):
    depth, parts = lax.axis_size("dp") // 4, lax.axis_size("mp")
    rows, width = tokens.shape
    whole = grad.reshape(depth, 2, 2, grad.shape[0] // (4 * depth), -1)
    stops = depth + parts
    return pl.pallas_call(
        functools.partial(sum_attn_kernel, depth, parts),
        out_shape=[
            jax.ShapeDtypeStruct(whole.shape[3:], F32),
            jax.ShapeDtypeStruct((rows, width), BF16),
            jax.ShapeDtypeStruct((16, width), F32),
        ],
        in_specs=[ANY_SPEC, VMEM_SPEC, ANY_SPEC] + [VMEM_SPEC] * 4,
        out_specs=[VMEM_SPEC] * 3,
        scratch_shapes=[
            pltpu.VMEM((parts - 1, rows, width), BF16),
            pltpu.VMEM((80, width), F32),
            pltpu.VMEM((16 * stops, width), F32),
        ]
        + [DMA((parts - 1,))] * 2 + [DMA((stops,))] * 2
        + Sums.scratch(depth, pieces_of(whole.shape[4], 3), [whole]),
        compiler_params=pltpu.CompilerParams(
            collective_id=2, has_side_effects=True, vmem_limit_bytes=56 * 2**20
        ),
        name="sum_attn",
    )(whole, own_one, give_one, tokens, grad_residual, gain, gain_two_grad)


def own_and_give(whole, parts):
    me = lax.axis_index("mp")
    rows = whole.shape[0] // parts
    own = lax.dynamic_slice_in_dim(whole, me * rows, rows, 0)
    give = [
        lax.dynamic_slice_in_dim(whole, lax.rem(me + step, parts) * rows, rows, 0).astype(BF16)
        for step in range(1, parts)
    ]
    return own, jnp.stack(give)


def shards(
    tokens,
    seq_lengths,
    norm_attn,
    w_query,
    key_weight,
    value_weight,
    w_out,
    norm_mlp,
    w_gate,
    w_up,
    w_down,
    cotangent,
):
    parts = lax.axis_size("mp")
    rows = tokens.shape[0]
    group = rows * parts
    q_width, kv_width, hidden_width = w_query.shape[1], key_weight.shape[1], w_gate.shape[1]
    heads, kv_heads = q_width // HEAD_SIZE, kv_width // HEAD_SIZE
    members = heads // kv_heads
    factor = HEAD_SIZE ** (-0.5)

    mlp_w = lax.all_gather(
        jnp.concatenate([w_gate, w_up, w_down.T], axis=1), "dp", axis=0, tiled=True
    )
    inputs = tokens.astype(F32)
    gain_one, gain_two = norm_attn.astype(F32), norm_mlp.astype(F32)
    attn_w, normed_one, grad_rows = gather_attn(
        jnp.concatenate([w_query, key_weight, value_weight, w_out.T], axis=1),
        (rms_parts(inputs)[1] * gain_one).astype(BF16),
        cotangent,
    )
    width = tokens.shape[1]
    attn_w = attn_w.reshape(width, -1)
    normed_one, grad_rows = normed_one.reshape(group, width), grad_rows.reshape(group, width)
    cuts = (q_width, q_width + kv_width, q_width + 2 * kv_width)
    query_w, key_w, value_w, out_wt = jnp.split(attn_w, cuts, axis=1)
    gate_w, up_w, down_wt = jnp.split(mlp_w, 3, axis=1)

    segment, position = layout(seq_lengths[0], group)
    cosine, sine = rotation(position)
    places = jnp.arange(group, dtype=jnp.int32)
    allowed = (
        (places[:, None] >= places[None, :])
        & (segment[:, None] == segment[None, :])
        & ((segment[None, :] >= 0) | (places[:, None] == places[None, :]))
    )

    query = rotate(mul(normed_one, query_w).reshape(group, heads, HEAD_SIZE), cosine, sine)
    key = rotate(mul(normed_one, key_w).reshape(group, kv_heads, HEAD_SIZE), cosine, sine)
    value = mul(normed_one, value_w).astype(BF16).reshape(group, kv_heads, HEAD_SIZE)
    query = query.astype(BF16).reshape(group, kv_heads, members, HEAD_SIZE)
    key = key.astype(BF16)
    scores = jnp.einsum("qhgd,khd->hgqk", query, key, preferred_element_type=F32) * factor
    scores = jnp.where(allowed[None, None], scores, MASKED)
    peak = jnp.max(scores, axis=-1, keepdims=True)
    grown = jnp.exp(scores - peak)
    probs = grown / jnp.sum(grown, axis=-1, keepdims=True)
    probs_low = probs.astype(BF16)
    attended = (
        jnp.einsum("hgqk,khd->qhgd", probs_low, value, preferred_element_type=F32)
        .astype(BF16)
        .reshape(group, q_width)
    )
    residual = inputs + mp_sum_rows(mul_t(attended, out_wt), parts)
    normed_two = mp_gather((rms_parts(residual)[1] * gain_two).astype(BF16), parts)

    gate_act, up_act = mul(normed_two, gate_w), mul(normed_two, up_w)
    sigmoid_g = jax.nn.sigmoid(gate_act)
    swish = gate_act * sigmoid_g
    hidden = (swish * up_act).astype(BF16)
    branch = mul_t(hidden, down_wt)
    grad_hidden = mul(grad_rows, down_wt)
    grad_gate = (grad_hidden * up_act * sigmoid_g * (1.0 + gate_act * (1.0 - sigmoid_g))).astype(
        BF16
    )
    grad_up = (grad_hidden * swish).astype(BF16)
    grads_mlp = (
        outer_sum(normed_two, grad_gate).astype(BF16),
        outer_sum(normed_two, grad_up).astype(BF16),
        outer_sum(grad_rows, hidden).astype(BF16),
    )
    (grad_gate_w, grad_up_w, grad_down_w, block_out, grad_residual, grad_branch, gain_two_grad) = (
        sum_mlp(
            grads_mlp,
            *own_and_give(mul_t(grad_gate, gate_w) + mul_t(grad_up, up_w), parts),
            *own_and_give(branch, parts),
            residual,
            cotangent,
            gain_two[None, :],
        )
    )
    grad_branch = grad_branch.reshape(group, width)
    grad_attended = (
        mul(grad_branch, out_wt).astype(BF16).reshape(group, kv_heads, members, HEAD_SIZE)
    )
    dprob = jnp.einsum("qhgd,khd->hgqk", grad_attended, value, preferred_element_type=F32)
    inner = jnp.sum(probs * dprob, axis=-1, keepdims=True)
    dscore = (probs * (dprob - inner)).astype(BF16)
    grad_query = jnp.einsum("hgqk,khd->qhgd", dscore, key, preferred_element_type=F32) * factor
    grad_key = jnp.einsum("hgqk,qhgd->khd", dscore, query, preferred_element_type=F32) * factor
    grad_value = jnp.einsum(
        "hgqk,qhgd->khd", probs_low, grad_attended, preferred_element_type=F32
    )
    grad_query = rotate(grad_query.reshape(group, heads, HEAD_SIZE), cosine, -sine)
    grad_query = grad_query.astype(BF16).reshape(group, q_width)
    grad_key = rotate(grad_key, cosine, -sine).astype(BF16).reshape(group, kv_width)
    grad_value = grad_value.astype(BF16).reshape(group, kv_width)
    grad_attn = jnp.concatenate(
        [
            outer_sum(normed_one, grad_query).astype(BF16),
            outer_sum(normed_one, grad_key).astype(BF16),
            outer_sum(normed_one, grad_value).astype(BF16),
            outer_sum(grad_branch, attended).astype(BF16),
        ],
        axis=1,
    )
    grad_attn, grad_tokens, gains = sum_attn(
        grad_attn,
        *own_and_give(
            mul_t(grad_query, query_w) + mul_t(grad_key, key_w) + mul_t(grad_value, value_w), parts
        ),
        tokens,
        grad_residual,
        gain_one[None, :],
        gain_two_grad,
    )
    attn_parts = jnp.split(grad_attn, cuts, axis=1)
    gains = jnp.sum(gains.reshape(2, 8, width), axis=1)
    return (
        block_out,
        grad_tokens,
        gains[0],
        attn_parts[0],
        attn_parts[1],
        attn_parts[2],
        attn_parts[3].T,
        gains[1],
        grad_gate_w,
        grad_up_w,
        grad_down_w.T,
    )


def solution(mesh):
    rows, whole = P(("dp", "mp"), None), P()
    split, turned = P("dp", "mp"), P("mp", "dp")
    return jax.shard_map(
        shards,
        mesh=mesh,
        in_specs=(
            rows, P("dp", None), whole, split, split, split, turned, whole, split, split, turned, rows,
        ),
        out_specs=(
            rows, rows, whole, split, split, split, turned, whole, split, split, turned,
        ),
        check_vma=False,
    )
```

```python
import functools

import jax
import jax.numpy as jnp
from jax import lax
from jax.experimental import pallas as pl
from jax.experimental.pallas import tpu as pltpu
from jax.sharding import PartitionSpec as P

HEAD_SIZE = 96
EPSILON = 1e-05
ROPE_BASE = 100000.0
MASKED = -1e30
F32 = jnp.float32
BF16 = jnp.bfloat16


def layout(lengths, rows_total):
    places = jnp.arange(rows_total, dtype=jnp.int32)
    first_end = lengths[0]
    middle_end = lengths[0] + lengths[1]
    last_end = middle_end + lengths[2]
    segment = jnp.where(
        places < first_end,
        0,
        jnp.where(places < middle_end, 1, jnp.where(places < last_end, 2, -1)),
    ).astype(jnp.int32)
    offset = jnp.where(places < first_end, 0, jnp.where(places < middle_end, first_end, middle_end))
    position = jnp.where(segment >= 0, places - offset, 0)
    return segment, position


def rotation(position):
    half_dim = HEAD_SIZE // 2
    inverse = ROPE_BASE ** (-jnp.arange(half_dim, dtype=F32) * 2.0 / HEAD_SIZE)
    angles = position.astype(F32)[:, None] * inverse[None, :]
    return jnp.cos(angles)[:, None, :], jnp.sin(angles)[:, None, :]


def rotate(tensor, cosine, sine):
    half_dim = tensor.shape[-1] // 2
    lead, tail = tensor[..., :half_dim], tensor[..., half_dim:]
    return jnp.concatenate([lead * cosine - tail * sine, tail * cosine + lead * sine], axis=-1)


def rms_parts(inputs):
    factor = lax.rsqrt(jnp.mean(inputs * inputs, axis=-1, keepdims=True) + EPSILON)
    return factor, inputs * factor


def mul(left, right):
    return jnp.dot(left, right, preferred_element_type=F32)


def mul_t(left, right):
    return lax.dot_general(left, right, (((1,), (1,)), ((), ())), preferred_element_type=F32)


def outer_sum(left, right):
    return lax.dot_general(left, right, (((0,), (0,)), ((), ())), preferred_element_type=F32)


def mp_shift(block, step, parts):
    return lax.ppermute(block, "mp", [(i, (i + step) % parts) for i in range(parts)])


def mp_gather(block, parts):
    me = lax.axis_index("mp")
    rows = block.shape[0]
    whole = jnp.zeros((parts * rows,) + block.shape[1:], block.dtype)
    for step in range(parts):
        piece = block if step == 0 else mp_shift(block, step, parts)
        owner = lax.rem(me - step + parts, parts)
        whole = lax.dynamic_update_slice_in_dim(whole, piece, owner * rows, 0)
    return whole


def mp_sum_rows(whole, parts):
    me = lax.axis_index("mp")
    rows = whole.shape[0] // parts
    total = lax.dynamic_slice_in_dim(whole, me * rows, rows, 0)
    for step in range(1, parts):
        owner = lax.rem(me + step, parts)
        piece = lax.dynamic_slice_in_dim(whole, owner * rows, rows, 0).astype(BF16)
        total = total + mp_shift(piece, step, parts).astype(F32)
    return total


MESH = pl.DeviceIdType.MESH
VMEM_SPEC = pl.BlockSpec(memory_space=pltpu.VMEM)
ANY_SPEC = pl.BlockSpec(memory_space=pl.ANY)
DMA = pltpu.SemaphoreType.DMA


def place(depth, parts):
    me, part = lax.axis_index("dp"), lax.axis_index("mp")
    z, y, core = me // 4, lax.rem(me // 2, 2), lax.rem(me, 2)

    def dp_of(step, at_y, at_core):
        return lax.rem(z + step, depth) * 4 + at_y * 2 + at_core

    def mp_of(step):
        return lax.rem(part + step, parts)

    return me, part, z, y, core, dp_of, mp_of


def greet(depth, parts):
    me, part, z, y, core, dp_of, mp_of = place(depth, parts)
    near = [(dp_of(0, y, 1 - core), part), (dp_of(0, 1 - y, core), part)]
    near += [(dp_of(step, y, core), part) for step in range(1, depth)]
    near += [(me, mp_of(step)) for step in range(1, parts)]
    barrier = pltpu.get_barrier_semaphore()
    for device in near:
        pl.semaphore_signal(barrier, inc=1, device_id=device, device_id_type=MESH)
    pl.semaphore_wait(barrier, len(near))


def send(source, target, sems, at, device):
    sent, landed = sems
    return pltpu.make_async_remote_copy(
        src_ref=source,
        dst_ref=target,
        send_sem=sent.at[at],
        recv_sem=landed.at[at],
        device_id=device,
        device_id_type=MESH,
    )


def gather_kernel(depth, parts, count, *refs):
    shards, normed, cot = refs[:count], refs[count], refs[count + 1]
    weights, normed_all, cot_all = refs[count + 2 : 2 * count + 2], refs[-11], refs[-10]
    z_sent, z_got, y_sent, y_got, c_sent, c_got, x_sent, x_got, kept = refs[-9:]
    me, part, z, y, core, dp_of, mp_of = place(depth, parts)
    own = [
        pltpu.make_async_copy(shard, whole.at[me], kept.at[i])
        for i, (shard, whole) in enumerate(zip(shards, weights))
    ]
    own.append(pltpu.make_async_copy(normed, normed_all.at[part], kept.at[count]))
    own.append(pltpu.make_async_copy(cot, cot_all.at[part], kept.at[count + 1]))
    for copy in own:
        copy.start()
    greet(depth, parts)
    other_y, other_core = (dp_of(0, 1 - y, core), part), (dp_of(0, y, 1 - core), part)
    steps = [(step, i) for step in range(depth) for i in range(count)]

    along_z = [
        send(shards[i], weights[i].at[me], (z_sent, z_got), n, (dp_of(step, y, core), part))
        for n, (step, i) in enumerate(steps[count:])
    ]
    along_x = [
        send(source, target.at[part], (x_sent, x_got), i * (parts - 1) + step - 1,
             (me, mp_of(step)))
        for i, (source, target) in enumerate(((normed, normed_all), (cot, cot_all)))
        for step in range(1, parts)
    ]

    def block(step, i, at_y):
        return weights[i].at[dp_of(depth - step, at_y, core)]

    along_y, here_across, there_across = [], [], []
    for n, (step, i) in enumerate(steps):
        source = shards[i] if step == 0 else block(step, i, y)
        along_y.append(send(source, block(step, i, y), (y_sent, y_got), n, other_y))
        here_across.append(
            send(source, block(step, i, y), (c_sent, c_got), 2 * n, other_core)
        )
        there_across.append(
            send(block(step, i, 1 - y), block(step, i, 1 - y), (c_sent, c_got), 2 * n + 1,
                 other_core)
        )
    for copy in along_z:
        copy.start()
    for copy in along_y[:count] + here_across[:count]:
        copy.start()
    for copy in along_x:
        copy.start()
    for n in range(count, len(steps)):
        along_z[n - count].wait_recv()
        along_y[n].start()
        here_across[n].start()
    for n in range(len(steps)):
        along_y[n].wait_recv()
        there_across[n].start()
    for copy in along_x:
        copy.wait()
    for copy in along_z + along_y:
        copy.wait_send()
    for copy in here_across + there_across:
        copy.wait()
    for copy in own:
        copy.wait()


def gather_attn(shards, normed, cot):
    depth, parts, count = lax.axis_size("dp") // 4, lax.axis_size("mp"), len(shards)
    size = depth * 4
    return pl.pallas_call(
        functools.partial(gather_kernel, depth, parts, count),
        out_shape=[jax.ShapeDtypeStruct((size,) + shard.shape, shard.dtype) for shard in shards]
        + [jax.ShapeDtypeStruct((parts,) + rows.shape, rows.dtype) for rows in (normed, cot)],
        in_specs=[ANY_SPEC] * (count + 2),
        out_specs=[ANY_SPEC] * (count + 2),
        scratch_shapes=[DMA((count * (depth - 1),))] * 2 + [DMA((count * depth,))] * 2
        + [DMA((2 * count * depth,))] * 2 + [DMA((2 * (parts - 1),))] * 2 + [DMA((count + 2,))],
        compiler_params=pltpu.CompilerParams(collective_id=0, has_side_effects=True),
        name="gather_attn",
    )(*shards, normed, cot)


def add_rows(target, sources):
    def body(i, carry):
        here = pl.ds(pl.multiple_of(i * 16, 16), 16)
        total = sources[0][here, :].astype(F32)
        for source in sources[1:]:
            total = total + source[here, :].astype(F32)
        target[here, :] = total.astype(target.dtype)
        return carry

    lax.fori_loop(0, target.shape[0] // 16, body, 0)


SLOTS = 2


class Sums:
    def __init__(self, depth, parts, wholes, outs, scratch):
        self.depth, self.wholes, self.outs = depth, wholes, outs
        count = len(outs)
        self.held, self.ring, self.y_in, self.z_in = (
            scratch[i * count : (i + 1) * count] for i in range(4)
        )
        self.sems = scratch[4 * count :]
        self.order = [(step, k) for step in range(1, depth + 1) for k in range(count)]
        self.where = place(depth, parts)
        self.items = [self.item(n) for n in range(len(self.order))]

    @staticmethod
    def scratch(depth, blocks, computed):
        count = len(blocks)
        lead = (SLOTS, 2, 2) if computed else (SLOTS, 2)
        buffers = [pltpu.VMEM((depth, 2) + block, BF16) for block in blocks]
        buffers += [pltpu.VMEM(lead + block, BF16) for block in blocks]
        buffers += [pltpu.VMEM((depth,) + block, BF16) for block in blocks]
        buffers += [pltpu.VMEM((depth - 1,) + block, BF16) for block in blocks]
        return buffers + [DMA((depth * count,))] * 7

    def item(self, n):
        step, k = self.order[n]
        me, part, z, y, core, dp_of, mp_of = self.where
        at = lax.rem(z + step, self.depth)
        kept, c_sent, c_got, y_sent, y_got, z_sent, z_got = self.sems
        held, slot = self.held[k], (n // len(self.outs)) % SLOTS
        own = None
        if self.wholes is None:
            mine = self.ring[k].at[slot, :, core]
            give = self.ring[k].at[slot, :, 1 - core]
        else:
            mine = self.ring[k].at[slot]
            give = self.wholes[k].at[at, :, 1 - core]
            own = pltpu.make_async_copy(self.wholes[k].at[at, :, core], mine, kept.at[n])
        across = send(give, held.at[at], (c_sent, c_got), n, (dp_of(0, y, 1 - core), part))
        along_y = send(
            held.at[at, 1 - y], self.y_in[k].at[at], (y_sent, y_got), n,
            (dp_of(0, 1 - y, core), part),
        )
        along_z = None
        if step < self.depth:
            along_z = send(
                held.at[at, y], self.z_in[k].at[step - 1], (z_sent, z_got), n,
                (dp_of(step, y, core), part),
            )
        return at, k, slot, own, across, along_y, along_z

    def load(self, n):
        self.items[n][3].start()
        self.items[n][4].start()

    def begin(self):
        self.ahead = SLOTS * len(self.outs)
        for n in range(min(self.ahead, len(self.items))):
            self.load(n)

    def cross(self, n):
        core = self.where[4]
        at, k, slot, own, across, along_y, along_z = self.items[n]
        if own is not None:
            own.wait()
        across.wait_recv()
        for at_y in range(2):
            if own is not None:
                mine = self.ring[k].at[slot, at_y]
            else:
                mine = self.ring[k].at[slot, at_y, core]
            add_rows(self.held[k].at[at, at_y], (mine, self.held[k].at[at, at_y]))
        along_y.start()
        if own is not None and n + self.ahead < len(self.items):
            self.load(n + self.ahead)

    def onward(self, n):
        y = self.where[3]
        at, k, slot, own, across, along_y, along_z = self.items[n]
        along_y.wait_recv()
        held = self.held[k].at[at, y]
        add_rows(held, (held, self.y_in[k].at[at]))
        if along_z is not None:
            along_z.start()

    def end(self):
        z, y = self.where[2:4]
        for k, out in enumerate(self.outs):
            for item in self.items:
                if item[1] == k and item[6] is not None:
                    item[6].wait_recv()
            add_rows(
                out, [self.held[k].at[z, y]] + [self.z_in[k].at[i] for i in range(self.depth - 1)]
            )

    def drain(self, crossed=0):
        for n, (at, k, slot, own, across, along_y, along_z) in enumerate(self.items):
            if n >= crossed:
                across.wait_send()
            along_y.wait_send()
            if along_z is not None:
                along_z.wait_send()


class Gains:
    def __init__(self, depth, parts, held, around, sems):
        me, part, z, y, core, dp_of, mp_of = place(depth, parts)
        self.held = held
        stages = [
            [(dp_of(0, y, 1 - core), part)],
            [(me, mp_of(step)) for step in range(1, parts)],
            [(dp_of(step, y, core), part) for step in range(1, depth)],
            [(dp_of(0, 1 - y, core), part)],
        ]
        self.levels, slot = [], 0
        for number, stage in enumerate(stages):
            copies = []
            for device in stage:
                landing = around.at[pl.ds(16 * slot, 16)]
                source = held.at[pl.ds(16 * number, 16)]
                copies.append((send(source, landing, sems, slot, device), landing))
                slot += 1
            self.levels.append(copies)
        self.number = 0

    def begin(self):
        for copy, landing in self.levels[self.number]:
            copy.start()

    def advance(self):
        number = self.number
        if number == len(self.levels):
            return
        total = self.held[16 * number : 16 * number + 16]
        for copy, landing in self.levels[number]:
            copy.wait_recv()
            total = total + landing[...]
        self.held[16 * (number + 1) : 16 * (number + 2)] = total
        self.number += 1
        if self.number < len(self.levels):
            self.begin()

    def drain(self):
        for level in self.levels:
            for copy, landing in level:
                copy.wait_send()


def norm_back(rows_in, gain, gradient):
    factor = lax.rsqrt(jnp.mean(rows_in * rows_in, axis=-1, keepdims=True) + EPSILON)
    normed = rows_in * factor
    scaled = gradient * gain
    back = factor * (scaled - normed * jnp.mean(scaled * normed, axis=-1, keepdims=True))
    return back, gradient * normed


TILE = 16


def fold(terms):
    total = terms[0:8]
    for at in range(8, terms.shape[0], 8):
        total = total + terms[at : at + 8]
    return total


def tiles(rows, tile, body):
    def run(i, carry):
        body(pl.ds(pl.multiple_of(i * tile, tile), tile))
        return carry

    lax.fori_loop(0, rows // tile, run, 0)


def backward_kernel(depth, parts, heads, kv_heads, *refs):
    (gate, up, down, own_two_in, give_two, own_out_in, give_out, residual_in, cot_in, tokens_in,
     gain_one, gain_two, weights_in, out_w_in, normed_t_in, query_t_in, key_t_in, value_t_in,
     attended_in, id_col, id_row, cosine, sine) = refs[:23]
    (gate_out, up_out, down_out, attn_out, block_out, grad_tokens, gains, in_out) = refs[23:31]
    (work, work_out, residual, cot, tokens, weights, out_w, normed_t, query_t, key_t, value_t,
     attended, in_x, out_tile, branch, branch_t, grad_t, give_one, key_acc, value_acc, low,
     held, around, loaded, stored, two_sent, two_got, out_sent, out_got, b_sent, b_got,
     one_sent, one_got, g_sent, g_got) = refs[31:66]
    rest = refs[66:]
    me, part, z, y, core, dp_of, mp_of = place(depth, parts)
    rows, width = residual.shape
    group = rows * parts
    members = heads // kv_heads
    q_width, kv_width = heads * HEAD_SIZE, kv_heads * HEAD_SIZE
    all_width = q_width + 2 * kv_width
    half = HEAD_SIZE // 2
    scale = HEAD_SIZE ** (-0.5)
    mlp_refs = 4 * 3 + 7
    mlp = Sums(depth, parts, (gate, up, down), (gate_out, up_out, down_out), rest[:mlp_refs])
    attn = Sums(depth, parts, None, (attn_out,), rest[mlp_refs:])
    total_gains = Gains(depth, parts, held, around, (g_sent, g_got))

    pairs = [
        (own_two_in, work), (residual_in, residual), (cot_in, cot), (out_w_in, out_w),
        (query_t_in, query_t), (key_t_in, key_t), (value_t_in, value_t), (own_out_in, work_out),
        (weights_in, weights), (normed_t_in, normed_t), (attended_in, attended),
        (tokens_in, tokens),
    ]
    loads = [pltpu.make_async_copy(a, b, loaded.at[i]) for i, (a, b) in enumerate(pairs)]

    def along_x(source, target, sems):
        return [
            send(source(step), target(step), sems, step - 1, (me, mp_of(step)))
            for step in range(1, parts)
        ]

    to_two = along_x(lambda s: give_two.at[s - 1], lambda s: in_x.at[s - 1], (two_sent, two_got))
    to_out = along_x(lambda s: give_out.at[s - 1], lambda s: in_out.at[s - 1], (out_sent, out_got))
    to_branch = along_x(lambda s: branch.at[part], lambda s: branch.at[part], (b_sent, b_got))
    to_one = along_x(lambda s: give_one.at[s - 1], lambda s: in_x.at[s - 1], (one_sent, one_got))

    greet(depth, parts)
    for copy in to_two:
        copy.start()
    mlp.begin()
    for copy in loads:
        copy.start()
    items = len(mlp.items)
    early = min(8, items)
    for n in range(early):
        mlp.cross(n)
    for copy in loads[:3]:
        copy.wait()
    for copy in to_two:
        copy.wait_recv()

    held[0:16] = jnp.zeros((16, width), F32)

    def second(here):
        total = work[here, :]
        for step in range(parts - 1):
            total = total + in_x[step, here, :].astype(F32)
        back, terms = norm_back(residual[here, :], gain_two[...], total)
        held[8:16] += fold(terms)
        result = cot[here, :].astype(F32) + back
        work[here, :] = result
        branch[part, here, :] = result.astype(BF16)

    tiles(rows, TILE, second)
    for copy in to_branch + to_out:
        copy.start()
    for n in range(early, items):
        mlp.cross(n)
    mlp.onward(0)
    mlp.onward(1)
    for copy in to_branch:
        copy.wait()
    for copy in loads[3:7]:
        copy.wait()

    block = 256 if q_width % 256 == 0 else q_width
    for p in range(parts):
        across = slice(p * rows, (p + 1) * rows)
        for first in range(0, q_width, block):
            piece = jnp.dot(
                branch[p], out_w[:, first : first + block], preferred_element_type=F32
            )
            grad_t[first : first + block, across] = piece.T.astype(BF16)

        def turn(i, carry):
            here = pl.ds(pl.multiple_of(i * 128, 128), 128)
            branch_t[here, across] = branch[p, :, here].astype(F32).T.astype(BF16)
            return carry

        lax.fori_loop(0, width // 128, turn, 0)

    q_block = 256 if group <= 1024 else 128

    def one_kv_head(j, carry):
        kv_rows = pl.ds(pl.multiple_of(j * HEAD_SIZE, 32), HEAD_SIZE)
        key_acc[...] = jnp.zeros_like(key_acc)
        value_acc[...] = jnp.zeros_like(value_acc)
        for member in range(members):
            first = pl.multiple_of((j * members + member) * HEAD_SIZE, 32)
            head = pl.ds(first, HEAD_SIZE)
            for start in range(0, group, q_block):
                stop = start + q_block
                cols = slice(start, stop)
                query, grad = query_t[head, cols], grad_t[head, cols]
                key, value = key_t[kv_rows, :stop], value_t[kv_rows, :stop]
                scores = lax.dot_general(
                    query, key, (((0,), (0,)), ((), ())), preferred_element_type=F32
                )
                seen = id_col[cols, :] == id_row[:, :stop]
                at_row = start + lax.broadcasted_iota(jnp.int32, (q_block, stop), 0)
                at_col = lax.broadcasted_iota(jnp.int32, (q_block, stop), 1)
                scores = jnp.where(seen & (at_col <= at_row), scores * scale, MASKED)
                grown = jnp.exp(scores - jnp.max(scores, axis=-1, keepdims=True))
                probs = grown * (1.0 / jnp.sum(grown, axis=-1, keepdims=True))
                dprob = lax.dot_general(
                    grad, value, (((0,), (0,)), ((), ())), preferred_element_type=F32
                )
                inner = jnp.sum(probs * dprob, axis=-1, keepdims=True)
                dscore = (probs * (dprob - inner)).astype(BF16)
                key_acc[:, :stop] += jnp.dot(query, dscore, preferred_element_type=F32)
                value_acc[:, :stop] += jnp.dot(
                    grad, probs.astype(BF16), preferred_element_type=F32
                )
                dquery = scale * lax.dot_general(
                    key, dscore, (((1,), (1,)), ((), ())), preferred_element_type=F32
                )
                lead, tail = dquery[:half], dquery[half:]
                cos, sin = cosine[:, cols], sine[:, cols]
                grad_t[pl.ds(first, half), cols] = (lead * cos + tail * sin).astype(BF16)
                grad_t[pl.ds(first + half, half), cols] = (tail * cos - lead * sin).astype(BF16)
        lead, tail = key_acc[:half] * scale, key_acc[half:] * scale
        cos, sin = cosine[...], sine[...]
        first = pl.multiple_of(q_width + j * HEAD_SIZE, 32)
        grad_t[pl.ds(first, half), :] = (lead * cos + tail * sin).astype(BF16)
        grad_t[pl.ds(first + half, half), :] = (tail * cos - lead * sin).astype(BF16)
        first = pl.multiple_of(q_width + kv_width + j * HEAD_SIZE, 32)
        grad_t[pl.ds(first, HEAD_SIZE), :] = value_acc[...].astype(BF16)
        return carry

    cut = (kv_heads + 1) // 2
    lax.fori_loop(0, cut, one_kv_head, 0)
    mlp.onward(2)
    lax.fori_loop(cut, kv_heads, one_kv_head, 0)
    mlp.onward(3)

    def turn_back(i, carry):
        here = pl.ds(pl.multiple_of(i * 128, 128), 128)
        piece = grad_t[here, :].astype(F32).T.astype(BF16)
        for p in range(parts):
            branch[p, :, here] = piece[p * rows : (p + 1) * rows]
        return carry

    lax.fori_loop(0, all_width // 128, turn_back, 0)
    for copy in loads[7:]:
        copy.wait()

    def incoming(step, here):
        return lax.dot_general(
            branch[mp_of(step), :, :all_width], weights[here, :], (((1,), (1,)), ((), ())),
            preferred_element_type=F32,
        )

    for step in range(1, parts):
        for first in range(0, width, 512):
            give_one[step - 1, :, first : first + 512] = incoming(
                step, slice(first, first + 512)
            ).astype(BF16)
    for copy in to_one:
        copy.start()

    depth_rows = 4 * attn_out.shape[0]
    quarter = attn_out.shape[0]

    def weight_block(n):
        at, k, slot = attn.items[n][:3]
        lines = pl.ds(pl.multiple_of(at * depth_rows, 32), depth_rows)
        if n >= SLOTS:
            attn.items[n - SLOTS][4].wait_send()

        def put(value, first):
            for i in range(4):
                attn.ring[0][slot, i // 2, i % 2, :, first : first + value.shape[1]] = value[
                    i * quarter : (i + 1) * quarter
                ].astype(BF16)

        step = 512 if all_width % 512 == 0 else all_width
        for first in range(0, all_width, step):
            put(
                lax.dot_general(
                    normed_t[lines, :], grad_t[first : first + step, :],
                    (((1,), (1,)), ((), ())), preferred_element_type=F32,
                ),
                first,
            )
        put(jnp.dot(branch_t[lines, :], attended[...], preferred_element_type=F32), all_width)
        attn.items[n][4].start()

    done = 4
    for n in range(depth):
        weight_block(n)
        if n >= 1:
            attn.cross(n - 1)
        if done < items:
            mlp.onward(done)
            done += 1
    attn.cross(depth - 1)

    for copy in to_out:
        copy.wait_recv()
    tile = out_tile.shape[1]
    for first in range(0, rows, tile):
        fetch = pltpu.make_async_copy(in_out.at[:, pl.ds(first, tile)], out_tile, stored.at[0])
        fetch.start()
        fetch.wait()
        for line in range(first, first + tile, 16):
            here = slice(line, line + 16)
            total = work_out[here, :]
            for step in range(parts - 1):
                total = total + out_tile[step, line - first : line - first + 16, :].astype(F32)
            low[here, :] = (residual[here, :] + total).astype(BF16)
    put_out = pltpu.make_async_copy(low, block_out, stored.at[1])
    put_out.start()
    for first in range(0, width, 512):
        work_out[:, first : first + 512] = incoming(0, slice(first, first + 512))
    if done < items:
        mlp.onward(done)
        done += 1
    put_out.wait()

    for copy in to_one:
        copy.wait_recv()

    def first_norm(here):
        total = work_out[here, :]
        for step in range(parts - 1):
            total = total + in_x[step, here, :].astype(F32)
        back, terms = norm_back(tokens[here, :].astype(F32), gain_one[...], total)
        held[0:8] += fold(terms)
        low[here, :] = (work[here, :] + back).astype(BF16)

    tiles(rows, TILE, first_norm)
    put_tokens = pltpu.make_async_copy(low, grad_tokens, stored.at[2])
    put_tokens.start()
    total_gains.begin()
    while done < items:
        mlp.onward(done)
        done += 1
        total_gains.advance()
    while total_gains.number < 3:
        total_gains.advance()
    attn.onward(0)
    mlp.end()
    for n in range(1, depth):
        attn.onward(n)
    total_gains.advance()
    gains[...] = held[64:80]
    attn.end()
    put_tokens.wait()
    for copy in to_two + to_out + to_one:
        copy.wait_send()
    mlp.drain()
    attn.drain(crossed=max(depth - SLOTS, 0))
    total_gains.drain()


def backward(grads, own_two, give_two, own_out, give_out, residual, cot, tokens, gain_one,
             gain_two, weights, out_w, normed_t, query_t, key_t, value_t, attended, ids,
             cosine, sine):
    depth, parts = lax.axis_size("dp") // 4, lax.axis_size("mp")
    rows, width = residual.shape
    group = rows * parts
    wholes = [grad.reshape(depth, 2, 2, grad.shape[0] // (4 * depth), -1) for grad in grads]
    heads, kv_heads = query_t.shape[0] // HEAD_SIZE, key_t.shape[0] // HEAD_SIZE
    attn_block = (width // (4 * depth), weights.shape[1] + out_w.shape[1])
    stops = depth + parts
    loaded = (own_two, own_out, residual, cot, tokens, weights, out_w, normed_t, query_t, key_t,
              value_t, attended)
    outs = pl.pallas_call(
        functools.partial(backward_kernel, depth, parts, heads, kv_heads),
        out_shape=[jax.ShapeDtypeStruct(whole.shape[3:], F32) for whole in wholes]
        + [
            jax.ShapeDtypeStruct(attn_block, F32),
            jax.ShapeDtypeStruct((rows, width), BF16),
            jax.ShapeDtypeStruct((rows, width), BF16),
            jax.ShapeDtypeStruct((16, width), F32),
            jax.ShapeDtypeStruct((parts - 1, rows, width), BF16),
        ],
        in_specs=[ANY_SPEC] * 10 + [VMEM_SPEC] * 2 + [ANY_SPEC] * 7 + [VMEM_SPEC] * 4,
        out_specs=[VMEM_SPEC] * 4 + [ANY_SPEC] * 2 + [VMEM_SPEC, ANY_SPEC],
        scratch_shapes=[pltpu.VMEM(array.shape, array.dtype) for array in loaded]
        + [
            pltpu.VMEM((parts - 1, rows, width), BF16),
            pltpu.VMEM((parts - 1, 64, width), BF16),
            pltpu.VMEM((parts, rows, width), BF16),
            pltpu.VMEM((width, group), BF16),
            pltpu.VMEM((weights.shape[1], group), BF16),
            pltpu.VMEM((parts - 1, rows, width), BF16),
            pltpu.VMEM((HEAD_SIZE, group), F32),
            pltpu.VMEM((HEAD_SIZE, group), F32),
            pltpu.VMEM((rows, width), BF16),
            pltpu.VMEM((80, width), F32),
            pltpu.VMEM((16 * stops, width), F32),
            DMA((len(loaded),)),
            DMA((3,)),
        ]
        + [DMA((parts - 1,))] * 8 + [DMA((stops,))] * 2
        + Sums.scratch(depth, [whole.shape[3:] for whole in wholes], False)
        + Sums.scratch(depth, [attn_block], True),
        compiler_params=pltpu.CompilerParams(
            collective_id=1, has_side_effects=True, vmem_limit_bytes=63 * 2**20
        ),
        name="backward",
    )(*wholes, own_two, give_two, own_out, give_out, residual, cot, tokens, gain_one, gain_two,
      weights, out_w, normed_t, query_t, key_t, value_t, attended, *ids, cosine, sine)
    return outs[:7]


def own_and_give(whole, parts):
    me = lax.axis_index("mp")
    rows = whole.shape[0] // parts
    own = lax.dynamic_slice_in_dim(whole, me * rows, rows, 0)
    give = [
        lax.dynamic_slice_in_dim(whole, lax.rem(me + step, parts) * rows, rows, 0).astype(BF16)
        for step in range(1, parts)
    ]
    return own, jnp.stack(give)


def shards(
    tokens,
    seq_lengths,
    norm_attn,
    w_query,
    key_weight,
    value_weight,
    w_out,
    norm_mlp,
    w_gate,
    w_up,
    w_down,
    cotangent,
):
    parts = lax.axis_size("mp")
    rows = tokens.shape[0]
    group = rows * parts
    q_width, kv_width, hidden_width = w_query.shape[1], key_weight.shape[1], w_gate.shape[1]
    heads, kv_heads = q_width // HEAD_SIZE, kv_width // HEAD_SIZE
    members = heads // kv_heads
    factor = HEAD_SIZE ** (-0.5)

    width = tokens.shape[1]
    inputs = tokens.astype(F32)
    gain_one, gain_two = norm_attn.astype(F32), norm_mlp.astype(F32)
    mlp_shard = jnp.concatenate([w_gate, w_up, w_down.T], axis=1)
    attn_w, out_wt, normed_one, grad_rows = gather_attn(
        (jnp.concatenate([w_query, key_weight, value_weight], axis=1), w_out.T),
        (rms_parts(inputs)[1] * gain_one).astype(BF16),
        cotangent,
    )
    mlp_shard, attn_w = lax.optimization_barrier((mlp_shard, attn_w))
    mlp_w = lax.all_gather(mlp_shard, "dp", axis=0, tiled=True)
    attn_w, out_wt = attn_w.reshape(width, -1), out_wt.reshape(width, -1)
    normed_one, grad_rows = normed_one.reshape(group, width), grad_rows.reshape(group, width)
    cuts = (q_width, q_width + kv_width)
    query_w, key_w, value_w = jnp.split(attn_w, cuts, axis=1)
    gate_w, up_w, down_wt = jnp.split(mlp_w, 3, axis=1)

    segment, position = layout(seq_lengths[0], group)
    cosine, sine = rotation(position)
    places = jnp.arange(group, dtype=jnp.int32)
    allowed = (
        (places[:, None] >= places[None, :])
        & (segment[:, None] == segment[None, :])
        & ((segment[None, :] >= 0) | (places[:, None] == places[None, :]))
    )

    query = rotate(mul(normed_one, query_w).reshape(group, heads, HEAD_SIZE), cosine, sine)
    key = rotate(mul(normed_one, key_w).reshape(group, kv_heads, HEAD_SIZE), cosine, sine)
    value = mul(normed_one, value_w).astype(BF16).reshape(group, kv_heads, HEAD_SIZE)
    query = query.astype(BF16).reshape(group, kv_heads, members, HEAD_SIZE)
    key = key.astype(BF16)
    scores = jnp.einsum("qhgd,khd->hgqk", query, key, preferred_element_type=F32) * factor
    scores = jnp.where(allowed[None, None], scores, MASKED)
    peak = jnp.max(scores, axis=-1, keepdims=True)
    grown = jnp.exp(scores - peak)
    probs = grown / jnp.sum(grown, axis=-1, keepdims=True)
    probs_low = probs.astype(BF16)
    attended = (
        jnp.einsum("hgqk,khd->qhgd", probs_low, value, preferred_element_type=F32)
        .astype(BF16)
        .reshape(group, q_width)
    )
    residual = inputs + mp_sum_rows(mul_t(attended, out_wt), parts)
    normed_two = mp_gather((rms_parts(residual)[1] * gain_two).astype(BF16), parts)

    gate_act, up_act = mul(normed_two, gate_w), mul(normed_two, up_w)
    sigmoid_g = jax.nn.sigmoid(gate_act)
    swish = gate_act * sigmoid_g
    hidden = (swish * up_act).astype(BF16)
    branch = mul_t(hidden, down_wt)
    grad_hidden = mul(grad_rows, down_wt)
    grad_gate = (grad_hidden * up_act * sigmoid_g * (1.0 + gate_act * (1.0 - sigmoid_g))).astype(
        BF16
    )
    grad_up = (grad_hidden * swish).astype(BF16)
    grads_mlp = (
        outer_sum(normed_two, grad_gate).astype(BF16),
        outer_sum(normed_two, grad_up).astype(BF16),
        outer_sum(grad_rows, hidden).astype(BF16),
    )
    ids = jnp.where(segment >= 0, segment, 3 + places)
    grad_gate_w, grad_up_w, grad_down_w, grad_attn, block_out, grad_tokens, gains = backward(
        grads_mlp,
        *own_and_give(mul_t(grad_gate, gate_w) + mul_t(grad_up, up_w), parts),
        *own_and_give(branch, parts),
        residual,
        cotangent,
        tokens,
        gain_one[None, :],
        gain_two[None, :],
        attn_w,
        out_wt,
        normed_one.T,
        query.reshape(group, q_width).T,
        key.reshape(group, kv_width).T,
        value.reshape(group, kv_width).T,
        attended,
        (ids[:, None], ids[None, :]),
        cosine[:, 0, :].T,
        sine[:, 0, :].T,
    )
    attn_parts = jnp.split(grad_attn, cuts + (q_width + 2 * kv_width,), axis=1)
    gains = jnp.sum(gains.reshape(2, 8, width), axis=1)
    return (
        block_out,
        grad_tokens,
        gains[0],
        attn_parts[0],
        attn_parts[1],
        attn_parts[2],
        attn_parts[3].T,
        gains[1],
        grad_gate_w,
        grad_up_w,
        grad_down_w.T,
    )


def solution(mesh):
    rows, whole = P(("dp", "mp"), None), P()
    split, turned = P("dp", "mp"), P("mp", "dp")
    return jax.shard_map(
        shards,
        mesh=mesh,
        in_specs=(
            rows, P("dp", None), whole, split, split, split, turned, whole, split, split, turned, rows,
        ),
        out_specs=(
            rows, rows, whole, split, split, split, turned, whole, split, split, turned,
        ),
        check_vma=False,
    )
```

```python
import functools

import jax
import jax.numpy as jnp
from jax import lax
from jax.experimental import pallas as pl
from jax.experimental.pallas import tpu as pltpu
from jax.sharding import PartitionSpec as P

HEAD_SIZE = 96
EPSILON = 1e-05
ROPE_BASE = 100000.0
MASKED = -1e30
F32 = jnp.float32
BF16 = jnp.bfloat16


def layout(lengths, rows_total):
    places = jnp.arange(rows_total, dtype=jnp.int32)
    first_end = lengths[0]
    middle_end = lengths[0] + lengths[1]
    last_end = middle_end + lengths[2]
    segment = jnp.where(
        places < first_end,
        0,
        jnp.where(places < middle_end, 1, jnp.where(places < last_end, 2, -1)),
    ).astype(jnp.int32)
    offset = jnp.where(places < first_end, 0, jnp.where(places < middle_end, first_end, middle_end))
    position = jnp.where(segment >= 0, places - offset, 0)
    return segment, position


def rotation(position):
    half_dim = HEAD_SIZE // 2
    inverse = ROPE_BASE ** (-jnp.arange(half_dim, dtype=F32) * 2.0 / HEAD_SIZE)
    angles = position.astype(F32)[:, None] * inverse[None, :]
    return jnp.cos(angles)[:, None, :], jnp.sin(angles)[:, None, :]


def rotate(tensor, cosine, sine):
    half_dim = tensor.shape[-1] // 2
    lead, tail = tensor[..., :half_dim], tensor[..., half_dim:]
    return jnp.concatenate([lead * cosine - tail * sine, tail * cosine + lead * sine], axis=-1)


def rms_parts(inputs):
    factor = lax.rsqrt(jnp.mean(inputs * inputs, axis=-1, keepdims=True) + EPSILON)
    return factor, inputs * factor


def mul(left, right):
    return jnp.dot(left, right, preferred_element_type=F32)


def mul_t(left, right):
    return lax.dot_general(left, right, (((1,), (1,)), ((), ())), preferred_element_type=F32)


def outer_sum(left, right):
    return lax.dot_general(left, right, (((0,), (0,)), ((), ())), preferred_element_type=F32)


def mp_shift(block, step, parts):
    return lax.ppermute(block, "mp", [(i, (i + step) % parts) for i in range(parts)])


def mp_gather(block, parts):
    me = lax.axis_index("mp")
    rows = block.shape[0]
    whole = jnp.zeros((parts * rows,) + block.shape[1:], block.dtype)
    for step in range(parts):
        piece = block if step == 0 else mp_shift(block, step, parts)
        owner = lax.rem(me - step + parts, parts)
        whole = lax.dynamic_update_slice_in_dim(whole, piece, owner * rows, 0)
    return whole


def mp_sum_rows(whole, parts):
    me = lax.axis_index("mp")
    rows = whole.shape[0] // parts
    total = lax.dynamic_slice_in_dim(whole, me * rows, rows, 0)
    for step in range(1, parts):
        owner = lax.rem(me + step, parts)
        piece = lax.dynamic_slice_in_dim(whole, owner * rows, rows, 0).astype(BF16)
        total = total + mp_shift(piece, step, parts).astype(F32)
    return total


MESH = pl.DeviceIdType.MESH
VMEM_SPEC = pl.BlockSpec(memory_space=pltpu.VMEM)
ANY_SPEC = pl.BlockSpec(memory_space=pl.ANY)
DMA = pltpu.SemaphoreType.DMA


def place(depth, parts):
    me, part = lax.axis_index("dp"), lax.axis_index("mp")
    z, y, core = me // 4, lax.rem(me // 2, 2), lax.rem(me, 2)

    def dp_of(step, at_y, at_core):
        return lax.rem(z + step, depth) * 4 + at_y * 2 + at_core

    def mp_of(step):
        return lax.rem(part + step, parts)

    return me, part, z, y, core, dp_of, mp_of


def greet(depth, parts):
    me, part, z, y, core, dp_of, mp_of = place(depth, parts)
    near = [(dp_of(0, y, 1 - core), part), (dp_of(0, 1 - y, core), part)]
    near += [(dp_of(step, y, core), part) for step in range(1, depth)]
    near += [(me, mp_of(step)) for step in range(1, parts)]
    barrier = pltpu.get_barrier_semaphore()
    for device in near:
        pl.semaphore_signal(barrier, inc=1, device_id=device, device_id_type=MESH)
    pl.semaphore_wait(barrier, len(near))


def send(source, target, sems, at, device):
    sent, landed = sems
    return pltpu.make_async_remote_copy(
        src_ref=source,
        dst_ref=target,
        send_sem=sent.at[at],
        recv_sem=landed.at[at],
        device_id=device,
        device_id_type=MESH,
    )


class Gather:
    def __init__(self, depth, parts, shards, wholes, sems):
        self.depth, self.shards, self.wholes = depth, shards, wholes
        self.where = place(depth, parts)
        self.kept, self.z_sems, self.y_sems, self.c_sems = (
            sems[0], sems[1:3], sems[3:5], sems[5:7]
        )
        self.slots = 2 * depth - 1

    @staticmethod
    def semaphores(depth, count):
        slots = count * (2 * depth - 1)
        return [DMA((count,))] + [DMA((slots,))] * 4 + [DMA((2 * slots,))] * 2

    def block(self, i, move, at_y):
        me, part, z, y, core, dp_of, mp_of = self.where
        return self.wholes[i].at[(z + move) * 4 + at_y * 2 + core]

    def slot(self, move):
        return -move if move <= 0 else self.depth - 1 + move

    def source(self, i, move):
        return self.shards[i] if move == 0 else self.block(i, move, self.where[3])

    def along_z(self, i, move, ahead):
        me, part, z, y, core, dp_of, mp_of = self.where
        at = i * self.slots + self.slot(move - ahead)
        device = ((z + ahead) * 4 + y * 2 + core, part)
        return send(self.source(i, move), self.block(i, move, y), self.z_sems, at, device)

    def arrival(self, i, move):
        me, part, z, y, core, dp_of, mp_of = self.where
        at = i * self.slots + self.slot(move)
        block = self.block(i, move, y)
        return send(block, block, self.z_sems, at, (me, part))

    def along_y(self, i, move):
        me, part, z, y, core, dp_of, mp_of = self.where
        at = i * self.slots + self.slot(move)
        return send(self.source(i, move), self.block(i, move, y), self.y_sems, at,
                    (dp_of(0, 1 - y, core), part))

    def across(self, i, move, other):
        me, part, z, y, core, dp_of, mp_of = self.where
        at = 2 * (i * self.slots + self.slot(move)) + other
        at_y = 1 - y if other else y
        source = self.block(i, move, at_y) if other else self.source(i, move)
        return send(source, self.block(i, move, at_y), self.c_sems, at,
                    (dp_of(0, y, 1 - core), part))

    def there(self, move, action):
        z = self.where[2]
        if move == 0:
            action()
        else:
            pl.when((z + move >= 0) & (z + move < self.depth))(action)

    def begin(self, i):
        self.keep(i).start()
        for ahead in (1, -1):
            self.there(ahead, lambda ahead=ahead: self.along_z(i, 0, ahead).start())
        self.along_y(i, 0).start()
        self.across(i, 0, 0).start()

    def keep(self, i):
        return pltpu.make_async_copy(self.shards[i], self.wholes[i].at[self.where[0]],
                                     self.kept.at[i])

    def moves(self, step):
        return (0,) if step == 0 else (-step, step)

    def from_z(self, i, step):
        for move in self.moves(step):
            ahead = 1 if move < 0 else -1

            def pass_on(move=move, ahead=ahead):
                self.arrival(i, move).wait_recv()
                self.there(ahead, lambda: self.along_z(i, move, ahead).start())
                self.along_y(i, move).start()
                self.across(i, move, 0).start()

            self.there(move, pass_on)

    def from_y(self, i, step):
        for move in self.moves(step):

            def pass_on(move=move):
                self.along_y(i, move).wait_recv()
                self.across(i, move, 1).start()

            self.there(move, pass_on)

    def end(self, i):
        self.keep(i).wait()
        for step in range(self.depth):
            for move in self.moves(step):

                def settle(move=move):
                    self.across(i, move, 0).wait_recv()
                    self.across(i, move, 1).wait_recv()

                self.there(move, settle)

    def drain(self, i):
        for step in range(self.depth):
            for move in self.moves(step):

                def settle(move=move):
                    self.across(i, move, 0).wait_send()
                    self.across(i, move, 1).wait_send()
                    self.along_y(i, move).wait_send()
                    for ahead in (1, -1):
                        if move * ahead <= 0:
                            self.there(
                                ahead, lambda ahead=ahead: self.along_z(i, move, ahead).wait_send()
                            )

                self.there(move, settle)


def gather_kernel(depth, parts, count, *refs):
    shards, normed, cot = refs[:count], refs[count], refs[count + 1]
    weights = refs[count + 2 : 2 * count + 2]
    normed_all, cot_all, x_sent, x_got, kept = refs[2 * count + 2 : 2 * count + 7]
    me, part, z, y, core, dp_of, mp_of = place(depth, parts)
    work = Gather(depth, parts, shards, weights, refs[2 * count + 7 :])
    own = [
        pltpu.make_async_copy(normed, normed_all.at[part], kept.at[0]),
        pltpu.make_async_copy(cot, cot_all.at[part], kept.at[1]),
    ]
    greet(depth, parts)
    along_x = [
        send(source, target.at[part], (x_sent, x_got), i * (parts - 1) + step - 1,
             (me, mp_of(step)))
        for i, (source, target) in enumerate(((normed, normed_all), (cot, cot_all)))
        for step in range(1, parts)
    ]
    for i in range(count):
        work.begin(i)
    for copy in along_x + own:
        copy.start()
    for step in range(1, depth):
        for i in range(count):
            work.from_z(i, step)
        for i in range(count):
            work.from_y(i, step - 1)
    for i in range(count):
        work.from_y(i, depth - 1)
    for copy in along_x + own:
        copy.wait()
    for i in range(count):
        work.end(i)
    for i in range(count):
        work.drain(i)


def gather_attn(shards, normed, cot):
    depth, parts, count = lax.axis_size("dp") // 4, lax.axis_size("mp"), len(shards)
    size = depth * 4
    return pl.pallas_call(
        functools.partial(gather_kernel, depth, parts, count),
        out_shape=[jax.ShapeDtypeStruct((size,) + shard.shape, shard.dtype) for shard in shards]
        + [jax.ShapeDtypeStruct((parts,) + rows.shape, rows.dtype) for rows in (normed, cot)],
        in_specs=[VMEM_SPEC] * (count + 2),
        out_specs=[ANY_SPEC] * (count + 2),
        scratch_shapes=[DMA((2 * (parts - 1),))] * 2 + [DMA((2,))]
        + Gather.semaphores(depth, count),
        compiler_params=pltpu.CompilerParams(collective_id=0, has_side_effects=True),
        name="gather_attn",
    )(*shards, normed, cot)


def add_rows(target, sources):
    def body(i, carry):
        here = pl.ds(pl.multiple_of(i * 16, 16), 16)
        total = sources[0][here, :].astype(F32)
        for source in sources[1:]:
            total = total + source[here, :].astype(F32)
        target[here, :] = total.astype(target.dtype)
        return carry

    lax.fori_loop(0, target.shape[0] // 16, body, 0)


SLOTS = 2


class Sums:
    def __init__(self, depth, parts, wholes, outs, scratch):
        self.depth, self.wholes, self.outs = depth, wholes, outs
        count = len(outs)
        self.held, self.ring, self.y_in, self.z_in = (
            scratch[i * count : (i + 1) * count] for i in range(4)
        )
        self.sems = scratch[4 * count :]
        self.order = [(step, k) for step in range(1, depth + 1) for k in range(count)]
        self.where = place(depth, parts)
        self.items = [self.item(n) for n in range(len(self.order))]

    @staticmethod
    def scratch(depth, blocks, computed):
        count = len(blocks)
        lead = (SLOTS, 2, 2) if computed else (SLOTS, 2)
        buffers = [pltpu.VMEM((depth, 2) + block, BF16) for block in blocks]
        buffers += [pltpu.VMEM(lead + block, BF16) for block in blocks]
        buffers += [pltpu.VMEM((depth,) + block, BF16) for block in blocks]
        buffers += [pltpu.VMEM((depth - 1,) + block, BF16) for block in blocks]
        return buffers + [DMA((depth * count,))] * 7

    def item(self, n):
        step, k = self.order[n]
        me, part, z, y, core, dp_of, mp_of = self.where
        at = lax.rem(z + step, self.depth)
        kept, c_sent, c_got, y_sent, y_got, z_sent, z_got = self.sems
        held, slot = self.held[k], (n // len(self.outs)) % SLOTS
        own = None
        if self.wholes is None:
            mine = self.ring[k].at[slot, :, core]
            give = self.ring[k].at[slot, :, 1 - core]
        else:
            mine = self.ring[k].at[slot]
            give = self.wholes[k].at[at, :, 1 - core]
            own = pltpu.make_async_copy(self.wholes[k].at[at, :, core], mine, kept.at[n])
        across = send(give, held.at[at], (c_sent, c_got), n, (dp_of(0, y, 1 - core), part))
        along_y = send(
            held.at[at, 1 - y], self.y_in[k].at[at], (y_sent, y_got), n,
            (dp_of(0, 1 - y, core), part),
        )
        along_z = None
        if step < self.depth:
            along_z = send(
                held.at[at, y], self.z_in[k].at[step - 1], (z_sent, z_got), n,
                (dp_of(step, y, core), part),
            )
        return at, k, slot, own, across, along_y, along_z

    def load(self, n):
        self.items[n][3].start()
        self.items[n][4].start()

    def begin(self):
        self.ahead = SLOTS * len(self.outs)
        for n in range(min(self.ahead, len(self.items))):
            self.load(n)

    def cross(self, n):
        core = self.where[4]
        at, k, slot, own, across, along_y, along_z = self.items[n]
        if own is not None:
            own.wait()
        across.wait_recv()
        for at_y in range(2):
            if own is not None:
                mine = self.ring[k].at[slot, at_y]
            else:
                mine = self.ring[k].at[slot, at_y, core]
            add_rows(self.held[k].at[at, at_y], (mine, self.held[k].at[at, at_y]))
        along_y.start()
        if own is not None and n + self.ahead < len(self.items):
            self.load(n + self.ahead)

    def onward(self, n):
        y = self.where[3]
        at, k, slot, own, across, along_y, along_z = self.items[n]
        along_y.wait_recv()
        held = self.held[k].at[at, y]
        add_rows(held, (held, self.y_in[k].at[at]))
        if along_z is not None:
            along_z.start()

    def end(self):
        z, y = self.where[2:4]
        for k, out in enumerate(self.outs):
            for item in self.items:
                if item[1] == k and item[6] is not None:
                    item[6].wait_recv()
            add_rows(
                out, [self.held[k].at[z, y]] + [self.z_in[k].at[i] for i in range(self.depth - 1)]
            )

    def drain(self, crossed=0):
        for n, (at, k, slot, own, across, along_y, along_z) in enumerate(self.items):
            if n >= crossed:
                across.wait_send()
            along_y.wait_send()
            if along_z is not None:
                along_z.wait_send()


class Gains:
    def __init__(self, depth, parts, held, around, sems):
        me, part, z, y, core, dp_of, mp_of = place(depth, parts)
        self.held = held
        stages = [
            [(dp_of(0, y, 1 - core), part)],
            [(me, mp_of(step)) for step in range(1, parts)],
            [(dp_of(step, y, core), part) for step in range(1, depth)],
            [(dp_of(0, 1 - y, core), part)],
        ]
        self.levels, slot = [], 0
        for number, stage in enumerate(stages):
            copies = []
            for device in stage:
                landing = around.at[pl.ds(16 * slot, 16)]
                source = held.at[pl.ds(16 * number, 16)]
                copies.append((send(source, landing, sems, slot, device), landing))
                slot += 1
            self.levels.append(copies)
        self.number = 0

    def begin(self):
        for copy, landing in self.levels[self.number]:
            copy.start()

    def advance(self):
        number = self.number
        if number == len(self.levels):
            return
        total = self.held[16 * number : 16 * number + 16]
        for copy, landing in self.levels[number]:
            copy.wait_recv()
            total = total + landing[...]
        self.held[16 * (number + 1) : 16 * (number + 2)] = total
        self.number += 1
        if self.number < len(self.levels):
            self.begin()

    def drain(self):
        for level in self.levels:
            for copy, landing in level:
                copy.wait_send()


def norm_back(rows_in, gain, gradient):
    factor = lax.rsqrt(jnp.mean(rows_in * rows_in, axis=-1, keepdims=True) + EPSILON)
    normed = rows_in * factor
    scaled = gradient * gain
    back = factor * (scaled - normed * jnp.mean(scaled * normed, axis=-1, keepdims=True))
    return back, gradient * normed


TILE = 16


def fold(terms):
    total = terms[0:8]
    for at in range(8, terms.shape[0], 8):
        total = total + terms[at : at + 8]
    return total


def tiles(rows, tile, body):
    def run(i, carry):
        body(pl.ds(pl.multiple_of(i * tile, tile), tile))
        return carry

    lax.fori_loop(0, rows // tile, run, 0)


def backward_kernel(depth, parts, heads, kv_heads, *refs):
    (gate, up, down, own_two_in, give_two, own_out_in, give_out, residual_in, cot_in, tokens_in,
     gain_one, gain_two, weights_in, out_w_in, normed_t_in, query_t_in, key_t_in, value_t_in,
     attended_in, id_col, id_row, cosine, sine) = refs[:23]
    (gate_out, up_out, down_out, attn_out, block_out, grad_tokens, gains, in_out) = refs[23:31]
    (work, work_out, residual, cot, tokens, weights, out_w, normed_t, query_t, key_t, value_t,
     attended, in_x, out_tile, branch, branch_t, grad_t, give_one, key_acc, value_acc, low,
     held, around, loaded, stored, two_sent, two_got, out_sent, out_got, b_sent, b_got,
     one_sent, one_got, g_sent, g_got) = refs[31:66]
    rest = refs[66:]
    me, part, z, y, core, dp_of, mp_of = place(depth, parts)
    rows, width = residual.shape
    group = rows * parts
    members = heads // kv_heads
    q_width, kv_width = heads * HEAD_SIZE, kv_heads * HEAD_SIZE
    all_width = q_width + 2 * kv_width
    half = HEAD_SIZE // 2
    scale = HEAD_SIZE ** (-0.5)
    mlp_refs = 4 * 3 + 7
    mlp = Sums(depth, parts, (gate, up, down), (gate_out, up_out, down_out), rest[:mlp_refs])
    attn = Sums(depth, parts, None, (attn_out,), rest[mlp_refs:])
    total_gains = Gains(depth, parts, held, around, (g_sent, g_got))

    pairs = [
        (own_two_in, work), (residual_in, residual), (cot_in, cot), (out_w_in, out_w),
        (query_t_in, query_t), (key_t_in, key_t), (value_t_in, value_t), (own_out_in, work_out),
        (weights_in, weights), (normed_t_in, normed_t), (attended_in, attended),
        (tokens_in, tokens),
    ]
    loads = [pltpu.make_async_copy(a, b, loaded.at[i]) for i, (a, b) in enumerate(pairs)]

    def along_x(source, target, sems):
        return [
            send(source(step), target(step), sems, step - 1, (me, mp_of(step)))
            for step in range(1, parts)
        ]

    to_two = along_x(lambda s: give_two.at[s - 1], lambda s: in_x.at[s - 1], (two_sent, two_got))
    to_out = along_x(lambda s: give_out.at[s - 1], lambda s: in_out.at[s - 1], (out_sent, out_got))
    to_branch = along_x(lambda s: branch.at[part], lambda s: branch.at[part], (b_sent, b_got))
    to_one = along_x(lambda s: give_one.at[s - 1], lambda s: in_x.at[s - 1], (one_sent, one_got))

    greet(depth, parts)
    for copy in to_two:
        copy.start()
    mlp.begin()
    for copy in loads:
        copy.start()
    items = len(mlp.items)
    early = min(8, items)
    for n in range(early):
        mlp.cross(n)
    for copy in loads[:3]:
        copy.wait()
    for copy in to_two:
        copy.wait_recv()

    held[0:16] = jnp.zeros((16, width), F32)

    def second(here):
        total = work[here, :]
        for step in range(parts - 1):
            total = total + in_x[step, here, :].astype(F32)
        back, terms = norm_back(residual[here, :], gain_two[...], total)
        held[8:16] += fold(terms)
        result = cot[here, :].astype(F32) + back
        work[here, :] = result
        branch[part, here, :] = result.astype(BF16)

    tiles(rows, TILE, second)
    for copy in to_branch + to_out:
        copy.start()
    for n in range(early, items):
        mlp.cross(n)
    mlp.onward(0)
    mlp.onward(1)
    mlp.onward(2)
    for copy in to_branch:
        copy.wait()
    for copy in loads[3:7]:
        copy.wait()

    block = 256 if q_width % 256 == 0 else q_width
    for p in range(parts):
        across = slice(p * rows, (p + 1) * rows)
        for first in range(0, q_width, block):
            piece = jnp.dot(
                branch[p], out_w[:, first : first + block], preferred_element_type=F32
            )
            grad_t[first : first + block, across] = piece.T.astype(BF16)

        def turn(i, carry):
            here = pl.ds(pl.multiple_of(i * 128, 128), 128)
            branch_t[here, across] = branch[p, :, here].astype(F32).T.astype(BF16)
            return carry

        lax.fori_loop(0, width // 128, turn, 0)

    q_block = 256 if group <= 1024 else 128

    def one_kv_head(j):
        kv_rows = slice(j * HEAD_SIZE, (j + 1) * HEAD_SIZE)
        key_acc[...] = jnp.zeros_like(key_acc)
        value_acc[...] = jnp.zeros_like(value_acc)
        for member in range(members):
            first = (j * members + member) * HEAD_SIZE
            head = slice(first, first + HEAD_SIZE)
            for start in range(0, group, q_block):
                stop = start + q_block
                cols = slice(start, stop)
                query, grad = query_t[head, cols], grad_t[head, cols]
                key, value = key_t[kv_rows, :stop], value_t[kv_rows, :stop]
                scores = lax.dot_general(
                    query, key, (((0,), (0,)), ((), ())), preferred_element_type=F32
                )
                seen = id_col[cols, :] == id_row[:, :stop]
                at_row = start + lax.broadcasted_iota(jnp.int32, (q_block, stop), 0)
                at_col = lax.broadcasted_iota(jnp.int32, (q_block, stop), 1)
                scores = jnp.where(seen & (at_col <= at_row), scores * scale, MASKED)
                grown = jnp.exp(scores - jnp.max(scores, axis=-1, keepdims=True))
                probs = grown * (1.0 / jnp.sum(grown, axis=-1, keepdims=True))
                dprob = lax.dot_general(
                    grad, value, (((0,), (0,)), ((), ())), preferred_element_type=F32
                )
                inner = jnp.sum(probs * dprob, axis=-1, keepdims=True)
                dscore = (probs * (dprob - inner)).astype(BF16)
                key_acc[:, :stop] += jnp.dot(query, dscore, preferred_element_type=F32)
                value_acc[:, :stop] += jnp.dot(
                    grad, probs.astype(BF16), preferred_element_type=F32
                )
                dquery = scale * lax.dot_general(
                    key, dscore, (((1,), (1,)), ((), ())), preferred_element_type=F32
                )
                lead, tail = dquery[:half], dquery[half:]
                cos, sin = cosine[:, cols], sine[:, cols]
                grad_t[first : first + half, cols] = (lead * cos + tail * sin).astype(BF16)
                grad_t[first + half : first + HEAD_SIZE, cols] = (tail * cos - lead * sin).astype(BF16)
        lead, tail = key_acc[:half] * scale, key_acc[half:] * scale
        cos, sin = cosine[...], sine[...]
        first = q_width + j * HEAD_SIZE
        grad_t[first : first + half, :] = (lead * cos + tail * sin).astype(BF16)
        grad_t[first + half : first + HEAD_SIZE, :] = (tail * cos - lead * sin).astype(BF16)
        first = q_width + kv_width + j * HEAD_SIZE
        grad_t[first : first + HEAD_SIZE, :] = value_acc[...].astype(BF16)

    done = 3
    if done < items:
        mlp.onward(done)
        done += 1
    for j in range(kv_heads):
        one_kv_head(j)
        if done < items:
            mlp.onward(done)
            done += 1

    def turn_back(i, carry):
        here = pl.ds(pl.multiple_of(i * 128, 128), 128)
        piece = grad_t[here, :].astype(F32).T.astype(BF16)
        for p in range(parts):
            branch[p, :, here] = piece[p * rows : (p + 1) * rows]
        return carry

    lax.fori_loop(0, all_width // 128, turn_back, 0)
    for copy in loads[7:]:
        copy.wait()

    def incoming(step, here):
        return lax.dot_general(
            branch[mp_of(step), :, :all_width], weights[here, :], (((1,), (1,)), ((), ())),
            preferred_element_type=F32,
        )

    for step in range(1, parts):
        for first in range(0, width, 512):
            give_one[step - 1, :, first : first + 512] = incoming(
                step, slice(first, first + 512)
            ).astype(BF16)
    for copy in to_one:
        copy.start()

    depth_rows = 4 * attn_out.shape[0]
    quarter = attn_out.shape[0]

    def weight_block(n):
        at, k, slot = attn.items[n][:3]
        lines = pl.ds(pl.multiple_of(at * depth_rows, 32), depth_rows)
        if n >= SLOTS:
            attn.items[n - SLOTS][4].wait_send()

        def put(value, first):
            for i in range(4):
                attn.ring[0][slot, i // 2, i % 2, :, first : first + value.shape[1]] = value[
                    i * quarter : (i + 1) * quarter
                ].astype(BF16)

        step = 512 if all_width % 512 == 0 else all_width
        for first in range(0, all_width, step):
            put(
                lax.dot_general(
                    normed_t[lines, :], grad_t[first : first + step, :],
                    (((1,), (1,)), ((), ())), preferred_element_type=F32,
                ),
                first,
            )
        put(jnp.dot(branch_t[lines, :], attended[...], preferred_element_type=F32), all_width)
        attn.items[n][4].start()

    for n in range(depth):
        weight_block(n)
        if n >= 1:
            attn.cross(n - 1)
        if done < items:
            mlp.onward(done)
            done += 1
    attn.cross(depth - 1)

    for copy in to_out:
        copy.wait_recv()
    tile = out_tile.shape[1]
    for first in range(0, rows, tile):
        fetch = pltpu.make_async_copy(in_out.at[:, pl.ds(first, tile)], out_tile, stored.at[0])
        fetch.start()
        fetch.wait()
        for line in range(first, first + tile, 16):
            here = slice(line, line + 16)
            total = work_out[here, :]
            for step in range(parts - 1):
                total = total + out_tile[step, line - first : line - first + 16, :].astype(F32)
            low[here, :] = (residual[here, :] + total).astype(BF16)
    put_out = pltpu.make_async_copy(low, block_out, stored.at[1])
    put_out.start()
    for first in range(0, width, 512):
        work_out[:, first : first + 512] = incoming(0, slice(first, first + 512))
    if done < items:
        mlp.onward(done)
        done += 1
    put_out.wait()

    for copy in to_one:
        copy.wait_recv()

    def first_norm(here):
        total = work_out[here, :]
        for step in range(parts - 1):
            total = total + in_x[step, here, :].astype(F32)
        back, terms = norm_back(tokens[here, :].astype(F32), gain_one[...], total)
        held[0:8] += fold(terms)
        low[here, :] = (work[here, :] + back).astype(BF16)

    tiles(rows, TILE, first_norm)
    put_tokens = pltpu.make_async_copy(low, grad_tokens, stored.at[2])
    put_tokens.start()
    total_gains.begin()
    while done < items:
        mlp.onward(done)
        done += 1
        total_gains.advance()
    while total_gains.number < 3:
        total_gains.advance()
    attn.onward(0)
    mlp.end()
    for n in range(1, depth):
        attn.onward(n)
    total_gains.advance()
    gains[...] = held[64:80]
    attn.end()
    put_tokens.wait()
    for copy in to_two + to_out + to_one:
        copy.wait_send()
    mlp.drain()
    attn.drain(crossed=max(depth - SLOTS, 0))
    total_gains.drain()


def backward(grads, own_two, give_two, own_out, give_out, residual, cot, tokens, gain_one,
             gain_two, weights, out_w, normed_t, query_t, key_t, value_t, attended, ids,
             cosine, sine):
    depth, parts = lax.axis_size("dp") // 4, lax.axis_size("mp")
    rows, width = residual.shape
    group = rows * parts
    wholes = [grad.reshape(depth, 2, 2, grad.shape[0] // (4 * depth), -1) for grad in grads]
    heads, kv_heads = query_t.shape[0] // HEAD_SIZE, key_t.shape[0] // HEAD_SIZE
    attn_block = (width // (4 * depth), weights.shape[1] + out_w.shape[1])
    stops = depth + parts
    loaded = (own_two, own_out, residual, cot, tokens, weights, out_w, normed_t, query_t, key_t,
              value_t, attended)
    outs = pl.pallas_call(
        functools.partial(backward_kernel, depth, parts, heads, kv_heads),
        out_shape=[jax.ShapeDtypeStruct(whole.shape[3:], F32) for whole in wholes]
        + [
            jax.ShapeDtypeStruct(attn_block, F32),
            jax.ShapeDtypeStruct((rows, width), BF16),
            jax.ShapeDtypeStruct((rows, width), BF16),
            jax.ShapeDtypeStruct((16, width), F32),
            jax.ShapeDtypeStruct((parts - 1, rows, width), BF16),
        ],
        in_specs=[ANY_SPEC] * 10 + [VMEM_SPEC] * 2 + [ANY_SPEC] * 7 + [VMEM_SPEC] * 4,
        out_specs=[VMEM_SPEC] * 4 + [ANY_SPEC] * 2 + [VMEM_SPEC, ANY_SPEC],
        scratch_shapes=[pltpu.VMEM(array.shape, array.dtype) for array in loaded]
        + [
            pltpu.VMEM((parts - 1, rows, width), BF16),
            pltpu.VMEM((parts - 1, 64, width), BF16),
            pltpu.VMEM((parts, rows, width), BF16),
            pltpu.VMEM((width, group), BF16),
            pltpu.VMEM((weights.shape[1], group), BF16),
            pltpu.VMEM((parts - 1, rows, width), BF16),
            pltpu.VMEM((HEAD_SIZE, group), F32),
            pltpu.VMEM((HEAD_SIZE, group), F32),
            pltpu.VMEM((rows, width), BF16),
            pltpu.VMEM((80, width), F32),
            pltpu.VMEM((16 * stops, width), F32),
            DMA((len(loaded),)),
            DMA((3,)),
        ]
        + [DMA((parts - 1,))] * 8 + [DMA((stops,))] * 2
        + Sums.scratch(depth, [whole.shape[3:] for whole in wholes], False)
        + Sums.scratch(depth, [attn_block], True),
        compiler_params=pltpu.CompilerParams(
            collective_id=1, has_side_effects=True, vmem_limit_bytes=63 * 2**20
        ),
        name="backward",
    )(*wholes, own_two, give_two, own_out, give_out, residual, cot, tokens, gain_one, gain_two,
      weights, out_w, normed_t, query_t, key_t, value_t, attended, *ids, cosine, sine)
    return outs[:7]


def own_and_give(whole, parts):
    me = lax.axis_index("mp")
    rows = whole.shape[0] // parts
    own = lax.dynamic_slice_in_dim(whole, me * rows, rows, 0)
    give = [
        lax.dynamic_slice_in_dim(whole, lax.rem(me + step, parts) * rows, rows, 0).astype(BF16)
        for step in range(1, parts)
    ]
    return own, jnp.stack(give)


def shards(
    tokens,
    seq_lengths,
    norm_attn,
    w_query,
    key_weight,
    value_weight,
    w_out,
    norm_mlp,
    w_gate,
    w_up,
    w_down,
    cotangent,
):
    parts = lax.axis_size("mp")
    rows = tokens.shape[0]
    group = rows * parts
    q_width, kv_width, hidden_width = w_query.shape[1], key_weight.shape[1], w_gate.shape[1]
    heads, kv_heads = q_width // HEAD_SIZE, kv_width // HEAD_SIZE
    members = heads // kv_heads
    factor = HEAD_SIZE ** (-0.5)

    width = tokens.shape[1]
    inputs = tokens.astype(F32)
    gain_one, gain_two = norm_attn.astype(F32), norm_mlp.astype(F32)
    mlp_shard = jnp.concatenate([w_gate, w_up, w_down.T], axis=1)
    attn_w, out_wt, normed_one, grad_rows = gather_attn(
        (jnp.concatenate([w_query, key_weight, value_weight], axis=1), w_out.T),
        (rms_parts(inputs)[1] * gain_one).astype(BF16),
        cotangent,
    )
    mlp_shard, attn_w = lax.optimization_barrier((mlp_shard, attn_w))
    mlp_w = lax.all_gather(mlp_shard, "dp", axis=0, tiled=True)
    attn_w, out_wt = attn_w.reshape(width, -1), out_wt.reshape(width, -1)
    normed_one, grad_rows = normed_one.reshape(group, width), grad_rows.reshape(group, width)
    cuts = (q_width, q_width + kv_width)
    query_w, key_w, value_w = jnp.split(attn_w, cuts, axis=1)
    gate_w, up_w, down_wt = jnp.split(mlp_w, 3, axis=1)

    segment, position = layout(seq_lengths[0], group)
    cosine, sine = rotation(position)
    places = jnp.arange(group, dtype=jnp.int32)
    allowed = (
        (places[:, None] >= places[None, :])
        & (segment[:, None] == segment[None, :])
        & ((segment[None, :] >= 0) | (places[:, None] == places[None, :]))
    )

    query = rotate(mul(normed_one, query_w).reshape(group, heads, HEAD_SIZE), cosine, sine)
    key = rotate(mul(normed_one, key_w).reshape(group, kv_heads, HEAD_SIZE), cosine, sine)
    value = mul(normed_one, value_w).astype(BF16).reshape(group, kv_heads, HEAD_SIZE)
    query = query.astype(BF16).reshape(group, kv_heads, members, HEAD_SIZE)
    key = key.astype(BF16)
    scores = jnp.einsum("qhgd,khd->hgqk", query, key, preferred_element_type=F32) * factor
    scores = jnp.where(allowed[None, None], scores, MASKED)
    peak = jnp.max(scores, axis=-1, keepdims=True)
    grown = jnp.exp(scores - peak)
    probs = grown / jnp.sum(grown, axis=-1, keepdims=True)
    probs_low = probs.astype(BF16)
    attended = (
        jnp.einsum("hgqk,khd->qhgd", probs_low, value, preferred_element_type=F32)
        .astype(BF16)
        .reshape(group, q_width)
    )
    residual = inputs + mp_sum_rows(mul_t(attended, out_wt), parts)
    normed_two = mp_gather((rms_parts(residual)[1] * gain_two).astype(BF16), parts)

    gate_act, up_act = mul(normed_two, gate_w), mul(normed_two, up_w)
    sigmoid_g = jax.nn.sigmoid(gate_act)
    swish = gate_act * sigmoid_g
    hidden = (swish * up_act).astype(BF16)
    branch = mul_t(hidden, down_wt)
    grad_hidden = mul(grad_rows, down_wt)
    grad_gate = (grad_hidden * up_act * sigmoid_g * (1.0 + gate_act * (1.0 - sigmoid_g))).astype(
        BF16
    )
    grad_up = (grad_hidden * swish).astype(BF16)
    grads_mlp = (
        outer_sum(normed_two, grad_gate).astype(BF16),
        outer_sum(normed_two, grad_up).astype(BF16),
        outer_sum(grad_rows, hidden).astype(BF16),
    )
    ids = jnp.where(segment >= 0, segment, 3 + places)
    grad_gate_w, grad_up_w, grad_down_w, grad_attn, block_out, grad_tokens, gains = backward(
        grads_mlp,
        *own_and_give(mul_t(grad_gate, gate_w) + mul_t(grad_up, up_w), parts),
        *own_and_give(branch, parts),
        residual,
        cotangent,
        tokens,
        gain_one[None, :],
        gain_two[None, :],
        attn_w,
        out_wt,
        normed_one.T,
        query.reshape(group, q_width).T,
        key.reshape(group, kv_width).T,
        value.reshape(group, kv_width).T,
        attended,
        (ids[:, None], ids[None, :]),
        cosine[:, 0, :].T,
        sine[:, 0, :].T,
    )
    attn_parts = jnp.split(grad_attn, cuts + (q_width + 2 * kv_width,), axis=1)
    gains = jnp.sum(gains.reshape(2, 8, width), axis=1)
    return (
        block_out,
        grad_tokens,
        gains[0],
        attn_parts[0],
        attn_parts[1],
        attn_parts[2],
        attn_parts[3].T,
        gains[1],
        grad_gate_w,
        grad_up_w,
        grad_down_w.T,
    )


def solution(mesh):
    rows, whole = P(("dp", "mp"), None), P()
    split, turned = P("dp", "mp"), P("mp", "dp")
    return jax.shard_map(
        shards,
        mesh=mesh,
        in_specs=(
            rows, P("dp", None), whole, split, split, split, turned, whole, split, split, turned, rows,
        ),
        out_specs=(
            rows, rows, whole, split, split, split, turned, whole, split, split, turned,
        ),
        check_vma=False,
    )
```

```python
import functools

import jax
import jax.numpy as jnp
from jax import lax
from jax.experimental import pallas as pl
from jax.experimental.pallas import tpu as pltpu
from jax.sharding import PartitionSpec as P

HEAD_SIZE = 96
EPSILON = 1e-05
ROPE_BASE = 100000.0
MASKED = -1e30
F32 = jnp.float32
BF16 = jnp.bfloat16


def layout(lengths, rows_total):
    places = jnp.arange(rows_total, dtype=jnp.int32)
    first_end = lengths[0]
    middle_end = lengths[0] + lengths[1]
    last_end = middle_end + lengths[2]
    segment = jnp.where(
        places < first_end,
        0,
        jnp.where(places < middle_end, 1, jnp.where(places < last_end, 2, -1)),
    ).astype(jnp.int32)
    offset = jnp.where(places < first_end, 0, jnp.where(places < middle_end, first_end, middle_end))
    position = jnp.where(segment >= 0, places - offset, 0)
    return segment, position


def rotation(position):
    half_dim = HEAD_SIZE // 2
    inverse = ROPE_BASE ** (-jnp.arange(half_dim, dtype=F32) * 2.0 / HEAD_SIZE)
    angles = position.astype(F32)[:, None] * inverse[None, :]
    return jnp.cos(angles)[:, None, :], jnp.sin(angles)[:, None, :]


def rotate(tensor, cosine, sine):
    half_dim = tensor.shape[-1] // 2
    lead, tail = tensor[..., :half_dim], tensor[..., half_dim:]
    return jnp.concatenate([lead * cosine - tail * sine, tail * cosine + lead * sine], axis=-1)


def rms_parts(inputs):
    factor = lax.rsqrt(jnp.mean(inputs * inputs, axis=-1, keepdims=True) + EPSILON)
    return factor, inputs * factor


def mul(left, right):
    return jnp.dot(left, right, preferred_element_type=F32)


def mul_t(left, right):
    return lax.dot_general(left, right, (((1,), (1,)), ((), ())), preferred_element_type=F32)


def outer_sum(left, right):
    return lax.dot_general(left, right, (((0,), (0,)), ((), ())), preferred_element_type=F32)


def mp_shift(block, step, parts):
    return lax.ppermute(block, "mp", [(i, (i + step) % parts) for i in range(parts)])


def mp_gather(block, parts):
    me = lax.axis_index("mp")
    rows = block.shape[0]
    whole = jnp.zeros((parts * rows,) + block.shape[1:], block.dtype)
    for step in range(parts):
        piece = block if step == 0 else mp_shift(block, step, parts)
        owner = lax.rem(me - step + parts, parts)
        whole = lax.dynamic_update_slice_in_dim(whole, piece, owner * rows, 0)
    return whole


def mp_sum_rows(whole, parts):
    me = lax.axis_index("mp")
    rows = whole.shape[0] // parts
    total = lax.dynamic_slice_in_dim(whole, me * rows, rows, 0)
    for step in range(1, parts):
        owner = lax.rem(me + step, parts)
        piece = lax.dynamic_slice_in_dim(whole, owner * rows, rows, 0).astype(BF16)
        total = total + mp_shift(piece, step, parts).astype(F32)
    return total


MESH = pl.DeviceIdType.MESH
VMEM_SPEC = pl.BlockSpec(memory_space=pltpu.VMEM)
ANY_SPEC = pl.BlockSpec(memory_space=pl.ANY)
DMA = pltpu.SemaphoreType.DMA


def place(depth, parts):
    me, part = lax.axis_index("dp"), lax.axis_index("mp")
    z, y, core = me // 4, lax.rem(me // 2, 2), lax.rem(me, 2)

    def dp_of(step, at_y, at_core):
        return lax.rem(z + step, depth) * 4 + at_y * 2 + at_core

    def mp_of(step):
        return lax.rem(part + step, parts)

    return me, part, z, y, core, dp_of, mp_of


def flipped(value, mask):
    result = value
    for bit in (1 << i for i in range(mask.bit_length())):
        if mask & bit:
            result = result + bit * (1 - 2 * lax.rem(value // bit, 2))
    return result


def lowest(mask):
    return mask & -mask


def masks(depth):
    return sorted(range(1, depth), key=lambda m: (lowest(m), -m)) + [0]


def greet(depth, parts):
    me, part, z, y, core, dp_of, mp_of = place(depth, parts)
    near = [(dp_of(0, y, 1 - core), part), (dp_of(0, 1 - y, core), part)]
    near += [(dp_of(step, y, core), part) for step in range(1, depth)]
    near += [(me, mp_of(step)) for step in range(1, parts)]
    barrier = pltpu.get_barrier_semaphore()
    for device in near:
        pl.semaphore_signal(barrier, inc=1, device_id=device, device_id_type=MESH)
    pl.semaphore_wait(barrier, len(near))


def send(source, target, sems, at, device):
    sent, landed = sems
    return pltpu.make_async_remote_copy(
        src_ref=source,
        dst_ref=target,
        send_sem=sent.at[at],
        recv_sem=landed.at[at],
        device_id=device,
        device_id_type=MESH,
    )


class Gather:
    def __init__(self, depth, parts, shards, wholes, sems):
        self.depth, self.shards, self.wholes = depth, shards, wholes
        self.where = place(depth, parts)
        self.kept, self.z_sems, self.y_sems, self.c_sems = (
            sems[0], sems[1:3], sems[3:5], sems[5:7]
        )
        self.slots = 2 * depth - 1

    @staticmethod
    def semaphores(depth, count):
        slots = count * (2 * depth - 1)
        return [DMA((count,))] + [DMA((slots,))] * 4 + [DMA((2 * slots,))] * 2

    def block(self, i, move, at_y):
        me, part, z, y, core, dp_of, mp_of = self.where
        return self.wholes[i].at[(z + move) * 4 + at_y * 2 + core]

    def slot(self, move):
        return -move if move <= 0 else self.depth - 1 + move

    def source(self, i, move):
        return self.shards[i] if move == 0 else self.block(i, move, self.where[3])

    def along_z(self, i, move, ahead):
        me, part, z, y, core, dp_of, mp_of = self.where
        at = i * self.slots + self.slot(move - ahead)
        device = ((z + ahead) * 4 + y * 2 + core, part)
        return send(self.source(i, move), self.block(i, move, y), self.z_sems, at, device)

    def arrival(self, i, move):
        me, part, z, y, core, dp_of, mp_of = self.where
        at = i * self.slots + self.slot(move)
        block = self.block(i, move, y)
        return send(block, block, self.z_sems, at, (me, part))

    def along_y(self, i, move):
        me, part, z, y, core, dp_of, mp_of = self.where
        at = i * self.slots + self.slot(move)
        return send(self.source(i, move), self.block(i, move, y), self.y_sems, at,
                    (dp_of(0, 1 - y, core), part))

    def across(self, i, move, other):
        me, part, z, y, core, dp_of, mp_of = self.where
        at = 2 * (i * self.slots + self.slot(move)) + other
        at_y = 1 - y if other else y
        source = self.block(i, move, at_y) if other else self.source(i, move)
        return send(source, self.block(i, move, at_y), self.c_sems, at,
                    (dp_of(0, y, 1 - core), part))

    def there(self, move, action):
        z = self.where[2]
        if move == 0:
            action()
        else:
            pl.when((z + move >= 0) & (z + move < self.depth))(action)

    def begin(self, i):
        self.keep(i).start()
        for ahead in (1, -1):
            self.there(ahead, lambda ahead=ahead: self.along_z(i, 0, ahead).start())
        self.along_y(i, 0).start()
        self.across(i, 0, 0).start()

    def keep(self, i):
        return pltpu.make_async_copy(self.shards[i], self.wholes[i].at[self.where[0]],
                                     self.kept.at[i])

    def moves(self, step):
        return (0,) if step == 0 else (-step, step)

    def from_z(self, i, step):
        for move in self.moves(step):
            ahead = 1 if move < 0 else -1

            def pass_on(move=move, ahead=ahead):
                self.arrival(i, move).wait_recv()
                self.there(ahead, lambda: self.along_z(i, move, ahead).start())
                self.along_y(i, move).start()
                self.across(i, move, 0).start()

            self.there(move, pass_on)

    def from_y(self, i, step):
        for move in self.moves(step):

            def pass_on(move=move):
                self.along_y(i, move).wait_recv()
                self.across(i, move, 1).start()

            self.there(move, pass_on)

    def end(self, i):
        self.keep(i).wait()
        for step in range(self.depth):
            for move in self.moves(step):

                def settle(move=move):
                    self.across(i, move, 0).wait_recv()
                    self.across(i, move, 1).wait_recv()

                self.there(move, settle)

    def drain(self, i):
        for step in range(self.depth):
            for move in self.moves(step):

                def settle(move=move):
                    self.across(i, move, 0).wait_send()
                    self.across(i, move, 1).wait_send()
                    self.along_y(i, move).wait_send()
                    for ahead in (1, -1):
                        if move * ahead <= 0:
                            self.there(
                                ahead, lambda ahead=ahead: self.along_z(i, move, ahead).wait_send()
                            )

                self.there(move, settle)


def gather_kernel(depth, parts, count, *refs):
    shards, normed, cot = refs[:count], refs[count], refs[count + 1]
    weights = refs[count + 2 : 2 * count + 2]
    normed_all, cot_all, x_sent, x_got, kept = refs[2 * count + 2 : 2 * count + 7]
    me, part, z, y, core, dp_of, mp_of = place(depth, parts)
    work = Gather(depth, parts, shards, weights, refs[2 * count + 7 :])
    own = [
        pltpu.make_async_copy(normed, normed_all.at[part], kept.at[0]),
        pltpu.make_async_copy(cot, cot_all.at[part], kept.at[1]),
    ]
    greet(depth, parts)
    along_x = [
        send(source, target.at[part], (x_sent, x_got), i * (parts - 1) + step - 1,
             (me, mp_of(step)))
        for i, (source, target) in enumerate(((normed, normed_all), (cot, cot_all)))
        for step in range(1, parts)
    ]
    for i in range(count):
        work.begin(i)
    for copy in along_x + own:
        copy.start()
    for step in range(1, depth):
        for i in range(count):
            work.from_z(i, step)
        for i in range(count):
            work.from_y(i, step - 1)
    for i in range(count):
        work.from_y(i, depth - 1)
    for copy in along_x + own:
        copy.wait()
    for i in range(count):
        work.end(i)
    for i in range(count):
        work.drain(i)


def gather_attn(shards, normed, cot):
    depth, parts, count = lax.axis_size("dp") // 4, lax.axis_size("mp"), len(shards)
    size = depth * 4
    return pl.pallas_call(
        functools.partial(gather_kernel, depth, parts, count),
        out_shape=[jax.ShapeDtypeStruct((size,) + shard.shape, shard.dtype) for shard in shards]
        + [jax.ShapeDtypeStruct((parts,) + rows.shape, rows.dtype) for rows in (normed, cot)],
        in_specs=[VMEM_SPEC] * (count + 2),
        out_specs=[ANY_SPEC] * (count + 2),
        scratch_shapes=[DMA((2 * (parts - 1),))] * 2 + [DMA((2,))]
        + Gather.semaphores(depth, count),
        compiler_params=pltpu.CompilerParams(collective_id=0, has_side_effects=True),
        name="gather_attn",
    )(*shards, normed, cot)


def add_rows(target, sources):
    def body(i, carry):
        here = pl.ds(pl.multiple_of(i * 16, 16), 16)
        total = sources[0][here, :].astype(F32)
        for source in sources[1:]:
            total = total + source[here, :].astype(F32)
        target[here, :] = total.astype(target.dtype)
        return carry

    lax.fori_loop(0, target.shape[0] // 16, body, 0)


class Ring:
    def __init__(self, buffer):
        self.buffer, self.users, self.next = buffer, [None] * buffer.shape[0], 0

    def take(self, copy):
        slot = self.next
        if self.users[slot] is not None:
            self.users[slot].wait_send()
        self.users[slot] = copy
        self.next = (slot + 1) % len(self.users)

    def peek(self, ahead):
        return (self.next + ahead) % len(self.users)

    def drain(self):
        for copy in self.users:
            if copy is not None:
                copy.wait_send()


class Sums:
    def __init__(self, depth, parts, order, widths, rows, refs, wholes, ring, start, outs):
        self.depth, self.wholes, self.outs, self.order = depth, wholes, outs, order
        self.rows, self.widths, self.ring = rows, widths, ring
        count = len(widths)
        self.held = refs[:count]
        self.y_in, self.z_in = refs[count : 2 * count], refs[2 * count : 3 * count]
        self.y_tile, self.z_tile, self.stage = refs[3 * count : 3 * count + 3]
        self.sems = refs[3 * count + 3 :]
        self.where = place(depth, parts)
        slots = len(ring.users)
        self.slots = [(start + n) % slots for n in range(len(order))]
        self.items = [self.item(n) for n in range(len(order))]
        self.crossed = self.passed = 0
        self.pending = self.putting = None

    @staticmethod
    def held_shapes(depth, widths, rows):
        return [pltpu.VMEM((depth, 2, rows, width), BF16) for width in widths]

    @staticmethod
    def landing_shapes(depth, widths, rows):
        return [jax.ShapeDtypeStruct((depth, rows, width), BF16) for width in widths] + [
            jax.ShapeDtypeStruct((depth - 1, rows, width), BF16) for width in widths
        ]

    @staticmethod
    def tiles(depth, widths, rows):
        wide = max(widths)
        return [
            pltpu.VMEM((rows, wide), BF16),
            pltpu.VMEM((depth - 1, rows, wide), BF16),
            pltpu.VMEM((rows, wide), F32),
        ] + [DMA((depth * len(widths),))] * 7 + [DMA((depth + 2,))]

    def item(self, n):
        k, mask = self.order[n]
        me, part, z, y, core, dp_of, mp_of = self.where
        at = flipped(z, mask)
        kept, c_sent, c_got, y_sent, y_got, z_sent, z_got, moved = self.sems
        held, width = self.held[k], self.widths[k]
        every, slot = pl.ds(0, width), self.slots[n]
        own = None
        if self.wholes is None:
            give = self.ring.buffer.at[slot, :, 1 - core, :, every]
        else:
            give = self.wholes[k].at[at, :, 1 - core]
            own = pltpu.make_async_copy(
                self.wholes[k].at[at, :, core], self.ring.buffer.at[slot], kept.at[n]
            )
        across = send(give, held.at[at], (c_sent, c_got), n, (dp_of(0, y, 1 - core), part))
        along_y = send(
            held.at[at, 1 - y], self.y_in[k].at[at], (y_sent, y_got), n,
            (dp_of(0, 1 - y, core), part),
        )
        along_z = None
        if mask > 0:
            along_z = send(
                held.at[at, y], self.z_in[k].at[mask - 1], (z_sent, z_got), n,
                (flipped(z, lowest(mask)) * 4 + y * 2 + core, part),
            )
        return at, k, own, across, along_y, along_z

    def load(self, n):
        at, k, own, across, along_y, along_z = self.items[n]
        self.ring.take(across)
        own.start()
        across.start()

    def begin(self):
        self.ahead = min(len(self.ring.users), len(self.items))
        for n in range(self.ahead):
            self.load(n)

    def slot_for(self, n):
        self.ring.take(self.items[n][3])
        return self.ring.buffer.at[self.slots[n]]

    def cross(self):
        core = self.where[4]
        n = self.crossed
        self.crossed += 1
        at, k, own, across, along_y, along_z = self.items[n]
        if own is not None:
            own.wait()
        across.wait_recv()
        for at_y in range(2):
            if own is not None:
                mine = self.ring.buffer.at[self.slots[n], at_y]
            else:
                mine = self.ring.buffer.at[self.slots[n], at_y, core, :, pl.ds(0, self.widths[k])]
            held = self.held[k].at[at, at_y]
            add_rows(held, (mine, held))
        along_y.start()
        if own is not None and n + self.ahead < len(self.items):
            self.load(n + self.ahead)

    def onward(self):
        self.settle()
        n = self.passed
        if n >= self.crossed:
            return
        self.passed += 1
        moved = self.sems[7]
        at, k, own, across, along_y, along_z = self.items[n]
        mask, every = self.order[n][1], pl.ds(0, self.widths[k])
        along_y.wait_recv()
        tile = self.y_tile.at[:, every]
        fetches = [pltpu.make_async_copy(self.y_in[k].at[at], tile, moved.at[0])]
        fetches[0].start()
        tiles_in = [tile]
        if mask > 0:
            more, from_z = self.from_z(k, mask)
            fetches += more
            tiles_in += from_z
        self.pending = n, fetches, tiles_in

    def settle(self):
        if self.pending is None:
            return
        n, fetches, landed = self.pending
        self.pending = None
        at, k, own, across, along_y, along_z = self.items[n]
        for fetch in fetches:
            fetch.wait()
        held = self.held[k].at[at, self.where[3]]
        add_rows(held, [held] + landed)
        if along_z is not None:
            along_z.start()

    def from_z(self, k, mask):
        moved, every = self.sems[7], pl.ds(0, self.widths[k])
        fetches, landed = [], []
        bit = 1
        while bit < (lowest(mask) if mask else self.depth):
            sender = mask ^ bit
            self.items[self.order.index((k, sender))][5].wait_recv()
            tile = self.z_tile.at[len(landed), :, every]
            fetch = pltpu.make_async_copy(
                self.z_in[k].at[sender - 1], tile, moved.at[1 + len(landed)]
            )
            fetch.start()
            fetches.append(fetch)
            landed.append(tile)
            bit *= 2
        return fetches, landed

    def finish(self, k):
        self.settle()
        z, y = self.where[2:4]
        moved, every = self.sems[7], pl.ds(0, self.widths[k])
        fetches, landed = self.from_z(k, 0)
        for fetch in fetches:
            fetch.wait()
        stage = self.stage.at[:, every]
        if self.putting is not None:
            self.putting.wait()
        add_rows(stage, [self.held[k].at[z, y]] + landed)
        self.putting = pltpu.make_async_copy(stage, self.outs[k], moved.at[self.depth + 1])
        self.putting.start()

    def drain(self):
        self.putting.wait()
        for at, k, own, across, along_y, along_z in self.items:
            along_y.wait_send()
            if along_z is not None:
                along_z.wait_send()


class Gains:
    def __init__(self, depth, parts, held, around, sems):
        me, part, z, y, core, dp_of, mp_of = place(depth, parts)
        self.held = held
        stages = [
            [(dp_of(0, y, 1 - core), part)],
            [(me, mp_of(step)) for step in range(1, parts)],
            [(dp_of(step, y, core), part) for step in range(1, depth)],
            [(dp_of(0, 1 - y, core), part)],
        ]
        self.levels, slot = [], 0
        for number, stage in enumerate(stages):
            copies = []
            for device in stage:
                landing = around.at[pl.ds(16 * slot, 16)]
                source = held.at[pl.ds(16 * number, 16)]
                copies.append((send(source, landing, sems, slot, device), landing))
                slot += 1
            self.levels.append(copies)
        self.number = 0

    def begin(self):
        for copy, landing in self.levels[self.number]:
            copy.start()

    def advance(self):
        number = self.number
        if number == len(self.levels):
            return
        total = self.held[16 * number : 16 * number + 16]
        for copy, landing in self.levels[number]:
            copy.wait_recv()
            total = total + landing[...]
        self.held[16 * (number + 1) : 16 * (number + 2)] = total
        self.number += 1
        if self.number < len(self.levels):
            self.begin()

    def drain(self):
        for level in self.levels:
            for copy, landing in level:
                copy.wait_send()


def norm_back(rows_in, gain, gradient):
    factor = lax.rsqrt(jnp.mean(rows_in * rows_in, axis=-1, keepdims=True) + EPSILON)
    normed = rows_in * factor
    scaled = gradient * gain
    back = factor * (scaled - normed * jnp.mean(scaled * normed, axis=-1, keepdims=True))
    return back, gradient * normed


TILE = 16


def fold(terms):
    total = terms[0:8]
    for at in range(8, terms.shape[0], 8):
        total = total + terms[at : at + 8]
    return total


def tiles(rows, tile, body):
    def run(i, carry):
        body(pl.ds(pl.multiple_of(i * tile, tile), tile))
        return carry

    lax.fori_loop(0, rows // tile, run, 0, unroll=4)


def dot_nt(left, right):
    return lax.dot_general(
        left, right, (((1,), (1,)), ((), ())), preferred_element_type=F32
    )


class Named(dict):
    __getattr__ = dict.get


def backward_kernel(depth, parts, heads, kv_heads, chunks, names, *refs):
    r = Named(zip(names, refs))
    rest = refs[len(names) :]
    me, part, z, y, core, dp_of, mp_of = place(depth, parts)
    work, work_out, residual = r.work, r.work_out, r.residual
    branch, branch_t, grad_t = r.branch, r.branch_t, r.grad_t
    in_x, give_x, low, held = r.in_x, r.give_x, r.low, r.held
    weights, out_w, normed_t, attended = (
        r.weights, r.out_w, r.normed_t, r.attended
    )
    rows, width = work.shape
    group = rows * parts
    members = heads // kv_heads
    q_width, kv_width = heads * HEAD_SIZE, kv_heads * HEAD_SIZE
    all_width = q_width + 2 * kv_width
    half = HEAD_SIZE // 2
    scale = HEAD_SIZE ** (-0.5)
    quarter = width // (4 * depth)
    inside = chunks > 0
    if inside:
        weights, out_w = r.wide.at[0], r.wide.at[1, :, pl.ds(0, q_width)]
        residual = r.others_two.at[0]

    mlp_widths, attn_widths = mlp_and_attn_widths(
        r, inside, chunks, r.attended_in.shape[1], all_width
    )
    count = len(mlp_widths)
    if inside:
        mlp_order = [(k, mask) for k in range(count) for mask in masks(depth)]
        ring = attn_ring = Ring(r.ring)
        attn_start = len(mlp_order) % len(ring.users)
        wholes = None
    else:
        mlp_order = [(k, mask) for mask in masks(depth) for k in range(count)]
        ring, attn_ring, attn_start = Ring(r.ring), Ring(r.attn_ring), 0
        wholes = [r["grad%d" % k] for k in range(count)]
    attn_order = [(k, mask) for mask in masks(depth) for k in range(2)]
    mlp_refs = (
        [r["mlp_held%d" % k] for k in range(count)]
        + [r["mlp_y%d" % k] for k in range(count)]
        + [r["mlp_z%d" % k] for k in range(count)]
        + list(rest[:11])
    )
    attn_refs = (
        [r["attn_held%d" % k] for k in range(2)]
        + [r["attn_y%d" % k] for k in range(2)]
        + [r["attn_z%d" % k] for k in range(2)]
        + list(rest[11:22])
    )
    mlp = Sums(depth, parts, mlp_order, mlp_widths, quarter, mlp_refs, wholes, ring, 0,
               [r["mlp_out%d" % k] for k in range(count)])
    attn = Sums(depth, parts, attn_order, attn_widths, quarter, attn_refs, None, attn_ring,
                attn_start, [r["attn_out%d" % k] for k in range(2)])
    total_gains = Gains(depth, parts, held, r.around, (r.g_sent, r.g_got))

    loading = [0]

    def load(source, target):
        copy = pltpu.make_async_copy(source, target, r.loaded.at[loading[0]])
        loading[0] += 1
        copy.start()
        return copy

    def wait(copies):
        for copy in copies:
            copy.wait()

    def along_x(source, target, name):
        sems = (r[name + "_sent"], r[name + "_got"])
        return [
            send(source(step), target(step), sems, step - 1, (me, mp_of(step)))
            for step in range(1, parts)
        ]

    give_two = give_x if inside else r.give_two
    give_out = r.give_out_low if inside else r.give_out
    to_two = along_x(lambda s: give_two.at[s - 1], lambda s: in_x.at[s - 1], "two")
    to_out = along_x(lambda s: give_out.at[s - 1], lambda s: r.in_out.at[s - 1], "out")
    to_branch = along_x(lambda s: branch.at[part], lambda s: branch.at[part], "branch")
    to_one = along_x(lambda s: give_x.at[s - 1], lambda s: in_x.at[s - 1], "one")

    if inside:
        hidden_width = mlp_widths[0] // 3
        gate_cols, up_cols, down_cols = (
            slice(i * hidden_width, (i + 1) * hidden_width) for i in range(3)
        )

        def load_chunk(k):
            lanes = pl.ds(k * 3 * hidden_width, 3 * hidden_width)
            return load(r.mlp_w_in.at[:, lanes], r.wide.at[k % 2])

        def load_part(i):
            lanes = pl.ds(i * hidden_width, hidden_width)
            return load(r.mlp_w_in.at[:, lanes], r.wide.at[0, :, lanes])

        first_loads = [load(r.normed_two_in, branch), load_part(0), load_part(1)]
        next_loads = [load(r.cot_in, r.cot), load_part(2)]
        block_loads = [load(r.normed_two_t_in, branch_t), load(r.cot_t_in, normed_t)]
        chunk_loads = [None]
        if chunks > 1:
            chunk_loads.append(load_chunk(1))
        greet(depth, parts)
        late_loads = [
            load(r.query_t_in, r.query_t), load(r.key_t_in, r.key_t),
            load(r.value_t_in, r.value_t), load(r.attended_in, attended),
            load(r.tokens_in, r.tokens),
        ]
        wait(first_loads)

        def add_to(own, others, k, product):
            for step in range(parts):
                target = own if step == 0 else others.at[step - 1]
                value = product(step)
                if k == 0:
                    target[...] = value
                else:
                    target[...] += value

        hidden, grad_gate, grad_up = r.hidden, r.grad_gate, r.grad_up

        def feed_forward(k):
            if k > 0:
                chunk_loads[k].wait()
            wide = r.wide.at[k % 2]
            here = slice(k * hidden_width, (k + 1) * hidden_width)
            for p in range(parts):
                lines = slice(p * rows, (p + 1) * rows)
                gate = jnp.dot(branch[p], wide[:, gate_cols], preferred_element_type=F32)
                up = jnp.dot(branch[p], wide[:, up_cols], preferred_element_type=F32)
                if k == 0 and p == 0:
                    wait(next_loads)
                back = jnp.dot(r.cot[p], wide[:, down_cols], preferred_element_type=F32)
                sigmoid = 1.0 / (1.0 + jnp.exp(-gate))
                swish = gate * sigmoid
                hidden[lines, here] = (swish * up).astype(BF16)
                grad_gate[lines, here] = (
                    back * up * sigmoid * (1.0 + gate * (1.0 - sigmoid))
                ).astype(BF16)
                grad_up[lines, here] = (back * swish).astype(BF16)

            def lines_of(step):
                return pl.ds(pl.multiple_of(mp_of(step) * rows, rows), rows)

            add_to(
                work, r.others_two, k,
                lambda step: dot_nt(grad_gate[lines_of(step), here], wide[:, gate_cols])
                + dot_nt(grad_up[lines_of(step), here], wide[:, up_cols]),
            )
            add_to(
                work_out, r.others_out, k,
                lambda step: dot_nt(hidden[lines_of(step), here], wide[:, down_cols]),
            )
            if k + 2 < chunks:
                chunk_loads.append(load_chunk(k + 2))

        def mlp_block(n):
            k = mlp_order[n][0]
            here = slice(k * hidden_width, (k + 1) * hidden_width)
            at = mlp.items[n][0]
            lines = pl.ds(pl.multiple_of(at * 4 * quarter, 32), 4 * quarter)
            slot = mlp.slot_for(n)
            for value, cols in (
                (jnp.dot(branch_t[lines, :], grad_gate[:, here], preferred_element_type=F32),
                 gate_cols),
                (jnp.dot(branch_t[lines, :], grad_up[:, here], preferred_element_type=F32),
                 up_cols),
                (jnp.dot(normed_t[lines, :], hidden[:, here], preferred_element_type=F32),
                 down_cols),
            ):
                for i in range(4):
                    slot[i // 2, i % 2, :, cols] = value[
                        i * quarter : (i + 1) * quarter
                    ].astype(BF16)
            mlp.items[n][3].start()

        made = [0]

        def make_blocks(stop):
            while made[0] < stop:
                mlp_block(made[0])
                made[0] += 1
                if made[0] >= 2:
                    mlp.cross()

        for k in range(chunks):
            feed_forward(k)
            if k == 0:
                wait(block_loads)
                make_blocks(depth)
                mlp.cross()
            else:
                mlp.onward()
        for step in range(1, parts):
            give_x[step - 1] = r.others_two[step - 1].astype(BF16)
            give_out[step - 1] = r.others_out[step - 1].astype(BF16)
        for copy in to_two:
            copy.start()
        residual_load = load(r.residual_in, residual)
        attn_loads = [load(r.weights_in, weights), load(r.out_w_in, out_w)]
        total_blocks = len(mlp_order)

        def more_blocks(stop):
            while made[0] < min(stop, total_blocks):
                mlp_block(made[0])
                made[0] += 1
                if made[0] - mlp.crossed == 2 or made[0] == total_blocks:
                    mlp.cross()
                if made[0] % 3 == 0:
                    mlp.onward()

        more_blocks(3 * depth)
        wait([residual_load])
        own_cot = r.cot.at[part]
    else:
        greet(depth, parts)
        for copy in to_two:
            copy.start()
        mlp.begin()
        first_loads = [
            load(r.own_two_in, work), load(r.residual_in, residual),
            load(r.cot_in, r.cot),
        ]
        late_loads = [
            load(r[name + "_in"], r[name])
            for name in ("out_w", "query_t", "key_t", "value_t", "weights", "normed_t",
                         "attended", "tokens")
        ] + [load(r.own_out_in, work_out)]
        attn_loads = []
        for n in range(min(8, len(mlp_order))):
            mlp.cross()
        wait(first_loads)
        own_cot = r.cot
    items = len(mlp_order)
    mlp.settle()
    for copy in to_two:
        copy.wait_recv()

    held[0:16] = jnp.zeros((16, width), F32)

    def second(here):
        total = work[here, :]
        for step in range(parts - 1):
            total = total + in_x[step, here, :].astype(F32)
        back, terms = norm_back(residual[here, :], r.gain_two[...], total)
        held[8:16] += fold(terms)
        result = own_cot[here, :].astype(F32) + back
        work[here, :] = result
        branch[part, here, :] = result.astype(BF16)

    tiles(rows, TILE, second)
    for copy in to_branch + to_out:
        copy.start()
    if inside:
        more_blocks(total_blocks)
        attn_loads.append(load(r.normed_t_in, normed_t))
    while mlp.crossed < items:
        mlp.cross()
    block = 256 if q_width % 256 == 0 else q_width

    def take_rows(step):
        p = mp_of(step)
        across = pl.ds(pl.multiple_of(p * rows, rows), rows)
        for first in range(0, q_width, block):
            piece = jnp.dot(
                branch[p], out_w[:, first : first + block], preferred_element_type=F32
            )
            grad_t[first : first + block, across] = piece.T.astype(BF16)

        def turn(i, carry):
            here = pl.ds(pl.multiple_of(i * 128, 128), 128)
            branch_t[here, across] = branch[p, :, here].astype(F32).T.astype(BF16)
            return carry

        lax.fori_loop(0, width // 128, turn, 0)

    wait(late_loads + attn_loads)
    mlp.onward()
    take_rows(0)
    mlp.onward()
    mlp.settle()
    for copy in to_branch:
        copy.wait()
    for step in range(1, parts):
        take_rows(step)

    q_block = 256 if group <= 1024 else 128
    key_acc, value_acc = r.key_acc, r.value_acc
    query_t, key_t, value_t, cosine, sine = (
        r.query_t, r.key_t, r.value_t, r.cosine, r.sine
    )

    def one_kv_head(j):
        kv_rows = slice(j * HEAD_SIZE, (j + 1) * HEAD_SIZE)
        key_acc[...] = jnp.zeros_like(key_acc)
        value_acc[...] = jnp.zeros_like(value_acc)
        for member in range(members):
            first = (j * members + member) * HEAD_SIZE
            head = slice(first, first + HEAD_SIZE)
            for start in range(0, group, q_block):
                stop = start + q_block
                cols = slice(start, stop)
                query, grad = query_t[head, cols], grad_t[head, cols]
                key, value = key_t[kv_rows, :stop], value_t[kv_rows, :stop]
                scores = lax.dot_general(
                    query, key, (((0,), (0,)), ((), ())), preferred_element_type=F32
                )
                seen = r.id_col[cols, :] == r.id_row[:, :stop]
                at_row = start + lax.broadcasted_iota(jnp.int32, (q_block, stop), 0)
                at_col = lax.broadcasted_iota(jnp.int32, (q_block, stop), 1)
                scores = jnp.where(seen & (at_col <= at_row), scores * scale, MASKED)
                grown = jnp.exp(scores - jnp.max(scores, axis=-1, keepdims=True))
                probs = grown * (1.0 / jnp.sum(grown, axis=-1, keepdims=True))
                dprob = lax.dot_general(
                    grad, value, (((0,), (0,)), ((), ())), preferred_element_type=F32
                )
                inner = jnp.sum(probs * dprob, axis=-1, keepdims=True)
                dscore = (probs * (dprob - inner)).astype(BF16)
                key_acc[:, :stop] += jnp.dot(query, dscore, preferred_element_type=F32)
                value_acc[:, :stop] += jnp.dot(
                    grad, probs.astype(BF16), preferred_element_type=F32
                )
                dquery = scale * dot_nt(key, dscore)
                lead, tail = dquery[:half], dquery[half:]
                cos, sin = cosine[:, cols], sine[:, cols]
                grad_t[first : first + half, cols] = (lead * cos + tail * sin).astype(BF16)
                grad_t[first + half : first + HEAD_SIZE, cols] = (
                    tail * cos - lead * sin
                ).astype(BF16)
        lead, tail = key_acc[:half] * scale, key_acc[half:] * scale
        cos, sin = cosine[...], sine[...]
        first = q_width + j * HEAD_SIZE
        grad_t[first : first + half, :] = (lead * cos + tail * sin).astype(BF16)
        grad_t[first + half : first + HEAD_SIZE, :] = (tail * cos - lead * sin).astype(BF16)
        first = q_width + kv_width + j * HEAD_SIZE
        grad_t[first : first + HEAD_SIZE, :] = value_acc[...].astype(BF16)

    if not inside:
        mlp.onward()
    for j in range(kv_heads):
        one_kv_head(j)
        if not inside or j % 4 != 2:
            mlp.onward()

    def turn_back(i, carry):
        here = pl.ds(pl.multiple_of(i * 128, 128), 128)
        piece = grad_t[here, :].astype(F32).T.astype(BF16)
        for p in range(parts):
            branch[p, :, here] = piece[p * rows : (p + 1) * rows]
        return carry

    lax.fori_loop(0, all_width // 128, turn_back, 0)
    for copy in to_two:
        copy.wait_send()

    def incoming(step, here):
        return dot_nt(branch[mp_of(step), :, :all_width], weights[here, :])

    for step in range(1, parts):
        for first in range(0, width, 512):
            give_x[step - 1, :, first : first + 512] = incoming(
                step, slice(first, first + 512)
            ).astype(BF16)
    for copy in to_one:
        copy.start()
    mlp.onward()

    def attn_block(n):
        k = attn_order[n][0]
        lines = pl.ds(pl.multiple_of(attn.items[n][0] * 4 * quarter, 32), 4 * quarter)
        slot = attn.slot_for(n)

        def put(value, first):
            for i in range(4):
                slot[i // 2, i % 2, :, first : first + value.shape[1]] = value[
                    i * quarter : (i + 1) * quarter
                ].astype(BF16)

        if k == 0:
            wide = 512 if all_width % 512 == 0 else all_width
            for first in range(0, all_width, wide):
                put(dot_nt(normed_t[lines, :], grad_t[first : first + wide, :]), first)
        else:
            put(jnp.dot(branch_t[lines, :], attended[...], preferred_element_type=F32), 0)
        attn.items[n][3].start()

    for n in range(len(attn_order)):
        attn_block(n)
        if n >= 1:
            attn.cross()
        if n % 2 == 1 and not (inside and n < 2):
            mlp.onward()
    attn.cross()

    for copy in to_out:
        copy.wait_recv()
    if inside:
        for copy in to_out:
            copy.wait_send()
    out_tile, stored = r.out_tile, r.stored
    tile = out_tile.shape[1]
    for first in range(0, rows, tile):
        fetch = pltpu.make_async_copy(r.in_out.at[:, pl.ds(first, tile)], out_tile, stored.at[0])
        fetch.start()
        fetch.wait()
        for line in range(first, first + tile, 16):
            here = slice(line, line + 16)
            total = work_out[here, :]
            for step in range(parts - 1):
                total = total + out_tile[step, line - first : line - first + 16, :].astype(F32)
            low[here, :] = (residual[here, :] + total).astype(BF16)
    put_out = pltpu.make_async_copy(low, r.block_out, stored.at[1])
    put_out.start()
    for first in range(0, width, 512):
        work_out[:, first : first + 512] = incoming(0, slice(first, first + 512))
    mlp.onward()
    mlp.settle()
    put_out.wait()

    for copy in to_one:
        copy.wait_recv()

    def first_norm(here):
        total = work_out[here, :]
        for step in range(parts - 1):
            total = total + in_x[step, here, :].astype(F32)
        back, terms = norm_back(r.tokens[here, :].astype(F32), r.gain_one[...], total)
        held[0:8] += fold(terms)
        low[here, :] = (work[here, :] + back).astype(BF16)

    tiles(rows, TILE, first_norm)
    put_tokens = pltpu.make_async_copy(low, r.grad_tokens, stored.at[2])
    put_tokens.start()
    total_gains.begin()
    while mlp.passed < items:
        mlp.onward()
        total_gains.advance()
    mlp.settle()
    while total_gains.number < 3:
        total_gains.advance()
    attn.onward()
    for k in range(count):
        mlp.finish(k)
        attn.onward()
    while attn.passed < len(attn_order):
        attn.onward()
    total_gains.advance()
    r.gains[...] = held[64:80]
    for k in range(2):
        attn.finish(k)
    put_tokens.wait()
    for copy in to_one + ([] if inside else to_out):
        copy.wait_send()
    mlp.drain()
    attn.drain()
    ring.drain()
    if attn_ring is not ring:
        attn_ring.drain()
    total_gains.drain()


def mlp_and_attn_widths(r, inside, chunks, out_width, all_width):
    if inside:
        widths = [r.mlp_w_in.shape[1] // chunks] * chunks
    else:
        widths = [r["grad%d" % k].shape[4] for k in range(3)]
    return widths, [all_width, out_width]


def backward(mlp_args, chunks, residual, cot, tokens, gain_one, gain_two, weights, out_w, normed_t,
             query_t, key_t, value_t, attended, ids, cosine, sine):
    depth, parts = lax.axis_size("dp") // 4, lax.axis_size("mp")
    rows, width = residual.shape
    group = rows * parts
    quarter = width // (4 * depth)
    heads, kv_heads = query_t.shape[0] // HEAD_SIZE, key_t.shape[0] // HEAD_SIZE
    inside = chunks > 0
    small = dict(
        gain_one=gain_one, gain_two=gain_two, id_col=ids[0], id_row=ids[1],
        cosine=cosine, sine=sine,
    )
    large = dict(
        residual_in=residual, cot_in=cot, tokens_in=tokens, weights_in=weights,
        out_w_in=out_w, normed_t_in=normed_t, query_t_in=query_t, key_t_in=key_t,
        value_t_in=value_t, attended_in=attended,
    )
    large.update(mlp_args)
    shapes = Named(large)
    mlp_widths, attn_widths = mlp_and_attn_widths(
        shapes, inside, chunks, attended.shape[1], weights.shape[1]
    )
    count = len(mlp_widths)
    struct = jax.ShapeDtypeStruct
    outs = {"mlp_out%d" % k: struct((quarter, w), F32) for k, w in enumerate(mlp_widths)}
    outs.update({"attn_out%d" % k: struct((quarter, w), F32) for k, w in enumerate(attn_widths)})
    rows_out = struct((rows, width), BF16)
    outs.update(
        block_out=rows_out, grad_tokens=rows_out, in_out=struct((parts - 1, rows, width), BF16)
    )
    for kind, widths in (("mlp", mlp_widths), ("attn", attn_widths)):
        landing = Sums.landing_shapes(depth, widths, quarter)
        for k in range(len(widths)):
            outs["%s_y%d" % (kind, k)] = landing[k]
            outs["%s_z%d" % (kind, k)] = landing[len(widths) + k]
    gains_out = dict(gains=struct((16, width), F32))

    def like(array):
        return pltpu.VMEM(array.shape, array.dtype)

    rows_f32, rows_low = pltpu.VMEM((rows, width), F32), pltpu.VMEM((rows, width), BF16)
    x_low = pltpu.VMEM((parts - 1, rows, width), BF16)
    stops = depth + parts
    scratch = dict(
        work=rows_f32, work_out=rows_f32, cot=like(cot), tokens=rows_low,
        normed_t=like(normed_t), query_t=like(query_t), key_t=like(key_t),
        value_t=like(value_t), attended=like(attended), in_x=x_low, give_x=x_low,
        out_tile=pltpu.VMEM((parts - 1, 64, width), BF16),
        branch=pltpu.VMEM((parts, rows, width), BF16),
        branch_t=pltpu.VMEM((width, group), BF16),
        grad_t=pltpu.VMEM((weights.shape[1], group), BF16),
        key_acc=pltpu.VMEM((HEAD_SIZE, group), F32),
        value_acc=pltpu.VMEM((HEAD_SIZE, group), F32),
        held=pltpu.VMEM((80, width), F32), around=pltpu.VMEM((16 * stops, width), F32),
        loaded=DMA((20 + chunks,)), stored=DMA((3,)), g_sent=DMA((stops,)), g_got=DMA((stops,)),
    )
    for name in ("two", "out", "branch", "one"):
        scratch[name + "_sent"] = scratch[name + "_got"] = DMA((parts - 1,))
    if inside:
        hidden = pltpu.VMEM((group, chunks * mlp_widths[0] // 3), BF16)
        others = pltpu.VMEM((parts - 1, rows, width), F32)
        scratch.update(
            wide=pltpu.VMEM((2, width, mlp_widths[0]), BF16),
            hidden=hidden, grad_gate=hidden, grad_up=hidden,
            others_two=others, others_out=others, give_out_low=x_low,
            ring=pltpu.VMEM((3, 2, 2, quarter, mlp_widths[0]), BF16),
        )
    else:
        scratch.update(
            residual=rows_f32, weights=like(weights), out_w=like(out_w),
            ring=pltpu.VMEM((6, 2, quarter, mlp_widths[0]), BF16),
            attn_ring=pltpu.VMEM((3, 2, 2, quarter, max(attn_widths)), BF16),
        )
    scratch.update(low=rows_low)
    for kind, widths in (("mlp", mlp_widths), ("attn", attn_widths)):
        for k, shape in enumerate(Sums.held_shapes(depth, widths, quarter)):
            scratch["%s_held%d" % (kind, k)] = shape
    names = list(large) + list(small) + list(outs) + list(gains_out) + list(scratch)
    kernel = functools.partial(
        backward_kernel, depth, parts, heads, kv_heads, chunks, names
    )
    results = pl.pallas_call(
        kernel,
        out_shape=list(outs.values()) + list(gains_out.values()),
        in_specs=[ANY_SPEC] * len(large) + [VMEM_SPEC] * len(small),
        out_specs=[ANY_SPEC] * len(outs) + [VMEM_SPEC],
        scratch_shapes=list(scratch.values())
        + Sums.tiles(depth, mlp_widths, quarter)
        + Sums.tiles(depth, attn_widths, quarter),
        compiler_params=pltpu.CompilerParams(
            collective_id=1, has_side_effects=True, vmem_limit_bytes=63 * 2**20
        ),
        name="backward",
    )(*large.values(), *small.values())
    return Named(zip(list(outs) + list(gains_out), results))


def own_and_give(whole, parts):
    me = lax.axis_index("mp")
    rows = whole.shape[0] // parts
    own = lax.dynamic_slice_in_dim(whole, me * rows, rows, 0)
    give = [
        lax.dynamic_slice_in_dim(whole, lax.rem(me + step, parts) * rows, rows, 0).astype(BF16)
        for step in range(1, parts)
    ]
    return own, jnp.stack(give)


def shards(
    tokens,
    seq_lengths,
    norm_attn,
    w_query,
    key_weight,
    value_weight,
    w_out,
    norm_mlp,
    w_gate,
    w_up,
    w_down,
    cotangent,
):
    parts = lax.axis_size("mp")
    rows = tokens.shape[0]
    group = rows * parts
    q_width, kv_width, hidden_width = w_query.shape[1], key_weight.shape[1], w_gate.shape[1]
    heads, kv_heads = q_width // HEAD_SIZE, kv_width // HEAD_SIZE
    members = heads // kv_heads
    factor = HEAD_SIZE ** (-0.5)

    width = tokens.shape[1]
    inputs = tokens.astype(F32)
    gain_one, gain_two = norm_attn.astype(F32), norm_mlp.astype(F32)
    chunks = hidden_width // 512 if group <= 512 and hidden_width % 512 == 0 else 0
    turned = w_down.T
    unit = hidden_width // max(chunks, 1)
    mlp_shard = jnp.concatenate(
        [
            part[:, k * unit : (k + 1) * unit]
            for k in range(max(chunks, 1))
            for part in (w_gate, w_up, turned)
        ],
        axis=1,
    )
    attn_w, out_wt, normed_one, grad_rows = gather_attn(
        (jnp.concatenate([w_query, key_weight, value_weight], axis=1), w_out.T),
        (rms_parts(inputs)[1] * gain_one).astype(BF16),
        cotangent,
    )
    mlp_shard, attn_w = lax.optimization_barrier((mlp_shard, attn_w))
    mlp_w = lax.all_gather(mlp_shard, "dp", axis=0, tiled=True)
    attn_w, out_wt = attn_w.reshape(width, -1), out_wt.reshape(width, -1)
    normed_one, grad_rows = normed_one.reshape(group, width), grad_rows.reshape(group, width)
    cuts = (q_width, q_width + kv_width)
    query_w, key_w, value_w = jnp.split(attn_w, cuts, axis=1)

    segment, position = layout(seq_lengths[0], group)
    cosine, sine = rotation(position)
    places = jnp.arange(group, dtype=jnp.int32)
    allowed = (
        (places[:, None] >= places[None, :])
        & (segment[:, None] == segment[None, :])
        & ((segment[None, :] >= 0) | (places[:, None] == places[None, :]))
    )

    query = rotate(mul(normed_one, query_w).reshape(group, heads, HEAD_SIZE), cosine, sine)
    key = rotate(mul(normed_one, key_w).reshape(group, kv_heads, HEAD_SIZE), cosine, sine)
    value = mul(normed_one, value_w).astype(BF16).reshape(group, kv_heads, HEAD_SIZE)
    query = query.astype(BF16).reshape(group, kv_heads, members, HEAD_SIZE)
    key = key.astype(BF16)
    scores = jnp.einsum("qhgd,khd->hgqk", query, key, preferred_element_type=F32) * factor
    scores = jnp.where(allowed[None, None], scores, MASKED)
    peak = jnp.max(scores, axis=-1, keepdims=True)
    grown = jnp.exp(scores - peak)
    probs = grown / jnp.sum(grown, axis=-1, keepdims=True)
    probs_low = probs.astype(BF16)
    attended = (
        jnp.einsum("hgqk,khd->qhgd", probs_low, value, preferred_element_type=F32)
        .astype(BF16)
        .reshape(group, q_width)
    )
    residual = inputs + mp_sum_rows(mul_t(attended, out_wt), parts)
    normed_two = mp_gather((rms_parts(residual)[1] * gain_two).astype(BF16), parts)

    if chunks:
        mlp_args = dict(
            mlp_w_in=mlp_w,
            normed_two_in=normed_two.reshape(parts, rows, width),
            normed_two_t_in=normed_two.T,
            cot_t_in=grad_rows.T,
        )
    else:
        gate_w, up_w, down_wt = jnp.split(mlp_w, 3, axis=1)
        gate_act, up_act = mul(normed_two, gate_w), mul(normed_two, up_w)
        sigmoid_g = jax.nn.sigmoid(gate_act)
        swish = gate_act * sigmoid_g
        hidden = (swish * up_act).astype(BF16)
        grad_hidden = mul(grad_rows, down_wt)
        grad_gate = (
            grad_hidden * up_act * sigmoid_g * (1.0 + gate_act * (1.0 - sigmoid_g))
        ).astype(BF16)
        grad_up = (grad_hidden * swish).astype(BF16)
        grads = (
            outer_sum(normed_two, grad_gate).astype(BF16),
            outer_sum(normed_two, grad_up).astype(BF16),
            outer_sum(grad_rows, hidden).astype(BF16),
        )
        depth = lax.axis_size("dp") // 4
        mlp_args = {
            "grad%d" % k: grad.reshape(depth, 2, 2, width // (4 * depth), -1)
            for k, grad in enumerate(grads)
        }
        own_two, give_two = own_and_give(
            mul_t(grad_gate, gate_w) + mul_t(grad_up, up_w), parts
        )
        own_out, give_out = own_and_give(mul_t(hidden, down_wt), parts)
        mlp_args.update(
            own_two_in=own_two, give_two=give_two, own_out_in=own_out, give_out=give_out
        )
    ids = jnp.where(segment >= 0, segment, 3 + places)
    done = backward(
        mlp_args,
        chunks,
        residual,
        grad_rows.reshape(parts, rows, width) if chunks else cotangent,
        tokens,
        gain_one[None, :],
        gain_two[None, :],
        attn_w,
        out_wt,
        normed_one.T,
        query.reshape(group, q_width).T,
        key.reshape(group, kv_width).T,
        value.reshape(group, kv_width).T,
        jnp.pad(attended, ((0, 0), (0, -q_width % 128))),
        (ids[:, None], ids[None, :]),
        cosine[:, 0, :].T,
        sine[:, 0, :].T,
    )
    block_out, grad_tokens = done.block_out, done.grad_tokens
    mlp_parts = [done["mlp_out%d" % k] for k in range(chunks or 3)]
    if chunks:
        mlp_parts = [
            jnp.concatenate(part, axis=1)
            for part in zip(*(jnp.split(piece, 3, axis=1) for piece in mlp_parts))
        ]
    grad_gate_w, grad_up_w, grad_down_w = mlp_parts
    attn_parts = jnp.split(done.attn_out0, cuts, axis=1) + [done.attn_out1[:, :q_width]]
    gains = jnp.sum(done.gains.reshape(2, 8, width), axis=1)
    return (
        block_out,
        grad_tokens,
        gains[0],
        attn_parts[0],
        attn_parts[1],
        attn_parts[2],
        attn_parts[3].T,
        gains[1],
        grad_gate_w,
        grad_up_w,
        grad_down_w.T,
    )


def solution(mesh):
    rows, whole = P(("dp", "mp"), None), P()
    split, turned = P("dp", "mp"), P("mp", "dp")
    return jax.shard_map(
        shards,
        mesh=mesh,
        in_specs=(
            rows, P("dp", None), whole, split, split, split, turned, whole, split, split, turned, rows,
        ),
        out_specs=(
            rows, rows, whole, split, split, split, turned, whole, split, split, turned,
        ),
        check_vma=False,
    )
```

```python
import functools

import jax
import jax.numpy as jnp
from jax import lax
from jax.experimental import pallas as pl
from jax.experimental.pallas import tpu as pltpu
from jax.sharding import PartitionSpec as P

HEAD_SIZE = 96
EPSILON = 1e-05
ROPE_BASE = 100000.0
MASKED = -1e30
F32 = jnp.float32
BF16 = jnp.bfloat16


def layout(lengths, rows_total):
    places = jnp.arange(rows_total, dtype=jnp.int32)
    first_end = lengths[0]
    middle_end = lengths[0] + lengths[1]
    last_end = middle_end + lengths[2]
    segment = jnp.where(
        places < first_end,
        0,
        jnp.where(places < middle_end, 1, jnp.where(places < last_end, 2, -1)),
    ).astype(jnp.int32)
    offset = jnp.where(places < first_end, 0, jnp.where(places < middle_end, first_end, middle_end))
    position = jnp.where(segment >= 0, places - offset, 0)
    return segment, position


def rotation(position):
    half_dim = HEAD_SIZE // 2
    inverse = ROPE_BASE ** (-jnp.arange(half_dim, dtype=F32) * 2.0 / HEAD_SIZE)
    angles = position.astype(F32)[:, None] * inverse[None, :]
    return jnp.cos(angles)[:, None, :], jnp.sin(angles)[:, None, :]


def rotate(tensor, cosine, sine):
    half_dim = tensor.shape[-1] // 2
    lead, tail = tensor[..., :half_dim], tensor[..., half_dim:]
    return jnp.concatenate([lead * cosine - tail * sine, tail * cosine + lead * sine], axis=-1)


def rms_parts(inputs):
    factor = lax.rsqrt(jnp.mean(inputs * inputs, axis=-1, keepdims=True) + EPSILON)
    return factor, inputs * factor


def mul(left, right):
    return jnp.dot(left, right, preferred_element_type=F32)


def mul_t(left, right):
    return lax.dot_general(left, right, (((1,), (1,)), ((), ())), preferred_element_type=F32)


def outer_sum(left, right):
    return lax.dot_general(left, right, (((0,), (0,)), ((), ())), preferred_element_type=F32)


def mp_shift(block, step, parts):
    return lax.ppermute(block, "mp", [(i, (i + step) % parts) for i in range(parts)])


def mp_gather(block, parts):
    me = lax.axis_index("mp")
    rows = block.shape[0]
    whole = jnp.zeros((parts * rows,) + block.shape[1:], block.dtype)
    for step in range(parts):
        piece = block if step == 0 else mp_shift(block, step, parts)
        owner = lax.rem(me - step + parts, parts)
        whole = lax.dynamic_update_slice_in_dim(whole, piece, owner * rows, 0)
    return whole


def mp_sum_rows(whole, parts):
    me = lax.axis_index("mp")
    rows = whole.shape[0] // parts
    total = lax.dynamic_slice_in_dim(whole, me * rows, rows, 0)
    for step in range(1, parts):
        owner = lax.rem(me + step, parts)
        piece = lax.dynamic_slice_in_dim(whole, owner * rows, rows, 0).astype(BF16)
        total = total + mp_shift(piece, step, parts).astype(F32)
    return total


MESH = pl.DeviceIdType.MESH
VMEM_SPEC = pl.BlockSpec(memory_space=pltpu.VMEM)
ANY_SPEC = pl.BlockSpec(memory_space=pl.ANY)
DMA = pltpu.SemaphoreType.DMA


def place(depth, parts):
    me, part = lax.axis_index("dp"), lax.axis_index("mp")
    z, y, core = me // 4, lax.rem(me // 2, 2), lax.rem(me, 2)

    def dp_of(step, at_y, at_core):
        return lax.rem(z + step, depth) * 4 + at_y * 2 + at_core

    def mp_of(step):
        return lax.rem(part + step, parts)

    return me, part, z, y, core, dp_of, mp_of


def flipped(value, mask):
    result = value
    for bit in (1 << i for i in range(mask.bit_length())):
        if mask & bit:
            result = result + bit * (1 - 2 * lax.rem(value // bit, 2))
    return result


def lowest(mask):
    return mask & -mask


def masks(depth):
    return sorted(range(1, depth), key=lambda m: (lowest(m), -m)) + [0]


def greet(depth, parts):
    me, part, z, y, core, dp_of, mp_of = place(depth, parts)
    near = [(dp_of(0, y, 1 - core), part), (dp_of(0, 1 - y, core), part)]
    near += [(dp_of(step, y, core), part) for step in range(1, depth)]
    near += [(me, mp_of(step)) for step in range(1, parts)]
    barrier = pltpu.get_barrier_semaphore()
    for device in near:
        pl.semaphore_signal(barrier, inc=1, device_id=device, device_id_type=MESH)
    pl.semaphore_wait(barrier, len(near))


def send(source, target, sems, at, device):
    sent, landed = sems
    return pltpu.make_async_remote_copy(
        src_ref=source,
        dst_ref=target,
        send_sem=sent.at[at],
        recv_sem=landed.at[at],
        device_id=device,
        device_id_type=MESH,
    )


class Gather:
    def __init__(self, depth, parts, shards, wholes, sems):
        self.depth, self.shards, self.wholes = depth, shards, wholes
        self.where = place(depth, parts)
        self.kept, self.z_sems, self.y_sems, self.c_sems = (
            sems[0], sems[1:3], sems[3:5], sems[5:7]
        )
        self.slots = 2 * depth - 1

    @staticmethod
    def semaphores(depth, count):
        slots = count * (2 * depth - 1)
        return [DMA((count,))] + [DMA((slots,))] * 4 + [DMA((2 * slots,))] * 2

    def block(self, i, move, at_y):
        me, part, z, y, core, dp_of, mp_of = self.where
        return self.wholes[i].at[(z + move) * 4 + at_y * 2 + core]

    def slot(self, move):
        return -move if move <= 0 else self.depth - 1 + move

    def source(self, i, move):
        return self.shards[i] if move == 0 else self.block(i, move, self.where[3])

    def along_z(self, i, move, ahead):
        me, part, z, y, core, dp_of, mp_of = self.where
        at = i * self.slots + self.slot(move - ahead)
        device = ((z + ahead) * 4 + y * 2 + core, part)
        return send(self.source(i, move), self.block(i, move, y), self.z_sems, at, device)

    def arrival(self, i, move):
        me, part, z, y, core, dp_of, mp_of = self.where
        at = i * self.slots + self.slot(move)
        block = self.block(i, move, y)
        return send(block, block, self.z_sems, at, (me, part))

    def along_y(self, i, move):
        me, part, z, y, core, dp_of, mp_of = self.where
        at = i * self.slots + self.slot(move)
        return send(self.source(i, move), self.block(i, move, y), self.y_sems, at,
                    (dp_of(0, 1 - y, core), part))

    def across(self, i, move, other):
        me, part, z, y, core, dp_of, mp_of = self.where
        at = 2 * (i * self.slots + self.slot(move)) + other
        at_y = 1 - y if other else y
        source = self.block(i, move, at_y) if other else self.source(i, move)
        return send(source, self.block(i, move, at_y), self.c_sems, at,
                    (dp_of(0, y, 1 - core), part))

    def there(self, move, action):
        z = self.where[2]
        if move == 0:
            action()
        else:
            pl.when((z + move >= 0) & (z + move < self.depth))(action)

    def begin(self, i):
        self.keep(i).start()
        for ahead in (1, -1):
            self.there(ahead, lambda ahead=ahead: self.along_z(i, 0, ahead).start())
        self.along_y(i, 0).start()
        self.across(i, 0, 0).start()

    def keep(self, i):
        return pltpu.make_async_copy(self.shards[i], self.wholes[i].at[self.where[0]],
                                     self.kept.at[i])

    def moves(self, step):
        return (0,) if step == 0 else (-step, step)

    def from_z(self, i, step):
        for move in self.moves(step):
            ahead = 1 if move < 0 else -1

            def pass_on(move=move, ahead=ahead):
                self.arrival(i, move).wait_recv()
                self.there(ahead, lambda: self.along_z(i, move, ahead).start())
                self.along_y(i, move).start()
                self.across(i, move, 0).start()

            self.there(move, pass_on)

    def from_y(self, i, step):
        for move in self.moves(step):

            def pass_on(move=move):
                self.along_y(i, move).wait_recv()
                self.across(i, move, 1).start()

            self.there(move, pass_on)

    def end(self, i):
        self.keep(i).wait()
        for step in range(self.depth):
            for move in self.moves(step):

                def settle(move=move):
                    self.across(i, move, 0).wait_recv()
                    self.across(i, move, 1).wait_recv()

                self.there(move, settle)

    def drain(self, i):
        for step in range(self.depth):
            for move in self.moves(step):

                def settle(move=move):
                    self.across(i, move, 0).wait_send()
                    self.across(i, move, 1).wait_send()
                    self.along_y(i, move).wait_send()
                    for ahead in (1, -1):
                        if move * ahead <= 0:
                            self.there(
                                ahead, lambda ahead=ahead: self.along_z(i, move, ahead).wait_send()
                            )

                self.there(move, settle)


def gather_kernel(depth, parts, count, *refs):
    shards, normed, cot = refs[:count], refs[count], refs[count + 1]
    weights = refs[count + 2 : 2 * count + 2]
    normed_all, cot_all, x_sent, x_got, kept = refs[2 * count + 2 : 2 * count + 7]
    me, part, z, y, core, dp_of, mp_of = place(depth, parts)
    work = Gather(depth, parts, shards, weights, refs[2 * count + 7 :])
    own = [
        pltpu.make_async_copy(normed, normed_all.at[part], kept.at[0]),
        pltpu.make_async_copy(cot, cot_all.at[part], kept.at[1]),
    ]
    greet(depth, parts)
    along_x = [
        send(source, target.at[part], (x_sent, x_got), i * (parts - 1) + step - 1,
             (me, mp_of(step)))
        for i, (source, target) in enumerate(((normed, normed_all), (cot, cot_all)))
        for step in range(1, parts)
    ]
    for i in range(count):
        work.begin(i)
    for copy in along_x + own:
        copy.start()
    for step in range(1, depth):
        for i in range(count):
            work.from_z(i, step)
        for i in range(count):
            work.from_y(i, step - 1)
    for i in range(count):
        work.from_y(i, depth - 1)
    for copy in along_x + own:
        copy.wait()
    for i in range(count):
        work.end(i)
    for i in range(count):
        work.drain(i)


def gather_attn(shards, normed, cot):
    depth, parts, count = lax.axis_size("dp") // 4, lax.axis_size("mp"), len(shards)
    size = depth * 4
    return pl.pallas_call(
        functools.partial(gather_kernel, depth, parts, count),
        out_shape=[jax.ShapeDtypeStruct((size,) + shard.shape, shard.dtype) for shard in shards]
        + [jax.ShapeDtypeStruct((parts,) + rows.shape, rows.dtype) for rows in (normed, cot)],
        in_specs=[VMEM_SPEC] * (count + 2),
        out_specs=[ANY_SPEC] * (count + 2),
        scratch_shapes=[DMA((2 * (parts - 1),))] * 2 + [DMA((2,))]
        + Gather.semaphores(depth, count),
        compiler_params=pltpu.CompilerParams(collective_id=0, has_side_effects=True),
        name="gather_attn",
    )(*shards, normed, cot)


def add_rows(target, sources):
    def body(i, carry):
        here = pl.ds(pl.multiple_of(i * 16, 16), 16)
        total = sources[0][here, :].astype(F32)
        for source in sources[1:]:
            total = total + source[here, :].astype(F32)
        target[here, :] = total.astype(target.dtype)
        return carry

    lax.fori_loop(0, target.shape[0] // 16, body, 0)


class Ring:
    def __init__(self, buffer):
        self.buffer, self.users, self.next = buffer, [None] * buffer.shape[0], 0

    def take(self, copy):
        slot = self.next
        if self.users[slot] is not None:
            self.users[slot].wait_send()
        self.users[slot] = copy
        self.next = (slot + 1) % len(self.users)

    def peek(self, ahead):
        return (self.next + ahead) % len(self.users)

    def drain(self):
        for copy in self.users:
            if copy is not None:
                copy.wait_send()


class Sums:
    def __init__(self, depth, parts, order, widths, rows, refs, wholes, ring, start, outs):
        self.depth, self.wholes, self.outs, self.order = depth, wholes, outs, order
        self.rows, self.widths, self.ring = rows, widths, ring
        count = len(widths)
        self.held = refs[:count]
        self.y_in, self.z_in = refs[count : 2 * count], refs[2 * count : 3 * count]
        self.y_tile, self.z_tile, self.stage = refs[3 * count : 3 * count + 3]
        self.sems = refs[3 * count + 3 :]
        self.where = place(depth, parts)
        slots = len(ring.users)
        self.slots = [(start + n) % slots for n in range(len(order))]
        self.items = [self.item(n) for n in range(len(order))]
        self.crossed = self.passed = 0
        self.pending = self.putting = None

    @staticmethod
    def held_shapes(depth, widths, rows):
        return [pltpu.VMEM((depth, 2, rows, width), BF16) for width in widths]

    @staticmethod
    def landing_shapes(depth, widths, rows):
        return [jax.ShapeDtypeStruct((depth, rows, width), BF16) for width in widths] + [
            jax.ShapeDtypeStruct((depth - 1, rows, width), BF16) for width in widths
        ]

    @staticmethod
    def tiles(depth, widths, rows):
        wide = max(widths)
        return [
            pltpu.VMEM((rows, wide), BF16),
            pltpu.VMEM((depth - 1, rows, wide), BF16),
            pltpu.VMEM((rows, wide), F32),
        ] + [DMA((depth * len(widths),))] * 7 + [DMA((depth + 2,))]

    def item(self, n):
        k, mask = self.order[n]
        me, part, z, y, core, dp_of, mp_of = self.where
        at = flipped(z, mask)
        kept, c_sent, c_got, y_sent, y_got, z_sent, z_got, moved = self.sems
        held, width = self.held[k], self.widths[k]
        every, slot = pl.ds(0, width), self.slots[n]
        own = None
        if self.wholes is None:
            give = self.ring.buffer.at[slot, :, 1 - core, :, every]
        else:
            give = self.wholes[k].at[at, :, 1 - core]
            own = pltpu.make_async_copy(
                self.wholes[k].at[at, :, core], self.ring.buffer.at[slot], kept.at[n]
            )
        across = send(give, held.at[at], (c_sent, c_got), n, (dp_of(0, y, 1 - core), part))
        along_y = send(
            held.at[at, 1 - y], self.y_in[k].at[at], (y_sent, y_got), n,
            (dp_of(0, 1 - y, core), part),
        )
        along_z = None
        if mask > 0:
            along_z = send(
                held.at[at, y], self.z_in[k].at[mask - 1], (z_sent, z_got), n,
                (flipped(z, lowest(mask)) * 4 + y * 2 + core, part),
            )
        return at, k, own, across, along_y, along_z

    def load(self, n):
        at, k, own, across, along_y, along_z = self.items[n]
        self.ring.take(across)
        own.start()
        across.start()

    def begin(self):
        self.ahead = min(len(self.ring.users), len(self.items))
        for n in range(self.ahead):
            self.load(n)

    def slot_for(self, n):
        self.ring.take(self.items[n][3])
        return self.ring.buffer.at[self.slots[n]]

    def cross(self):
        core = self.where[4]
        n = self.crossed
        self.crossed += 1
        at, k, own, across, along_y, along_z = self.items[n]
        if own is not None:
            own.wait()
        across.wait_recv()
        for at_y in range(2):
            if own is not None:
                mine = self.ring.buffer.at[self.slots[n], at_y]
            else:
                mine = self.ring.buffer.at[self.slots[n], at_y, core, :, pl.ds(0, self.widths[k])]
            held = self.held[k].at[at, at_y]
            add_rows(held, (mine, held))
        along_y.start()
        if own is not None and n + self.ahead < len(self.items):
            self.load(n + self.ahead)

    def onward(self):
        self.settle()
        n = self.passed
        if n >= self.crossed:
            return
        self.passed += 1
        moved = self.sems[7]
        at, k, own, across, along_y, along_z = self.items[n]
        mask, every = self.order[n][1], pl.ds(0, self.widths[k])
        along_y.wait_recv()
        tile = self.y_tile.at[:, every]
        fetches = [pltpu.make_async_copy(self.y_in[k].at[at], tile, moved.at[0])]
        fetches[0].start()
        tiles_in = [tile]
        if mask > 0:
            more, from_z = self.from_z(k, mask)
            fetches += more
            tiles_in += from_z
        self.pending = n, fetches, tiles_in

    def settle(self):
        if self.pending is None:
            return
        n, fetches, landed = self.pending
        self.pending = None
        at, k, own, across, along_y, along_z = self.items[n]
        for fetch in fetches:
            fetch.wait()
        held = self.held[k].at[at, self.where[3]]
        add_rows(held, [held] + landed)
        if along_z is not None:
            along_z.start()

    def from_z(self, k, mask):
        moved, every = self.sems[7], pl.ds(0, self.widths[k])
        fetches, landed = [], []
        bit = 1
        while bit < (lowest(mask) if mask else self.depth):
            sender = mask ^ bit
            self.items[self.order.index((k, sender))][5].wait_recv()
            tile = self.z_tile.at[len(landed), :, every]
            fetch = pltpu.make_async_copy(
                self.z_in[k].at[sender - 1], tile, moved.at[1 + len(landed)]
            )
            fetch.start()
            fetches.append(fetch)
            landed.append(tile)
            bit *= 2
        return fetches, landed

    def finish(self, k):
        self.settle()
        z, y = self.where[2:4]
        moved, every = self.sems[7], pl.ds(0, self.widths[k])
        fetches, landed = self.from_z(k, 0)
        for fetch in fetches:
            fetch.wait()
        stage = self.stage.at[:, every]
        if self.putting is not None:
            self.putting.wait()
        add_rows(stage, [self.held[k].at[z, y]] + landed)
        self.putting = pltpu.make_async_copy(stage, self.outs[k], moved.at[self.depth + 1])
        self.putting.start()

    def drain(self):
        self.putting.wait()
        for at, k, own, across, along_y, along_z in self.items:
            along_y.wait_send()
            if along_z is not None:
                along_z.wait_send()


class Gains:
    def __init__(self, depth, parts, held, around, sems):
        me, part, z, y, core, dp_of, mp_of = place(depth, parts)
        self.held = held
        stages = [
            [(dp_of(0, y, 1 - core), part)],
            [(me, mp_of(step)) for step in range(1, parts)],
            [(dp_of(step, y, core), part) for step in range(1, depth)],
            [(dp_of(0, 1 - y, core), part)],
        ]
        self.levels, slot = [], 0
        for number, stage in enumerate(stages):
            copies = []
            for device in stage:
                landing = around.at[pl.ds(16 * slot, 16)]
                source = held.at[pl.ds(16 * number, 16)]
                copies.append((send(source, landing, sems, slot, device), landing))
                slot += 1
            self.levels.append(copies)
        self.number = 0

    def begin(self):
        for copy, landing in self.levels[self.number]:
            copy.start()

    def advance(self):
        number = self.number
        if number == len(self.levels):
            return
        total = self.held[16 * number : 16 * number + 16]
        for copy, landing in self.levels[number]:
            copy.wait_recv()
            total = total + landing[...]
        self.held[16 * (number + 1) : 16 * (number + 2)] = total
        self.number += 1
        if self.number < len(self.levels):
            self.begin()

    def drain(self):
        for level in self.levels:
            for copy, landing in level:
                copy.wait_send()


def norm_back(rows_in, gain, gradient):
    factor = lax.rsqrt(jnp.mean(rows_in * rows_in, axis=-1, keepdims=True) + EPSILON)
    normed = rows_in * factor
    scaled = gradient * gain
    back = factor * (scaled - normed * jnp.mean(scaled * normed, axis=-1, keepdims=True))
    return back, gradient * normed


TILE = 16


def fold(terms):
    total = terms[0:8]
    for at in range(8, terms.shape[0], 8):
        total = total + terms[at : at + 8]
    return total


def tiles(rows, tile, body):
    def run(i, carry):
        body(pl.ds(pl.multiple_of(i * tile, tile), tile))
        return carry

    lax.fori_loop(0, rows // tile, run, 0, unroll=4)


def dot_nt(left, right):
    return lax.dot_general(
        left, right, (((1,), (1,)), ((), ())), preferred_element_type=F32
    )


class Named(dict):
    __getattr__ = dict.get


def backward_kernel(depth, parts, heads, kv_heads, chunks, names, *refs):
    r = Named(zip(names, refs))
    rest = refs[len(names) :]
    me, part, z, y, core, dp_of, mp_of = place(depth, parts)
    work, work_out, residual = r.work, r.work_out, r.residual
    branch, branch_t, grad_t = r.branch, r.branch_t, r.grad_t
    in_x, give_x, low, held = r.in_x, r.give_x, r.low, r.held
    weights, out_w, normed_t, attended = (
        r.weights, r.out_w, r.normed_t, r.attended
    )
    rows, width = work.shape
    group = rows * parts
    members = heads // kv_heads
    q_width, kv_width = heads * HEAD_SIZE, kv_heads * HEAD_SIZE
    all_width = q_width + 2 * kv_width
    half = HEAD_SIZE // 2
    scale = HEAD_SIZE ** (-0.5)
    quarter = width // (4 * depth)
    inside = chunks > 0
    if inside:
        weights, out_w = r.wide.at[0], r.wide.at[1, :, pl.ds(0, q_width)]
        residual = r.others_two.at[0]

    mlp_widths, attn_widths = mlp_and_attn_widths(
        r, inside, chunks, r.attended_in.shape[1], all_width
    )
    count = len(mlp_widths)
    if inside:
        mlp_order = [(k, mask) for k in range(count) for mask in masks(depth)]
        ring = attn_ring = Ring(r.ring)
        attn_start = len(mlp_order) % len(ring.users)
        wholes = None
    else:
        mlp_order = [(k, mask) for mask in masks(depth) for k in range(count)]
        ring, attn_ring, attn_start = Ring(r.ring), Ring(r.attn_ring), 0
        wholes = [r["grad%d" % k] for k in range(count)]
    attn_order = [(k, mask) for mask in masks(depth) for k in range(2)]
    mlp_refs = (
        [r["mlp_held%d" % k] for k in range(count)]
        + [r["mlp_y%d" % k] for k in range(count)]
        + [r["mlp_z%d" % k] for k in range(count)]
        + list(rest[:11])
    )
    attn_refs = (
        [r["attn_held%d" % k] for k in range(2)]
        + [r["attn_y%d" % k] for k in range(2)]
        + [r["attn_z%d" % k] for k in range(2)]
        + list(rest[11:22])
    )
    mlp = Sums(depth, parts, mlp_order, mlp_widths, quarter, mlp_refs, wholes, ring, 0,
               [r["mlp_out%d" % k] for k in range(count)])
    attn = Sums(depth, parts, attn_order, attn_widths, quarter, attn_refs, None, attn_ring,
                attn_start, [r["attn_out%d" % k] for k in range(2)])
    total_gains = Gains(depth, parts, held, r.around, (r.g_sent, r.g_got))

    loading = [0]

    def load(source, target):
        copy = pltpu.make_async_copy(source, target, r.loaded.at[loading[0]])
        loading[0] += 1
        copy.start()
        return copy

    def wait(copies):
        for copy in copies:
            copy.wait()

    def along_x(source, target, name):
        sems = (r[name + "_sent"], r[name + "_got"])
        return [
            send(source(step), target(step), sems, step - 1, (me, mp_of(step)))
            for step in range(1, parts)
        ]

    give_two = give_x if inside else r.give_two
    give_out = r.give_out_low if inside else r.give_out
    to_two = along_x(lambda s: give_two.at[s - 1], lambda s: in_x.at[s - 1], "two")
    to_out = along_x(lambda s: give_out.at[s - 1], lambda s: r.in_out.at[s - 1], "out")
    to_branch = along_x(lambda s: branch.at[part], lambda s: branch.at[part], "branch")
    to_one = along_x(lambda s: give_x.at[s - 1], lambda s: in_x.at[s - 1], "one")

    if inside:
        hidden_width = mlp_widths[0] // 3
        gate_cols, up_cols, down_cols = (
            slice(i * hidden_width, (i + 1) * hidden_width) for i in range(3)
        )

        def load_chunk(k):
            lanes = pl.ds(k * 3 * hidden_width, 3 * hidden_width)
            return load(r.mlp_w_in.at[:, lanes], r.wide.at[k % 2])

        def load_part(i):
            lanes = pl.ds(i * hidden_width, hidden_width)
            return load(r.mlp_w_in.at[:, lanes], r.wide.at[0, :, lanes])

        first_loads = [load(r.normed_two_in, branch), load_part(0), load_part(1)]
        next_loads = [load(r.cot_in, r.cot), load_part(2)]
        block_loads = [load(r.normed_two_t_in, branch_t), load(r.cot_t_in, normed_t)]
        chunk_loads = [None]
        if chunks > 1:
            chunk_loads.append(load_chunk(1))
        greet(depth, parts)
        late_loads = [
            load(r.query_t_in, r.query_t), load(r.key_t_in, r.key_t),
            load(r.value_t_in, r.value_t), load(r.attended_in, attended),
            load(r.tokens_in, r.tokens),
        ]
        wait(first_loads)

        def add_to(own, others, k, product):
            for step in range(parts):
                target = own if step == 0 else others.at[step - 1]
                value = product(step)
                if k == 0:
                    target[...] = value
                else:
                    target[...] += value

        hidden, grad_gate, grad_up = r.hidden, r.grad_gate, r.grad_up

        def feed_forward(k):
            if k > 0:
                chunk_loads[k].wait()
            wide = r.wide.at[k % 2]
            here = slice(k * hidden_width, (k + 1) * hidden_width)
            for p in range(parts):
                lines = slice(p * rows, (p + 1) * rows)
                gate = jnp.dot(branch[p], wide[:, gate_cols], preferred_element_type=F32)
                up = jnp.dot(branch[p], wide[:, up_cols], preferred_element_type=F32)
                if k == 0 and p == 0:
                    wait(next_loads)
                back = jnp.dot(r.cot[p], wide[:, down_cols], preferred_element_type=F32)
                sigmoid = 1.0 / (1.0 + jnp.exp(-gate))
                swish = gate * sigmoid
                hidden[lines, here] = (swish * up).astype(BF16)
                grad_gate[lines, here] = (
                    back * up * sigmoid * (1.0 + gate * (1.0 - sigmoid))
                ).astype(BF16)
                grad_up[lines, here] = (back * swish).astype(BF16)

            if k == 0:
                wait(block_loads)
                make_blocks(depth)
                mlp.cross()

            def lines_of(step):
                return pl.ds(pl.multiple_of(mp_of(step) * rows, rows), rows)

            add_to(
                work, r.others_two, k,
                lambda step: dot_nt(grad_gate[lines_of(step), here], wide[:, gate_cols])
                + dot_nt(grad_up[lines_of(step), here], wide[:, up_cols]),
            )
            add_to(
                work_out, r.others_out, k,
                lambda step: dot_nt(hidden[lines_of(step), here], wide[:, down_cols]),
            )
            if k + 2 < chunks:
                chunk_loads.append(load_chunk(k + 2))

        def mlp_block(n):
            k = mlp_order[n][0]
            here = slice(k * hidden_width, (k + 1) * hidden_width)
            at = mlp.items[n][0]
            lines = pl.ds(pl.multiple_of(at * 4 * quarter, 32), 4 * quarter)
            slot = mlp.slot_for(n)
            for value, cols in (
                (jnp.dot(branch_t[lines, :], grad_gate[:, here], preferred_element_type=F32),
                 gate_cols),
                (jnp.dot(branch_t[lines, :], grad_up[:, here], preferred_element_type=F32),
                 up_cols),
                (jnp.dot(normed_t[lines, :], hidden[:, here], preferred_element_type=F32),
                 down_cols),
            ):
                for i in range(4):
                    slot[i // 2, i % 2, :, cols] = value[
                        i * quarter : (i + 1) * quarter
                    ].astype(BF16)
            mlp.items[n][3].start()

        made = [0]

        def make_blocks(stop):
            while made[0] < stop:
                mlp_block(made[0])
                made[0] += 1
                if made[0] >= 2:
                    mlp.cross()

        for k in range(chunks):
            feed_forward(k)
            if k > 0:
                mlp.onward()
        for step in range(1, parts):
            give_x[step - 1] = r.others_two[step - 1].astype(BF16)
            give_out[step - 1] = r.others_out[step - 1].astype(BF16)
        for copy in to_two:
            copy.start()
        residual_load = load(r.residual_in, residual)
        attn_loads = [load(r.weights_in, weights), load(r.out_w_in, out_w)]
        total_blocks = len(mlp_order)

        def more_blocks(stop):
            while made[0] < min(stop, total_blocks):
                mlp_block(made[0])
                made[0] += 1
                if made[0] - mlp.crossed == 2 or made[0] == total_blocks:
                    mlp.cross()
                if made[0] % 3 == 0:
                    mlp.onward()

        more_blocks(3 * depth)
        wait([residual_load])
        own_cot = r.cot.at[part]
    else:
        greet(depth, parts)
        for copy in to_two:
            copy.start()
        mlp.begin()
        first_loads = [
            load(r.own_two_in, work), load(r.residual_in, residual),
            load(r.cot_in, r.cot),
        ]
        late_loads = [
            load(r[name + "_in"], r[name])
            for name in ("out_w", "query_t", "key_t", "value_t", "weights", "normed_t",
                         "attended", "tokens")
        ] + [load(r.own_out_in, work_out)]
        attn_loads = []
        for n in range(min(8, len(mlp_order))):
            mlp.cross()
        wait(first_loads)
        own_cot = r.cot
    items = len(mlp_order)
    mlp.settle()
    for copy in to_two:
        copy.wait_recv()

    held[0:16] = jnp.zeros((16, width), F32)

    def second(here):
        total = work[here, :]
        for step in range(parts - 1):
            total = total + in_x[step, here, :].astype(F32)
        back, terms = norm_back(residual[here, :], r.gain_two[...], total)
        held[8:16] += fold(terms)
        result = own_cot[here, :].astype(F32) + back
        work[here, :] = result
        branch[part, here, :] = result.astype(BF16)

    tiles(rows, TILE, second)
    for copy in to_branch + to_out:
        copy.start()
    if inside:
        more_blocks(total_blocks)
        attn_loads.append(load(r.normed_t_in, normed_t))
    while mlp.crossed < items:
        mlp.cross()
    block = 256 if q_width % 256 == 0 else q_width

    def take_rows(step):
        p = mp_of(step)
        across = pl.ds(pl.multiple_of(p * rows, rows), rows)
        for first in range(0, q_width, block):
            piece = jnp.dot(
                branch[p], out_w[:, first : first + block], preferred_element_type=F32
            )
            grad_t[first : first + block, across] = piece.T.astype(BF16)

        def turn(i, carry):
            here = pl.ds(pl.multiple_of(i * 128, 128), 128)
            branch_t[here, across] = branch[p, :, here].astype(F32).T.astype(BF16)
            return carry

        lax.fori_loop(0, width // 128, turn, 0)

    wait(late_loads + attn_loads)
    take_rows(0)
    mlp.onward()
    mlp.settle()
    finished = 0
    if inside and mlp.passed > depth:
        mlp.finish(0)
        finished = 1
    for copy in to_branch:
        copy.wait()
    for step in range(1, parts):
        take_rows(step)

    q_block = 256 if group <= 1024 else 128
    key_acc, value_acc = r.key_acc, r.value_acc
    query_t, key_t, value_t, cosine, sine = (
        r.query_t, r.key_t, r.value_t, r.cosine, r.sine
    )

    def one_kv_head(j):
        kv_rows = slice(j * HEAD_SIZE, (j + 1) * HEAD_SIZE)
        key_acc[...] = jnp.zeros_like(key_acc)
        value_acc[...] = jnp.zeros_like(value_acc)
        for member in range(members):
            first = (j * members + member) * HEAD_SIZE
            head = slice(first, first + HEAD_SIZE)
            for start in range(0, group, q_block):
                stop = start + q_block
                cols = slice(start, stop)
                query, grad = query_t[head, cols], grad_t[head, cols]
                key, value = key_t[kv_rows, :stop], value_t[kv_rows, :stop]
                scores = lax.dot_general(
                    query, key, (((0,), (0,)), ((), ())), preferred_element_type=F32
                )
                seen = r.id_col[cols, :] == r.id_row[:, :stop]
                at_row = start + lax.broadcasted_iota(jnp.int32, (q_block, stop), 0)
                at_col = lax.broadcasted_iota(jnp.int32, (q_block, stop), 1)
                scores = jnp.where(seen & (at_col <= at_row), scores * scale, MASKED)
                grown = jnp.exp(scores - jnp.max(scores, axis=-1, keepdims=True))
                probs = grown * (1.0 / jnp.sum(grown, axis=-1, keepdims=True))
                dprob = lax.dot_general(
                    grad, value, (((0,), (0,)), ((), ())), preferred_element_type=F32
                )
                inner = jnp.sum(probs * dprob, axis=-1, keepdims=True)
                dscore = (probs * (dprob - inner)).astype(BF16)
                key_acc[:, :stop] += jnp.dot(query, dscore, preferred_element_type=F32)
                value_acc[:, :stop] += jnp.dot(
                    grad, probs.astype(BF16), preferred_element_type=F32
                )
                dquery = scale * dot_nt(key, dscore)
                lead, tail = dquery[:half], dquery[half:]
                cos, sin = cosine[:, cols], sine[:, cols]
                grad_t[first : first + half, cols] = (lead * cos + tail * sin).astype(BF16)
                grad_t[first + half : first + HEAD_SIZE, cols] = (
                    tail * cos - lead * sin
                ).astype(BF16)
        lead, tail = key_acc[:half] * scale, key_acc[half:] * scale
        cos, sin = cosine[...], sine[...]
        first = q_width + j * HEAD_SIZE
        grad_t[first : first + half, :] = (lead * cos + tail * sin).astype(BF16)
        grad_t[first + half : first + HEAD_SIZE, :] = (tail * cos - lead * sin).astype(BF16)
        first = q_width + kv_width + j * HEAD_SIZE
        grad_t[first : first + HEAD_SIZE, :] = value_acc[...].astype(BF16)

    if not inside:
        mlp.onward()
    for j in range(kv_heads):
        one_kv_head(j)
        if not inside or j % 4 != 2:
            mlp.onward()

    def turn_back(i, carry):
        here = pl.ds(pl.multiple_of(i * 128, 128), 128)
        piece = grad_t[here, :].astype(F32).T.astype(BF16)
        for p in range(parts):
            branch[p, :, here] = piece[p * rows : (p + 1) * rows]
        return carry

    lax.fori_loop(0, all_width // 128, turn_back, 0)
    for copy in to_two:
        copy.wait_send()

    def incoming(step, here):
        return dot_nt(branch[mp_of(step), :, :all_width], weights[here, :])

    for step in range(1, parts):
        for first in range(0, width, 512):
            give_x[step - 1, :, first : first + 512] = incoming(
                step, slice(first, first + 512)
            ).astype(BF16)
    for copy in to_one:
        copy.start()
    mlp.onward()

    def attn_block(n):
        k = attn_order[n][0]
        lines = pl.ds(pl.multiple_of(attn.items[n][0] * 4 * quarter, 32), 4 * quarter)
        slot = attn.slot_for(n)

        def put(value, first):
            for i in range(4):
                slot[i // 2, i % 2, :, first : first + value.shape[1]] = value[
                    i * quarter : (i + 1) * quarter
                ].astype(BF16)

        if k == 0:
            wide = 512 if all_width % 512 == 0 else all_width
            for first in range(0, all_width, wide):
                put(dot_nt(normed_t[lines, :], grad_t[first : first + wide, :]), first)
        else:
            put(jnp.dot(branch_t[lines, :], attended[...], preferred_element_type=F32), 0)
        attn.items[n][3].start()

    for n in range(len(attn_order)):
        attn_block(n)
        if n >= 1:
            attn.cross()
        if n % 2 == 1 and not (inside and n < 2):
            mlp.onward()
    attn.cross()

    for copy in to_out:
        copy.wait_recv()
    if inside:
        for copy in to_out:
            copy.wait_send()
    out_tile, stored = r.out_tile, r.stored
    tile = out_tile.shape[1]
    for first in range(0, rows, tile):
        fetch = pltpu.make_async_copy(r.in_out.at[:, pl.ds(first, tile)], out_tile, stored.at[0])
        fetch.start()
        fetch.wait()
        for line in range(first, first + tile, 16):
            here = slice(line, line + 16)
            total = work_out[here, :]
            for step in range(parts - 1):
                total = total + out_tile[step, line - first : line - first + 16, :].astype(F32)
            low[here, :] = (residual[here, :] + total).astype(BF16)
    put_out = pltpu.make_async_copy(low, r.block_out, stored.at[1])
    put_out.start()
    for first in range(0, width, 512):
        work_out[:, first : first + 512] = incoming(0, slice(first, first + 512))
    mlp.onward()
    mlp.settle()
    put_out.wait()

    for copy in to_one:
        copy.wait_recv()

    def first_norm(here):
        total = work_out[here, :]
        for step in range(parts - 1):
            total = total + in_x[step, here, :].astype(F32)
        back, terms = norm_back(r.tokens[here, :].astype(F32), r.gain_one[...], total)
        held[0:8] += fold(terms)
        low[here, :] = (work[here, :] + back).astype(BF16)

    tiles(rows, TILE, first_norm)
    put_tokens = pltpu.make_async_copy(low, r.grad_tokens, stored.at[2])
    put_tokens.start()
    total_gains.begin()
    total_gains.advance()
    total_gains.advance()
    while mlp.passed < items:
        mlp.onward()
    mlp.settle()
    for n in range(len(attn_order) - 1):
        attn.onward()
        if finished < count:
            mlp.finish(finished)
            finished += 1
        if n == len(attn_order) - 4:
            total_gains.advance()
    attn.finish(0)
    attn.onward()
    total_gains.advance()
    r.gains[...] = held[64:80]
    attn.finish(1)
    put_tokens.wait()
    for copy in to_one + ([] if inside else to_out):
        copy.wait_send()
    mlp.drain()
    attn.drain()
    ring.drain()
    if attn_ring is not ring:
        attn_ring.drain()
    total_gains.drain()


def mlp_and_attn_widths(r, inside, chunks, out_width, all_width):
    if inside:
        widths = [r.mlp_w_in.shape[1] // chunks] * chunks
    else:
        widths = [r["grad%d" % k].shape[4] for k in range(3)]
    return widths, [all_width, out_width]


def backward(mlp_args, chunks, residual, cot, tokens, gain_one, gain_two, weights, out_w, normed_t,
             query_t, key_t, value_t, attended, ids, cosine, sine):
    depth, parts = lax.axis_size("dp") // 4, lax.axis_size("mp")
    rows, width = residual.shape
    group = rows * parts
    quarter = width // (4 * depth)
    heads, kv_heads = query_t.shape[0] // HEAD_SIZE, key_t.shape[0] // HEAD_SIZE
    inside = chunks > 0
    small = dict(
        gain_one=gain_one, gain_two=gain_two, id_col=ids[0], id_row=ids[1],
        cosine=cosine, sine=sine,
    )
    large = dict(
        residual_in=residual, cot_in=cot, tokens_in=tokens, weights_in=weights,
        out_w_in=out_w, normed_t_in=normed_t, query_t_in=query_t, key_t_in=key_t,
        value_t_in=value_t, attended_in=attended,
    )
    large.update(mlp_args)
    shapes = Named(large)
    mlp_widths, attn_widths = mlp_and_attn_widths(
        shapes, inside, chunks, attended.shape[1], weights.shape[1]
    )
    count = len(mlp_widths)
    struct = jax.ShapeDtypeStruct
    outs = {"mlp_out%d" % k: struct((quarter, w), F32) for k, w in enumerate(mlp_widths)}
    outs.update({"attn_out%d" % k: struct((quarter, w), F32) for k, w in enumerate(attn_widths)})
    rows_out = struct((rows, width), BF16)
    outs.update(
        block_out=rows_out, grad_tokens=rows_out, in_out=struct((parts - 1, rows, width), BF16)
    )
    for kind, widths in (("mlp", mlp_widths), ("attn", attn_widths)):
        landing = Sums.landing_shapes(depth, widths, quarter)
        for k in range(len(widths)):
            outs["%s_y%d" % (kind, k)] = landing[k]
            outs["%s_z%d" % (kind, k)] = landing[len(widths) + k]
    gains_out = dict(gains=struct((16, width), F32))

    def like(array):
        return pltpu.VMEM(array.shape, array.dtype)

    rows_f32, rows_low = pltpu.VMEM((rows, width), F32), pltpu.VMEM((rows, width), BF16)
    x_low = pltpu.VMEM((parts - 1, rows, width), BF16)
    stops = depth + parts
    scratch = dict(
        work=rows_f32, work_out=rows_f32, cot=like(cot), tokens=rows_low,
        normed_t=like(normed_t), query_t=like(query_t), key_t=like(key_t),
        value_t=like(value_t), attended=like(attended), in_x=x_low, give_x=x_low,
        out_tile=pltpu.VMEM((parts - 1, 64, width), BF16),
        branch=pltpu.VMEM((parts, rows, width), BF16),
        branch_t=pltpu.VMEM((width, group), BF16),
        grad_t=pltpu.VMEM((weights.shape[1], group), BF16),
        key_acc=pltpu.VMEM((HEAD_SIZE, group), F32),
        value_acc=pltpu.VMEM((HEAD_SIZE, group), F32),
        held=pltpu.VMEM((80, width), F32), around=pltpu.VMEM((16 * stops, width), F32),
        loaded=DMA((20 + chunks,)), stored=DMA((3,)), g_sent=DMA((stops,)), g_got=DMA((stops,)),
    )
    for name in ("two", "out", "branch", "one"):
        scratch[name + "_sent"] = scratch[name + "_got"] = DMA((parts - 1,))
    if inside:
        hidden = pltpu.VMEM((group, chunks * mlp_widths[0] // 3), BF16)
        others = pltpu.VMEM((parts - 1, rows, width), F32)
        scratch.update(
            wide=pltpu.VMEM((2, width, mlp_widths[0]), BF16),
            hidden=hidden, grad_gate=hidden, grad_up=hidden,
            others_two=others, others_out=others, give_out_low=x_low,
            ring=pltpu.VMEM((3, 2, 2, quarter, mlp_widths[0]), BF16),
        )
    else:
        scratch.update(
            residual=rows_f32, weights=like(weights), out_w=like(out_w),
            ring=pltpu.VMEM((6, 2, quarter, mlp_widths[0]), BF16),
            attn_ring=pltpu.VMEM((3, 2, 2, quarter, max(attn_widths)), BF16),
        )
    scratch.update(low=rows_low)
    for kind, widths in (("mlp", mlp_widths), ("attn", attn_widths)):
        for k, shape in enumerate(Sums.held_shapes(depth, widths, quarter)):
            scratch["%s_held%d" % (kind, k)] = shape
    names = list(large) + list(small) + list(outs) + list(gains_out) + list(scratch)
    kernel = functools.partial(
        backward_kernel, depth, parts, heads, kv_heads, chunks, names
    )
    results = pl.pallas_call(
        kernel,
        out_shape=list(outs.values()) + list(gains_out.values()),
        in_specs=[ANY_SPEC] * len(large) + [VMEM_SPEC] * len(small),
        out_specs=[ANY_SPEC] * len(outs) + [VMEM_SPEC],
        scratch_shapes=list(scratch.values())
        + Sums.tiles(depth, mlp_widths, quarter)
        + Sums.tiles(depth, attn_widths, quarter),
        compiler_params=pltpu.CompilerParams(
            collective_id=1, has_side_effects=True, vmem_limit_bytes=63 * 2**20
        ),
        name="backward",
    )(*large.values(), *small.values())
    return Named(zip(list(outs) + list(gains_out), results))


def own_and_give(whole, parts):
    me = lax.axis_index("mp")
    rows = whole.shape[0] // parts
    own = lax.dynamic_slice_in_dim(whole, me * rows, rows, 0)
    give = [
        lax.dynamic_slice_in_dim(whole, lax.rem(me + step, parts) * rows, rows, 0).astype(BF16)
        for step in range(1, parts)
    ]
    return own, jnp.stack(give)


def shards(
    tokens,
    seq_lengths,
    norm_attn,
    w_query,
    key_weight,
    value_weight,
    w_out,
    norm_mlp,
    w_gate,
    w_up,
    w_down,
    cotangent,
):
    parts = lax.axis_size("mp")
    rows = tokens.shape[0]
    group = rows * parts
    q_width, kv_width, hidden_width = w_query.shape[1], key_weight.shape[1], w_gate.shape[1]
    heads, kv_heads = q_width // HEAD_SIZE, kv_width // HEAD_SIZE
    members = heads // kv_heads
    factor = HEAD_SIZE ** (-0.5)

    width = tokens.shape[1]
    inputs = tokens.astype(F32)
    gain_one, gain_two = norm_attn.astype(F32), norm_mlp.astype(F32)
    chunks = hidden_width // 512 if group <= 512 and hidden_width % 512 == 0 else 0
    turned = w_down.T
    unit = hidden_width // max(chunks, 1)
    mlp_shard = jnp.concatenate(
        [
            part[:, k * unit : (k + 1) * unit]
            for k in range(max(chunks, 1))
            for part in (w_gate, w_up, turned)
        ],
        axis=1,
    )
    attn_w, out_wt, normed_one, grad_rows = gather_attn(
        (jnp.concatenate([w_query, key_weight, value_weight], axis=1), w_out.T),
        (rms_parts(inputs)[1] * gain_one).astype(BF16),
        cotangent,
    )
    mlp_shard, attn_w = lax.optimization_barrier((mlp_shard, attn_w))
    mlp_w = lax.all_gather(mlp_shard, "dp", axis=0, tiled=True)
    attn_w, out_wt = attn_w.reshape(width, -1), out_wt.reshape(width, -1)
    normed_one, grad_rows = normed_one.reshape(group, width), grad_rows.reshape(group, width)
    cuts = (q_width, q_width + kv_width)
    query_w, key_w, value_w = jnp.split(attn_w, cuts, axis=1)

    segment, position = layout(seq_lengths[0], group)
    cosine, sine = rotation(position)
    places = jnp.arange(group, dtype=jnp.int32)
    allowed = (
        (places[:, None] >= places[None, :])
        & (segment[:, None] == segment[None, :])
        & ((segment[None, :] >= 0) | (places[:, None] == places[None, :]))
    )

    query = rotate(mul(normed_one, query_w).reshape(group, heads, HEAD_SIZE), cosine, sine)
    key = rotate(mul(normed_one, key_w).reshape(group, kv_heads, HEAD_SIZE), cosine, sine)
    value = mul(normed_one, value_w).astype(BF16).reshape(group, kv_heads, HEAD_SIZE)
    query = query.astype(BF16).reshape(group, kv_heads, members, HEAD_SIZE)
    key = key.astype(BF16)
    scores = jnp.einsum("qhgd,khd->hgqk", query, key, preferred_element_type=F32) * factor
    scores = jnp.where(allowed[None, None], scores, MASKED)
    peak = jnp.max(scores, axis=-1, keepdims=True)
    grown = jnp.exp(scores - peak)
    probs = grown / jnp.sum(grown, axis=-1, keepdims=True)
    probs_low = probs.astype(BF16)
    attended = (
        jnp.einsum("hgqk,khd->qhgd", probs_low, value, preferred_element_type=F32)
        .astype(BF16)
        .reshape(group, q_width)
    )
    residual = inputs + mp_sum_rows(mul_t(attended, out_wt), parts)
    normed_two = mp_gather((rms_parts(residual)[1] * gain_two).astype(BF16), parts)

    if chunks:
        mlp_args = dict(
            mlp_w_in=mlp_w,
            normed_two_in=normed_two.reshape(parts, rows, width),
            normed_two_t_in=normed_two.T,
            cot_t_in=grad_rows.T,
        )
    else:
        gate_w, up_w, down_wt = jnp.split(mlp_w, 3, axis=1)
        gate_act, up_act = mul(normed_two, gate_w), mul(normed_two, up_w)
        sigmoid_g = jax.nn.sigmoid(gate_act)
        swish = gate_act * sigmoid_g
        hidden = (swish * up_act).astype(BF16)
        grad_hidden = mul(grad_rows, down_wt)
        grad_gate = (
            grad_hidden * up_act * sigmoid_g * (1.0 + gate_act * (1.0 - sigmoid_g))
        ).astype(BF16)
        grad_up = (grad_hidden * swish).astype(BF16)
        grads = (
            outer_sum(normed_two, grad_gate).astype(BF16),
            outer_sum(normed_two, grad_up).astype(BF16),
            outer_sum(grad_rows, hidden).astype(BF16),
        )
        depth = lax.axis_size("dp") // 4
        mlp_args = {
            "grad%d" % k: grad.reshape(depth, 2, 2, width // (4 * depth), -1)
            for k, grad in enumerate(grads)
        }
        own_two, give_two = own_and_give(
            mul_t(grad_gate, gate_w) + mul_t(grad_up, up_w), parts
        )
        own_out, give_out = own_and_give(mul_t(hidden, down_wt), parts)
        mlp_args.update(
            own_two_in=own_two, give_two=give_two, own_out_in=own_out, give_out=give_out
        )
    ids = jnp.where(segment >= 0, segment, 3 + places)
    done = backward(
        mlp_args,
        chunks,
        residual,
        grad_rows.reshape(parts, rows, width) if chunks else cotangent,
        tokens,
        gain_one[None, :],
        gain_two[None, :],
        attn_w,
        out_wt,
        normed_one.T,
        query.reshape(group, q_width).T,
        key.reshape(group, kv_width).T,
        value.reshape(group, kv_width).T,
        jnp.pad(attended, ((0, 0), (0, -q_width % 128))),
        (ids[:, None], ids[None, :]),
        cosine[:, 0, :].T,
        sine[:, 0, :].T,
    )
    block_out, grad_tokens = done.block_out, done.grad_tokens
    mlp_parts = [done["mlp_out%d" % k] for k in range(chunks or 3)]
    if chunks:
        mlp_parts = [
            jnp.concatenate(part, axis=1)
            for part in zip(*(jnp.split(piece, 3, axis=1) for piece in mlp_parts))
        ]
    grad_gate_w, grad_up_w, grad_down_w = mlp_parts
    attn_parts = jnp.split(done.attn_out0, cuts, axis=1) + [done.attn_out1[:, :q_width]]
    gains = jnp.sum(done.gains.reshape(2, 8, width), axis=1)
    return (
        block_out,
        grad_tokens,
        gains[0],
        attn_parts[0],
        attn_parts[1],
        attn_parts[2],
        attn_parts[3].T,
        gains[1],
        grad_gate_w,
        grad_up_w,
        grad_down_w.T,
    )


def solution(mesh):
    rows, whole = P(("dp", "mp"), None), P()
    split, turned = P("dp", "mp"), P("mp", "dp")
    return jax.shard_map(
        shards,
        mesh=mesh,
        in_specs=(
            rows, P("dp", None), whole, split, split, split, turned, whole, split, split, turned, rows,
        ),
        out_specs=(
            rows, rows, whole, split, split, split, turned, whole, split, split, turned,
        ),
        check_vma=False,
    )
```

```python
import functools

import jax
import jax.numpy as jnp
from jax import lax
from jax.experimental import pallas as pl
from jax.experimental.pallas import tpu as pltpu
from jax.sharding import PartitionSpec as P

HEAD_SIZE = 96
EPSILON = 1e-05
ROPE_BASE = 100000.0
MASKED = -1e30
F32 = jnp.float32
BF16 = jnp.bfloat16


def layout(lengths, rows_total):
    places = jnp.arange(rows_total, dtype=jnp.int32)
    first_end = lengths[0]
    middle_end = lengths[0] + lengths[1]
    last_end = middle_end + lengths[2]
    segment = jnp.where(
        places < first_end,
        0,
        jnp.where(places < middle_end, 1, jnp.where(places < last_end, 2, -1)),
    ).astype(jnp.int32)
    offset = jnp.where(places < first_end, 0, jnp.where(places < middle_end, first_end, middle_end))
    position = jnp.where(segment >= 0, places - offset, 0)
    return segment, position


def rotation(position):
    half_dim = HEAD_SIZE // 2
    inverse = ROPE_BASE ** (-jnp.arange(half_dim, dtype=F32) * 2.0 / HEAD_SIZE)
    angles = position.astype(F32)[:, None] * inverse[None, :]
    return jnp.cos(angles)[:, None, :], jnp.sin(angles)[:, None, :]


def rotate(tensor, cosine, sine):
    half_dim = tensor.shape[-1] // 2
    lead, tail = tensor[..., :half_dim], tensor[..., half_dim:]
    return jnp.concatenate([lead * cosine - tail * sine, tail * cosine + lead * sine], axis=-1)


def rms_parts(inputs):
    factor = lax.rsqrt(jnp.mean(inputs * inputs, axis=-1, keepdims=True) + EPSILON)
    return factor, inputs * factor


def mul(left, right):
    return jnp.dot(left, right, preferred_element_type=F32)


def mul_t(left, right):
    return lax.dot_general(left, right, (((1,), (1,)), ((), ())), preferred_element_type=F32)


def outer_sum(left, right):
    return lax.dot_general(left, right, (((0,), (0,)), ((), ())), preferred_element_type=F32)


def mp_shift(block, step, parts):
    return lax.ppermute(block, "mp", [(i, (i + step) % parts) for i in range(parts)])


def mp_gather(block, parts):
    me = lax.axis_index("mp")
    rows = block.shape[0]
    whole = jnp.zeros((parts * rows,) + block.shape[1:], block.dtype)
    for step in range(parts):
        piece = block if step == 0 else mp_shift(block, step, parts)
        owner = lax.rem(me - step + parts, parts)
        whole = lax.dynamic_update_slice_in_dim(whole, piece, owner * rows, 0)
    return whole


def mp_sum_rows(whole, parts):
    me = lax.axis_index("mp")
    rows = whole.shape[0] // parts
    total = lax.dynamic_slice_in_dim(whole, me * rows, rows, 0)
    for step in range(1, parts):
        owner = lax.rem(me + step, parts)
        piece = lax.dynamic_slice_in_dim(whole, owner * rows, rows, 0).astype(BF16)
        total = total + mp_shift(piece, step, parts).astype(F32)
    return total


MESH = pl.DeviceIdType.MESH
VMEM_SPEC = pl.BlockSpec(memory_space=pltpu.VMEM)
ANY_SPEC = pl.BlockSpec(memory_space=pl.ANY)
DMA = pltpu.SemaphoreType.DMA


def place(depth, parts):
    me, part = lax.axis_index("dp"), lax.axis_index("mp")
    z, y, core = me // 4, lax.rem(me // 2, 2), lax.rem(me, 2)

    def dp_of(step, at_y, at_core):
        return lax.rem(z + step, depth) * 4 + at_y * 2 + at_core

    def mp_of(step):
        return lax.rem(part + step, parts)

    return me, part, z, y, core, dp_of, mp_of


def flipped(value, mask):
    result = value
    for bit in (1 << i for i in range(mask.bit_length())):
        if mask & bit:
            result = result + bit * (1 - 2 * lax.rem(value // bit, 2))
    return result


def lowest(mask):
    return mask & -mask


def masks(depth):
    return sorted(range(1, depth), key=lambda m: (lowest(m), -m)) + [0]


def greet(depth, parts):
    me, part, z, y, core, dp_of, mp_of = place(depth, parts)
    near = [(dp_of(0, y, 1 - core), part), (dp_of(0, 1 - y, core), part)]
    near += [(dp_of(step, y, core), part) for step in range(1, depth)]
    near += [(me, mp_of(step)) for step in range(1, parts)]
    barrier = pltpu.get_barrier_semaphore()
    for device in near:
        pl.semaphore_signal(barrier, inc=1, device_id=device, device_id_type=MESH)
    pl.semaphore_wait(barrier, len(near))


def send(source, target, sems, at, device):
    sent, landed = sems
    return pltpu.make_async_remote_copy(
        src_ref=source,
        dst_ref=target,
        send_sem=sent.at[at],
        recv_sem=landed.at[at],
        device_id=device,
        device_id_type=MESH,
    )


class Gather:
    def __init__(self, depth, parts, shards, wholes, sems):
        self.depth, self.shards, self.wholes = depth, shards, wholes
        self.where = place(depth, parts)
        self.kept, self.z_sems, self.y_sems, self.c_sems = (
            sems[0], sems[1:3], sems[3:5], sems[5:7]
        )
        self.slots = 2 * depth - 1

    @staticmethod
    def semaphores(depth, count):
        slots = count * (2 * depth - 1)
        return [DMA((count,))] + [DMA((slots,))] * 4 + [DMA((2 * slots,))] * 2

    def block(self, i, move, at_y):
        me, part, z, y, core, dp_of, mp_of = self.where
        return self.wholes[i].at[(z + move) * 4 + at_y * 2 + core]

    def slot(self, move):
        return -move if move <= 0 else self.depth - 1 + move

    def source(self, i, move):
        return self.shards[i] if move == 0 else self.block(i, move, self.where[3])

    def along_z(self, i, move, ahead):
        me, part, z, y, core, dp_of, mp_of = self.where
        at = i * self.slots + self.slot(move - ahead)
        device = ((z + ahead) * 4 + y * 2 + core, part)
        return send(self.source(i, move), self.block(i, move, y), self.z_sems, at, device)

    def arrival(self, i, move):
        me, part, z, y, core, dp_of, mp_of = self.where
        at = i * self.slots + self.slot(move)
        block = self.block(i, move, y)
        return send(block, block, self.z_sems, at, (me, part))

    def along_y(self, i, move):
        me, part, z, y, core, dp_of, mp_of = self.where
        at = i * self.slots + self.slot(move)
        return send(self.source(i, move), self.block(i, move, y), self.y_sems, at,
                    (dp_of(0, 1 - y, core), part))

    def across(self, i, move, other):
        me, part, z, y, core, dp_of, mp_of = self.where
        at = 2 * (i * self.slots + self.slot(move)) + other
        at_y = 1 - y if other else y
        source = self.block(i, move, at_y) if other else self.source(i, move)
        return send(source, self.block(i, move, at_y), self.c_sems, at,
                    (dp_of(0, y, 1 - core), part))

    def there(self, move, action):
        z = self.where[2]
        if move == 0:
            action()
        else:
            pl.when((z + move >= 0) & (z + move < self.depth))(action)

    def begin(self, i):
        self.keep(i).start()
        for ahead in (1, -1):
            self.there(ahead, lambda ahead=ahead: self.along_z(i, 0, ahead).start())
        self.along_y(i, 0).start()
        self.across(i, 0, 0).start()

    def keep(self, i):
        return pltpu.make_async_copy(self.shards[i], self.wholes[i].at[self.where[0]],
                                     self.kept.at[i])

    def moves(self, step):
        return (0,) if step == 0 else (-step, step)

    def from_z(self, i, step):
        for move in self.moves(step):
            ahead = 1 if move < 0 else -1

            def pass_on(move=move, ahead=ahead):
                self.arrival(i, move).wait_recv()
                self.there(ahead, lambda: self.along_z(i, move, ahead).start())
                self.along_y(i, move).start()
                self.across(i, move, 0).start()

            self.there(move, pass_on)

    def from_y(self, i, step):
        for move in self.moves(step):

            def pass_on(move=move):
                self.along_y(i, move).wait_recv()
                self.across(i, move, 1).start()

            self.there(move, pass_on)

    def end(self, i):
        self.keep(i).wait()
        for step in range(self.depth):
            for move in self.moves(step):

                def settle(move=move):
                    self.across(i, move, 0).wait_recv()
                    self.across(i, move, 1).wait_recv()

                self.there(move, settle)

    def drain(self, i):
        for step in range(self.depth):
            for move in self.moves(step):

                def settle(move=move):
                    self.across(i, move, 0).wait_send()
                    self.across(i, move, 1).wait_send()
                    self.along_y(i, move).wait_send()
                    for ahead in (1, -1):
                        if move * ahead <= 0:
                            self.there(
                                ahead, lambda ahead=ahead: self.along_z(i, move, ahead).wait_send()
                            )

                self.there(move, settle)


def gather_kernel(depth, parts, count, *refs):
    shards, normed, cot = refs[:count], refs[count], refs[count + 1]
    weights = refs[count + 2 : 2 * count + 2]
    normed_all, cot_all, x_sent, x_got, kept = refs[2 * count + 2 : 2 * count + 7]
    me, part, z, y, core, dp_of, mp_of = place(depth, parts)
    work = Gather(depth, parts, shards, weights, refs[2 * count + 7 :])
    own = [
        pltpu.make_async_copy(normed, normed_all.at[part], kept.at[0]),
        pltpu.make_async_copy(cot, cot_all.at[part], kept.at[1]),
    ]
    greet(depth, parts)
    along_x = [
        send(source, target.at[part], (x_sent, x_got), i * (parts - 1) + step - 1,
             (me, mp_of(step)))
        for i, (source, target) in enumerate(((normed, normed_all), (cot, cot_all)))
        for step in range(1, parts)
    ]
    for i in range(count):
        work.begin(i)
    for copy in along_x + own:
        copy.start()
    for step in range(1, depth):
        for i in range(count):
            work.from_z(i, step)
        for i in range(count):
            work.from_y(i, step - 1)
    for i in range(count):
        work.from_y(i, depth - 1)
    for copy in along_x + own:
        copy.wait()
    for i in range(count):
        work.end(i)
    for i in range(count):
        work.drain(i)


def gather_attn(shards, normed, cot):
    depth, parts, count = lax.axis_size("dp") // 4, lax.axis_size("mp"), len(shards)
    size = depth * 4
    return pl.pallas_call(
        functools.partial(gather_kernel, depth, parts, count),
        out_shape=[jax.ShapeDtypeStruct((size,) + shard.shape, shard.dtype) for shard in shards]
        + [jax.ShapeDtypeStruct((parts,) + rows.shape, rows.dtype) for rows in (normed, cot)],
        in_specs=[VMEM_SPEC] * (count + 2),
        out_specs=[ANY_SPEC] * (count + 2),
        scratch_shapes=[DMA((2 * (parts - 1),))] * 2 + [DMA((2,))]
        + Gather.semaphores(depth, count),
        compiler_params=pltpu.CompilerParams(collective_id=0, has_side_effects=True),
        name="gather_attn",
    )(*shards, normed, cot)


def add_rows(target, sources):
    def body(i, carry):
        here = pl.ds(pl.multiple_of(i * 16, 16), 16)
        total = sources[0][here, :].astype(F32)
        for source in sources[1:]:
            total = total + source[here, :].astype(F32)
        target[here, :] = total.astype(target.dtype)
        return carry

    lax.fori_loop(0, target.shape[0] // 16, body, 0)


class Ring:
    def __init__(self, buffer):
        self.buffer, self.users, self.next = buffer, [None] * buffer.shape[0], 0

    def take(self, copy):
        slot = self.next
        if self.users[slot] is not None:
            self.users[slot].wait_send()
        self.users[slot] = copy
        self.next = (slot + 1) % len(self.users)

    def peek(self, ahead):
        return (self.next + ahead) % len(self.users)

    def drain(self):
        for copy in self.users:
            if copy is not None:
                copy.wait_send()


class Sums:
    def __init__(self, depth, parts, order, widths, rows, refs, wholes, ring, start, outs):
        self.depth, self.wholes, self.outs, self.order = depth, wholes, outs, order
        self.rows, self.widths, self.ring = rows, widths, ring
        count = len(widths)
        self.held = refs[:count]
        self.y_in, self.z_in = refs[count : 2 * count], refs[2 * count : 3 * count]
        self.y_tile, self.z_tile, self.stage = refs[3 * count : 3 * count + 3]
        self.sems = refs[3 * count + 3 :]
        self.where = place(depth, parts)
        slots = len(ring.users)
        self.slots = [(start + n) % slots for n in range(len(order))]
        self.items = [self.item(n) for n in range(len(order))]
        self.crossed = self.passed = 0
        self.pending = self.putting = None

    @staticmethod
    def held_shapes(depth, widths, rows):
        return [pltpu.VMEM((depth, 2, rows, width), BF16) for width in widths]

    @staticmethod
    def landing_shapes(depth, widths, rows):
        return [jax.ShapeDtypeStruct((depth, rows, width), BF16) for width in widths] + [
            jax.ShapeDtypeStruct((depth - 1, rows, width), BF16) for width in widths
        ]

    @staticmethod
    def tiles(depth, widths, rows):
        wide = max(widths)
        return [
            pltpu.VMEM((rows, wide), BF16),
            pltpu.VMEM((depth - 1, rows, wide), BF16),
            pltpu.VMEM((rows, wide), F32),
        ] + [DMA((depth * len(widths),))] * 7 + [DMA((depth + 2,))]

    def item(self, n):
        k, mask = self.order[n]
        me, part, z, y, core, dp_of, mp_of = self.where
        at = flipped(z, mask)
        kept, c_sent, c_got, y_sent, y_got, z_sent, z_got, moved = self.sems
        held, width = self.held[k], self.widths[k]
        every, slot = pl.ds(0, width), self.slots[n]
        own = None
        if self.wholes is None:
            give = self.ring.buffer.at[slot, :, 1 - core, :, every]
        else:
            give = self.wholes[k].at[at, :, 1 - core]
            own = pltpu.make_async_copy(
                self.wholes[k].at[at, :, core], self.ring.buffer.at[slot], kept.at[n]
            )
        across = send(give, held.at[at], (c_sent, c_got), n, (dp_of(0, y, 1 - core), part))
        along_y = send(
            held.at[at, 1 - y], self.y_in[k].at[at], (y_sent, y_got), n,
            (dp_of(0, 1 - y, core), part),
        )
        along_z = None
        if mask > 0:
            along_z = send(
                held.at[at, y], self.z_in[k].at[mask - 1], (z_sent, z_got), n,
                (flipped(z, lowest(mask)) * 4 + y * 2 + core, part),
            )
        return at, k, own, across, along_y, along_z

    def load(self, n):
        at, k, own, across, along_y, along_z = self.items[n]
        self.ring.take(across)
        own.start()
        across.start()

    def begin(self):
        self.ahead = min(len(self.ring.users), len(self.items))
        for n in range(self.ahead):
            self.load(n)

    def slot_for(self, n):
        self.ring.take(self.items[n][3])
        return self.ring.buffer.at[self.slots[n]]

    def cross(self):
        core = self.where[4]
        n = self.crossed
        self.crossed += 1
        at, k, own, across, along_y, along_z = self.items[n]
        if own is not None:
            own.wait()
        across.wait_recv()
        for at_y in range(2):
            if own is not None:
                mine = self.ring.buffer.at[self.slots[n], at_y]
            else:
                mine = self.ring.buffer.at[self.slots[n], at_y, core, :, pl.ds(0, self.widths[k])]
            held = self.held[k].at[at, at_y]
            add_rows(held, (mine, held))
        along_y.start()
        if own is not None and n + self.ahead < len(self.items):
            self.load(n + self.ahead)

    def onward(self):
        self.settle()
        n = self.passed
        if n >= self.crossed:
            return
        self.passed += 1
        moved = self.sems[7]
        at, k, own, across, along_y, along_z = self.items[n]
        mask, every = self.order[n][1], pl.ds(0, self.widths[k])
        along_y.wait_recv()
        tile = self.y_tile.at[:, every]
        fetches = [pltpu.make_async_copy(self.y_in[k].at[at], tile, moved.at[0])]
        fetches[0].start()
        tiles_in = [tile]
        if mask > 0:
            more, from_z = self.from_z(k, mask)
            fetches += more
            tiles_in += from_z
        self.pending = n, fetches, tiles_in

    def settle(self):
        if self.pending is None:
            return
        n, fetches, landed = self.pending
        self.pending = None
        at, k, own, across, along_y, along_z = self.items[n]
        for fetch in fetches:
            fetch.wait()
        held = self.held[k].at[at, self.where[3]]
        add_rows(held, [held] + landed)
        if along_z is not None:
            along_z.start()

    def from_z(self, k, mask):
        moved, every = self.sems[7], pl.ds(0, self.widths[k])
        fetches, landed = [], []
        bit = 1
        while bit < (lowest(mask) if mask else self.depth):
            sender = mask ^ bit
            self.items[self.order.index((k, sender))][5].wait_recv()
            tile = self.z_tile.at[len(landed), :, every]
            fetch = pltpu.make_async_copy(
                self.z_in[k].at[sender - 1], tile, moved.at[1 + len(landed)]
            )
            fetch.start()
            fetches.append(fetch)
            landed.append(tile)
            bit *= 2
        return fetches, landed

    def finish(self, k):
        self.settle()
        z, y = self.where[2:4]
        moved, every = self.sems[7], pl.ds(0, self.widths[k])
        fetches, landed = self.from_z(k, 0)
        for fetch in fetches:
            fetch.wait()
        stage = self.stage.at[:, every]
        if self.putting is not None:
            self.putting.wait()
        add_rows(stage, [self.held[k].at[z, y]] + landed)
        self.putting = pltpu.make_async_copy(stage, self.outs[k], moved.at[self.depth + 1])
        self.putting.start()

    def drain(self):
        self.putting.wait()
        for at, k, own, across, along_y, along_z in self.items:
            along_y.wait_send()
            if along_z is not None:
                along_z.wait_send()


class Gains:
    def __init__(self, depth, parts, held, around, sems):
        me, part, z, y, core, dp_of, mp_of = place(depth, parts)
        self.held = held
        stages = [
            [(dp_of(0, y, 1 - core), part)],
            [(me, mp_of(step)) for step in range(1, parts)],
            [(dp_of(step, y, core), part) for step in range(1, depth)],
            [(dp_of(0, 1 - y, core), part)],
        ]
        self.levels, slot = [], 0
        for number, stage in enumerate(stages):
            copies = []
            for device in stage:
                landing = around.at[pl.ds(16 * slot, 16)]
                source = held.at[pl.ds(16 * number, 16)]
                copies.append((send(source, landing, sems, slot, device), landing))
                slot += 1
            self.levels.append(copies)
        self.number = 0

    def begin(self):
        for copy, landing in self.levels[self.number]:
            copy.start()

    def advance(self):
        number = self.number
        if number == len(self.levels):
            return
        total = self.held[16 * number : 16 * number + 16]
        for copy, landing in self.levels[number]:
            copy.wait_recv()
            total = total + landing[...]
        self.held[16 * (number + 1) : 16 * (number + 2)] = total
        self.number += 1
        if self.number < len(self.levels):
            self.begin()

    def drain(self):
        for level in self.levels:
            for copy, landing in level:
                copy.wait_send()


def norm_back(rows_in, gain, gradient):
    factor = lax.rsqrt(jnp.mean(rows_in * rows_in, axis=-1, keepdims=True) + EPSILON)
    normed = rows_in * factor
    scaled = gradient * gain
    back = factor * (scaled - normed * jnp.mean(scaled * normed, axis=-1, keepdims=True))
    return back, gradient * normed


TILE = 16


def fold(terms):
    total = terms[0:8]
    for at in range(8, terms.shape[0], 8):
        total = total + terms[at : at + 8]
    return total


def tiles(rows, tile, body):
    def run(i, carry):
        body(pl.ds(pl.multiple_of(i * tile, tile), tile))
        return carry

    lax.fori_loop(0, rows // tile, run, 0, unroll=4)


def dot_nt(left, right):
    return lax.dot_general(
        left, right, (((1,), (1,)), ((), ())), preferred_element_type=F32
    )


class Named(dict):
    __getattr__ = dict.get


def backward_kernel(depth, parts, heads, kv_heads, chunks, names, *refs):
    r = Named(zip(names, refs))
    rest = refs[len(names) :]
    me, part, z, y, core, dp_of, mp_of = place(depth, parts)
    work, work_out, residual = r.work, r.work_out, r.residual
    branch, branch_t, grad_t = r.branch, r.branch_t, r.grad_t
    in_x, give_x, low, held = r.in_x, r.give_x, r.low, r.held
    weights, out_w, normed_t, attended = (
        r.weights, r.out_w, r.normed_t, r.attended
    )
    rows, width = work.shape
    group = rows * parts
    members = heads // kv_heads
    q_width, kv_width = heads * HEAD_SIZE, kv_heads * HEAD_SIZE
    all_width = q_width + 2 * kv_width
    half = HEAD_SIZE // 2
    scale = HEAD_SIZE ** (-0.5)
    quarter = width // (4 * depth)
    inside = chunks > 0
    if inside:
        weights, out_w = r.wide.at[0], r.wide.at[1, :, pl.ds(0, q_width)]
        residual = r.others_two.at[0]

    mlp_widths, attn_widths = mlp_and_attn_widths(
        r, inside, chunks, r.attended_in.shape[1], all_width
    )
    count = len(mlp_widths)
    if inside:
        mlp_order = [(k, mask) for k in range(count) for mask in masks(depth)]
        ring = attn_ring = Ring(r.ring)
        attn_start = len(mlp_order) % len(ring.users)
        wholes = None
    else:
        mlp_order = [(k, mask) for mask in masks(depth) for k in range(count)]
        ring, attn_ring, attn_start = Ring(r.ring), Ring(r.attn_ring), 0
        wholes = [r["grad%d" % k] for k in range(count)]
    attn_order = [(k, mask) for mask in masks(depth) for k in range(2)]
    mlp_refs = (
        [r["mlp_held%d" % k] for k in range(count)]
        + [r["mlp_y%d" % k] for k in range(count)]
        + [r["mlp_z%d" % k] for k in range(count)]
        + list(rest[:11])
    )
    attn_refs = (
        [r["attn_held%d" % k] for k in range(2)]
        + [r["attn_y%d" % k] for k in range(2)]
        + [r["attn_z%d" % k] for k in range(2)]
        + list(rest[11:22])
    )
    mlp = Sums(depth, parts, mlp_order, mlp_widths, quarter, mlp_refs, wholes, ring, 0,
               [r["mlp_out%d" % k] for k in range(count)])
    attn = Sums(depth, parts, attn_order, attn_widths, quarter, attn_refs, None, attn_ring,
                attn_start, [r["attn_out%d" % k] for k in range(2)])
    total_gains = Gains(depth, parts, held, r.around, (r.g_sent, r.g_got))

    loading = [0]

    def load(source, target):
        copy = pltpu.make_async_copy(source, target, r.loaded.at[loading[0]])
        loading[0] += 1
        copy.start()
        return copy

    def wait(copies):
        for copy in copies:
            copy.wait()

    def along_x(source, target, name):
        sems = (r[name + "_sent"], r[name + "_got"])
        return [
            send(source(step), target(step), sems, step - 1, (me, mp_of(step)))
            for step in range(1, parts)
        ]

    give_two = give_x if inside else r.give_two
    give_out = r.give_out_low if inside else r.give_out
    to_two = along_x(lambda s: give_two.at[s - 1], lambda s: in_x.at[s - 1], "two")
    to_out = along_x(lambda s: give_out.at[s - 1], lambda s: r.in_out.at[s - 1], "out")
    to_branch = along_x(lambda s: branch.at[part], lambda s: branch.at[part], "branch")
    to_one = along_x(lambda s: give_x.at[s - 1], lambda s: in_x.at[s - 1], "one")

    if inside:
        hidden_width = mlp_widths[0] // 3
        gate_cols, up_cols, down_cols = (
            slice(i * hidden_width, (i + 1) * hidden_width) for i in range(3)
        )

        def load_chunk(k):
            lanes = pl.ds(k * 3 * hidden_width, 3 * hidden_width)
            return load(r.mlp_w_in.at[:, lanes], r.wide.at[k % 2])

        def load_part(i):
            lanes = pl.ds(i * hidden_width, hidden_width)
            return load(r.mlp_w_in.at[:, lanes], r.wide.at[0, :, lanes])

        first_loads = [load(r.normed_two_in, branch), load_part(0), load_part(1)]
        next_loads = [load(r.cot_in, r.cot), load_part(2)]
        block_loads = [load(r.normed_two_t_in, branch_t), load(r.cot_t_in, normed_t)]
        chunk_loads = [None]
        if chunks > 1:
            chunk_loads.append(load_chunk(1))
        greet(depth, parts)
        late_loads = [
            load(r.query_t_in, r.query_t), load(r.key_t_in, r.key_t),
            load(r.value_t_in, r.value_t), load(r.attended_in, attended),
            load(r.tokens_in, r.tokens),
        ]
        wait(first_loads)

        def add_to(own, others, k, product):
            for step in range(parts):
                target = own if step == 0 else others.at[step - 1]
                value = product(step)
                if k == 0:
                    target[...] = value
                else:
                    target[...] += value

        hidden, grad_gate, grad_up = r.hidden, r.grad_gate, r.grad_up

        def feed_forward(k):
            if k > 0:
                chunk_loads[k].wait()
            wide = r.wide.at[k % 2]
            here = slice(k * hidden_width, (k + 1) * hidden_width)
            for p in range(parts):
                lines = slice(p * rows, (p + 1) * rows)
                gate = jnp.dot(branch[p], wide[:, gate_cols], preferred_element_type=F32)
                up = jnp.dot(branch[p], wide[:, up_cols], preferred_element_type=F32)
                if k == 0 and p == 0:
                    wait(next_loads)
                back = jnp.dot(r.cot[p], wide[:, down_cols], preferred_element_type=F32)
                sigmoid = 1.0 / (1.0 + jnp.exp(-gate))
                swish = gate * sigmoid
                hidden[lines, here] = (swish * up).astype(BF16)
                grad_gate[lines, here] = (
                    back * up * sigmoid * (1.0 + gate * (1.0 - sigmoid))
                ).astype(BF16)
                grad_up[lines, here] = (back * swish).astype(BF16)

            if k == 0:
                wait(block_loads)
                make_blocks(depth)
                mlp.cross()

            def lines_of(step):
                return pl.ds(pl.multiple_of(mp_of(step) * rows, rows), rows)

            add_to(
                work, r.others_two, k,
                lambda step: dot_nt(grad_gate[lines_of(step), here], wide[:, gate_cols])
                + dot_nt(grad_up[lines_of(step), here], wide[:, up_cols]),
            )
            add_to(
                work_out, r.others_out, k,
                lambda step: dot_nt(hidden[lines_of(step), here], wide[:, down_cols]),
            )
            if k + 2 < chunks:
                chunk_loads.append(load_chunk(k + 2))

        def mlp_block(n):
            k = mlp_order[n][0]
            here = slice(k * hidden_width, (k + 1) * hidden_width)
            at = mlp.items[n][0]
            lines = pl.ds(pl.multiple_of(at * 4 * quarter, 32), 4 * quarter)
            slot = mlp.slot_for(n)
            for value, cols in (
                (jnp.dot(branch_t[lines, :], grad_gate[:, here], preferred_element_type=F32),
                 gate_cols),
                (jnp.dot(branch_t[lines, :], grad_up[:, here], preferred_element_type=F32),
                 up_cols),
                (jnp.dot(normed_t[lines, :], hidden[:, here], preferred_element_type=F32),
                 down_cols),
            ):
                for i in range(4):
                    slot[i // 2, i % 2, :, cols] = value[
                        i * quarter : (i + 1) * quarter
                    ].astype(BF16)
            mlp.items[n][3].start()

        made = [0]

        def make_blocks(stop):
            while made[0] < stop:
                mlp_block(made[0])
                made[0] += 1
                if made[0] >= 2:
                    mlp.cross()

        for k in range(chunks):
            feed_forward(k)
            if k > 0:
                mlp.onward()
        for step in range(1, parts):
            give_x[step - 1] = r.others_two[step - 1].astype(BF16)
            give_out[step - 1] = r.others_out[step - 1].astype(BF16)
        for copy in to_two:
            copy.start()
        residual_load = load(r.residual_in, residual)
        attn_loads = [load(r.weights_in, weights), load(r.out_w_in, out_w)]
        total_blocks = len(mlp_order)

        def more_blocks(stop):
            while made[0] < min(stop, total_blocks):
                mlp_block(made[0])
                made[0] += 1
                if made[0] - mlp.crossed == 2 or made[0] == total_blocks:
                    mlp.cross()
                if made[0] % 3 == 0:
                    mlp.onward()

        more_blocks(3 * depth)
        wait([residual_load])
        own_cot = r.cot.at[part]
    else:
        greet(depth, parts)
        for copy in to_two:
            copy.start()
        mlp.begin()
        first_loads = [
            load(r.own_two_in, work), load(r.residual_in, residual),
            load(r.cot_in, r.cot),
        ]
        late_loads = [
            load(r[name + "_in"], r[name])
            for name in ("out_w", "query_t", "key_t", "value_t", "weights", "normed_t",
                         "attended", "tokens")
        ] + [load(r.own_out_in, work_out)]
        attn_loads = []
        for n in range(min(8, len(mlp_order))):
            mlp.cross()
        wait(first_loads)
        own_cot = r.cot
    items = len(mlp_order)
    mlp.settle()
    for copy in to_two:
        copy.wait_recv()

    held[0:16] = jnp.zeros((16, width), F32)

    def second(here):
        total = work[here, :]
        for step in range(parts - 1):
            total = total + in_x[step, here, :].astype(F32)
        back, terms = norm_back(residual[here, :], r.gain_two[...], total)
        held[8:16] += fold(terms)
        result = own_cot[here, :].astype(F32) + back
        work[here, :] = result
        branch[part, here, :] = result.astype(BF16)

    tiles(rows, TILE, second)
    for copy in to_branch + to_out:
        copy.start()
    if inside:
        more_blocks(total_blocks)
        attn_loads.append(load(r.normed_t_in, normed_t))
    while mlp.crossed < items:
        mlp.cross()
    block = 256 if q_width % 256 == 0 else q_width

    def take_rows(step):
        p = mp_of(step)
        across = pl.ds(pl.multiple_of(p * rows, rows), rows)
        for first in range(0, q_width, block):
            piece = jnp.dot(
                branch[p], out_w[:, first : first + block], preferred_element_type=F32
            )
            grad_t[first : first + block, across] = piece.T.astype(BF16)

        def turn(i, carry):
            here = pl.ds(pl.multiple_of(i * 128, 128), 128)
            branch_t[here, across] = branch[p, :, here].astype(F32).T.astype(BF16)
            return carry

        lax.fori_loop(0, width // 128, turn, 0, unroll=3)

    wait(late_loads + attn_loads)
    take_rows(0)
    mlp.onward()
    mlp.settle()
    finished = 0
    if inside and mlp.passed > depth:
        mlp.finish(0)
        finished = 1
    for copy in to_branch:
        copy.wait()
    for step in range(1, parts):
        take_rows(step)

    q_block = 256 if group <= 1024 else 128
    key_acc, value_acc = r.key_acc, r.value_acc
    query_t, key_t, value_t, cosine, sine = (
        r.query_t, r.key_t, r.value_t, r.cosine, r.sine
    )

    def one_kv_head(j):
        kv_rows = slice(j * HEAD_SIZE, (j + 1) * HEAD_SIZE)
        key_acc[...] = jnp.zeros_like(key_acc)
        value_acc[...] = jnp.zeros_like(value_acc)
        for member in range(members):
            first = (j * members + member) * HEAD_SIZE
            head = slice(first, first + HEAD_SIZE)
            for start in range(0, group, q_block):
                stop = start + q_block
                cols = slice(start, stop)
                query, grad = query_t[head, cols], grad_t[head, cols]
                key, value = key_t[kv_rows, :stop], value_t[kv_rows, :stop]
                scores = lax.dot_general(
                    query, key, (((0,), (0,)), ((), ())), preferred_element_type=F32
                )
                seen = r.id_col[cols, :] == r.id_row[:, :stop]
                at_row = start + lax.broadcasted_iota(jnp.int32, (q_block, stop), 0)
                at_col = lax.broadcasted_iota(jnp.int32, (q_block, stop), 1)
                scores = jnp.where(seen & (at_col <= at_row), scores * scale, MASKED)
                grown = jnp.exp(scores - jnp.max(scores, axis=-1, keepdims=True))
                probs = grown * (1.0 / jnp.sum(grown, axis=-1, keepdims=True))
                dprob = lax.dot_general(
                    grad, value, (((0,), (0,)), ((), ())), preferred_element_type=F32
                )
                inner = jnp.sum(probs * dprob, axis=-1, keepdims=True)
                dscore = (probs * (dprob - inner)).astype(BF16)
                key_acc[:, :stop] += jnp.dot(query, dscore, preferred_element_type=F32)
                value_acc[:, :stop] += jnp.dot(
                    grad, probs.astype(BF16), preferred_element_type=F32
                )
                dquery = scale * dot_nt(key, dscore)
                lead, tail = dquery[:half], dquery[half:]
                cos, sin = cosine[:, cols], sine[:, cols]
                grad_t[first : first + half, cols] = (lead * cos + tail * sin).astype(BF16)
                grad_t[first + half : first + HEAD_SIZE, cols] = (
                    tail * cos - lead * sin
                ).astype(BF16)
        lead, tail = key_acc[:half] * scale, key_acc[half:] * scale
        cos, sin = cosine[...], sine[...]
        first = q_width + j * HEAD_SIZE
        grad_t[first : first + half, :] = (lead * cos + tail * sin).astype(BF16)
        grad_t[first + half : first + HEAD_SIZE, :] = (tail * cos - lead * sin).astype(BF16)
        first = q_width + kv_width + j * HEAD_SIZE
        grad_t[first : first + HEAD_SIZE, :] = value_acc[...].astype(BF16)

    if not inside:
        mlp.onward()
    for j in range(kv_heads):
        one_kv_head(j)
        if not inside or j % 4 != 2:
            mlp.onward()

    def turn_back(i, carry):
        here = pl.ds(pl.multiple_of(i * 128, 128), 128)
        piece = grad_t[here, :].astype(F32).T.astype(BF16)
        for p in range(parts):
            branch[p, :, here] = piece[p * rows : (p + 1) * rows]
        return carry

    lax.fori_loop(0, all_width // 128, turn_back, 0, unroll=3)
    for copy in to_two:
        copy.wait_send()

    def incoming(step, here):
        return dot_nt(branch[mp_of(step), :, :all_width], weights[here, :])

    for step in range(1, parts):
        for first in range(0, width, 512):
            give_x[step - 1, :, first : first + 512] = incoming(
                step, slice(first, first + 512)
            ).astype(BF16)
    for copy in to_one:
        copy.start()
    mlp.onward()

    def attn_block(n):
        k = attn_order[n][0]
        lines = pl.ds(pl.multiple_of(attn.items[n][0] * 4 * quarter, 32), 4 * quarter)
        slot = attn.slot_for(n)

        def put(value, first):
            for i in range(4):
                slot[i // 2, i % 2, :, first : first + value.shape[1]] = value[
                    i * quarter : (i + 1) * quarter
                ].astype(BF16)

        if k == 0:
            wide = 512 if all_width % 512 == 0 else all_width
            for first in range(0, all_width, wide):
                put(dot_nt(normed_t[lines, :], grad_t[first : first + wide, :]), first)
        else:
            put(jnp.dot(branch_t[lines, :], attended[...], preferred_element_type=F32), 0)
        attn.items[n][3].start()

    for n in range(len(attn_order)):
        attn_block(n)
        if n >= 1:
            attn.cross()
        if n % 2 == 1 and not (inside and n < 2):
            mlp.onward()
    attn.cross()

    for copy in to_out:
        copy.wait_recv()
    if inside:
        for copy in to_out:
            copy.wait_send()
    out_tile, stored = r.out_tile, r.stored
    tile = out_tile.shape[1]
    for first in range(0, rows, tile):
        fetch = pltpu.make_async_copy(r.in_out.at[:, pl.ds(first, tile)], out_tile, stored.at[0])
        fetch.start()
        fetch.wait()
        for line in range(first, first + tile, 16):
            here = slice(line, line + 16)
            total = work_out[here, :]
            for step in range(parts - 1):
                total = total + out_tile[step, line - first : line - first + 16, :].astype(F32)
            low[here, :] = (residual[here, :] + total).astype(BF16)
    put_out = pltpu.make_async_copy(low, r.block_out, stored.at[1])
    put_out.start()
    for first in range(0, width, 512):
        work_out[:, first : first + 512] = incoming(0, slice(first, first + 512))
    mlp.onward()
    mlp.settle()
    put_out.wait()

    for copy in to_one:
        copy.wait_recv()

    def first_norm(here):
        total = work_out[here, :]
        for step in range(parts - 1):
            total = total + in_x[step, here, :].astype(F32)
        back, terms = norm_back(r.tokens[here, :].astype(F32), r.gain_one[...], total)
        held[0:8] += fold(terms)
        low[here, :] = (work[here, :] + back).astype(BF16)

    tiles(rows, TILE, first_norm)
    put_tokens = pltpu.make_async_copy(low, r.grad_tokens, stored.at[2])
    put_tokens.start()
    total_gains.begin()
    total_gains.advance()
    total_gains.advance()
    while mlp.passed < items:
        mlp.onward()
    mlp.settle()
    for n in range(len(attn_order) - 1):
        attn.onward()
        if finished < count:
            mlp.finish(finished)
            finished += 1
        if n == len(attn_order) - 4:
            total_gains.advance()
    attn.finish(0)
    attn.onward()
    total_gains.advance()
    r.gains[...] = held[64:80]
    attn.finish(1)
    put_tokens.wait()
    for copy in to_one + ([] if inside else to_out):
        copy.wait_send()
    mlp.drain()
    attn.drain()
    ring.drain()
    if attn_ring is not ring:
        attn_ring.drain()
    total_gains.drain()


def mlp_and_attn_widths(r, inside, chunks, out_width, all_width):
    if inside:
        widths = [r.mlp_w_in.shape[1] // chunks] * chunks
    else:
        widths = [r["grad%d" % k].shape[4] for k in range(3)]
    return widths, [all_width, out_width]


def backward(mlp_args, chunks, residual, cot, tokens, gain_one, gain_two, weights, out_w, normed_t,
             query_t, key_t, value_t, attended, ids, cosine, sine):
    depth, parts = lax.axis_size("dp") // 4, lax.axis_size("mp")
    rows, width = residual.shape
    group = rows * parts
    quarter = width // (4 * depth)
    heads, kv_heads = query_t.shape[0] // HEAD_SIZE, key_t.shape[0] // HEAD_SIZE
    inside = chunks > 0
    small = dict(
        gain_one=gain_one, gain_two=gain_two, id_col=ids[0], id_row=ids[1],
        cosine=cosine, sine=sine,
    )
    large = dict(
        residual_in=residual, cot_in=cot, tokens_in=tokens, weights_in=weights,
        out_w_in=out_w, normed_t_in=normed_t, query_t_in=query_t, key_t_in=key_t,
        value_t_in=value_t, attended_in=attended,
    )
    large.update(mlp_args)
    shapes = Named(large)
    mlp_widths, attn_widths = mlp_and_attn_widths(
        shapes, inside, chunks, attended.shape[1], weights.shape[1]
    )
    count = len(mlp_widths)
    struct = jax.ShapeDtypeStruct
    outs = {"mlp_out%d" % k: struct((quarter, w), F32) for k, w in enumerate(mlp_widths)}
    outs.update({"attn_out%d" % k: struct((quarter, w), F32) for k, w in enumerate(attn_widths)})
    rows_out = struct((rows, width), BF16)
    outs.update(
        block_out=rows_out, grad_tokens=rows_out, in_out=struct((parts - 1, rows, width), BF16)
    )
    for kind, widths in (("mlp", mlp_widths), ("attn", attn_widths)):
        landing = Sums.landing_shapes(depth, widths, quarter)
        for k in range(len(widths)):
            outs["%s_y%d" % (kind, k)] = landing[k]
            outs["%s_z%d" % (kind, k)] = landing[len(widths) + k]
    gains_out = dict(gains=struct((16, width), F32))

    def like(array):
        return pltpu.VMEM(array.shape, array.dtype)

    rows_f32, rows_low = pltpu.VMEM((rows, width), F32), pltpu.VMEM((rows, width), BF16)
    x_low = pltpu.VMEM((parts - 1, rows, width), BF16)
    stops = depth + parts
    scratch = dict(
        work=rows_f32, work_out=rows_f32, cot=like(cot), tokens=rows_low,
        normed_t=like(normed_t), query_t=like(query_t), key_t=like(key_t),
        value_t=like(value_t), attended=like(attended), in_x=x_low, give_x=x_low,
        out_tile=pltpu.VMEM((parts - 1, 64, width), BF16),
        branch=pltpu.VMEM((parts, rows, width), BF16),
        branch_t=pltpu.VMEM((width, group), BF16),
        grad_t=pltpu.VMEM((weights.shape[1], group), BF16),
        key_acc=pltpu.VMEM((HEAD_SIZE, group), F32),
        value_acc=pltpu.VMEM((HEAD_SIZE, group), F32),
        held=pltpu.VMEM((80, width), F32), around=pltpu.VMEM((16 * stops, width), F32),
        loaded=DMA((20 + chunks,)), stored=DMA((3,)), g_sent=DMA((stops,)), g_got=DMA((stops,)),
    )
    for name in ("two", "out", "branch", "one"):
        scratch[name + "_sent"] = scratch[name + "_got"] = DMA((parts - 1,))
    if inside:
        hidden = pltpu.VMEM((group, chunks * mlp_widths[0] // 3), BF16)
        others = pltpu.VMEM((parts - 1, rows, width), F32)
        scratch.update(
            wide=pltpu.VMEM((2, width, mlp_widths[0]), BF16),
            hidden=hidden, grad_gate=hidden, grad_up=hidden,
            others_two=others, others_out=others, give_out_low=x_low,
            ring=pltpu.VMEM((3, 2, 2, quarter, mlp_widths[0]), BF16),
        )
    else:
        scratch.update(
            residual=rows_f32, weights=like(weights), out_w=like(out_w),
            ring=pltpu.VMEM((6, 2, quarter, mlp_widths[0]), BF16),
            attn_ring=pltpu.VMEM((3, 2, 2, quarter, max(attn_widths)), BF16),
        )
    scratch.update(low=rows_low)
    for kind, widths in (("mlp", mlp_widths), ("attn", attn_widths)):
        for k, shape in enumerate(Sums.held_shapes(depth, widths, quarter)):
            scratch["%s_held%d" % (kind, k)] = shape
    names = list(large) + list(small) + list(outs) + list(gains_out) + list(scratch)
    kernel = functools.partial(
        backward_kernel, depth, parts, heads, kv_heads, chunks, names
    )
    results = pl.pallas_call(
        kernel,
        out_shape=list(outs.values()) + list(gains_out.values()),
        in_specs=[ANY_SPEC] * len(large) + [VMEM_SPEC] * len(small),
        out_specs=[ANY_SPEC] * len(outs) + [VMEM_SPEC],
        scratch_shapes=list(scratch.values())
        + Sums.tiles(depth, mlp_widths, quarter)
        + Sums.tiles(depth, attn_widths, quarter),
        compiler_params=pltpu.CompilerParams(
            collective_id=1, has_side_effects=True, vmem_limit_bytes=63 * 2**20
        ),
        name="backward",
    )(*large.values(), *small.values())
    return Named(zip(list(outs) + list(gains_out), results))


def own_and_give(whole, parts):
    me = lax.axis_index("mp")
    rows = whole.shape[0] // parts
    own = lax.dynamic_slice_in_dim(whole, me * rows, rows, 0)
    give = [
        lax.dynamic_slice_in_dim(whole, lax.rem(me + step, parts) * rows, rows, 0).astype(BF16)
        for step in range(1, parts)
    ]
    return own, jnp.stack(give)


def shards(
    tokens,
    seq_lengths,
    norm_attn,
    w_query,
    key_weight,
    value_weight,
    w_out,
    norm_mlp,
    w_gate,
    w_up,
    w_down,
    cotangent,
):
    parts = lax.axis_size("mp")
    rows = tokens.shape[0]
    group = rows * parts
    q_width, kv_width, hidden_width = w_query.shape[1], key_weight.shape[1], w_gate.shape[1]
    heads, kv_heads = q_width // HEAD_SIZE, kv_width // HEAD_SIZE
    members = heads // kv_heads
    factor = HEAD_SIZE ** (-0.5)

    width = tokens.shape[1]
    inputs = tokens.astype(F32)
    gain_one, gain_two = norm_attn.astype(F32), norm_mlp.astype(F32)
    chunks = hidden_width // 512 if group <= 512 and hidden_width % 512 == 0 else 0
    turned = w_down.T
    unit = hidden_width // max(chunks, 1)
    mlp_shard = jnp.concatenate(
        [
            part[:, k * unit : (k + 1) * unit]
            for k in range(max(chunks, 1))
            for part in (w_gate, w_up, turned)
        ],
        axis=1,
    )
    attn_w, out_wt, normed_one, grad_rows = gather_attn(
        (jnp.concatenate([w_query, key_weight, value_weight], axis=1), w_out.T),
        (rms_parts(inputs)[1] * gain_one).astype(BF16),
        cotangent,
    )
    mlp_shard, attn_w = lax.optimization_barrier((mlp_shard, attn_w))
    mlp_w = lax.all_gather(mlp_shard, "dp", axis=0, tiled=True)
    attn_w, out_wt = attn_w.reshape(width, -1), out_wt.reshape(width, -1)
    normed_one, grad_rows = normed_one.reshape(group, width), grad_rows.reshape(group, width)
    cuts = (q_width, q_width + kv_width)
    query_w, key_w, value_w = jnp.split(attn_w, cuts, axis=1)

    segment, position = layout(seq_lengths[0], group)
    cosine, sine = rotation(position)
    places = jnp.arange(group, dtype=jnp.int32)
    allowed = (
        (places[:, None] >= places[None, :])
        & (segment[:, None] == segment[None, :])
        & ((segment[None, :] >= 0) | (places[:, None] == places[None, :]))
    )

    query = rotate(mul(normed_one, query_w).reshape(group, heads, HEAD_SIZE), cosine, sine)
    key = rotate(mul(normed_one, key_w).reshape(group, kv_heads, HEAD_SIZE), cosine, sine)
    value = mul(normed_one, value_w).astype(BF16).reshape(group, kv_heads, HEAD_SIZE)
    query = query.astype(BF16).reshape(group, kv_heads, members, HEAD_SIZE)
    key = key.astype(BF16)
    scores = jnp.einsum("qhgd,khd->hgqk", query, key, preferred_element_type=F32) * factor
    scores = jnp.where(allowed[None, None], scores, MASKED)
    peak = jnp.max(scores, axis=-1, keepdims=True)
    grown = jnp.exp(scores - peak)
    probs = grown / jnp.sum(grown, axis=-1, keepdims=True)
    probs_low = probs.astype(BF16)
    attended = (
        jnp.einsum("hgqk,khd->qhgd", probs_low, value, preferred_element_type=F32)
        .astype(BF16)
        .reshape(group, q_width)
    )
    residual = inputs + mp_sum_rows(mul_t(attended, out_wt), parts)
    normed_two = mp_gather((rms_parts(residual)[1] * gain_two).astype(BF16), parts)

    if chunks:
        mlp_args = dict(
            mlp_w_in=mlp_w,
            normed_two_in=normed_two.reshape(parts, rows, width),
            normed_two_t_in=normed_two.T,
            cot_t_in=grad_rows.T,
        )
    else:
        gate_w, up_w, down_wt = jnp.split(mlp_w, 3, axis=1)
        gate_act, up_act = mul(normed_two, gate_w), mul(normed_two, up_w)
        sigmoid_g = jax.nn.sigmoid(gate_act)
        swish = gate_act * sigmoid_g
        hidden = (swish * up_act).astype(BF16)
        grad_hidden = mul(grad_rows, down_wt)
        grad_gate = (
            grad_hidden * up_act * sigmoid_g * (1.0 + gate_act * (1.0 - sigmoid_g))
        ).astype(BF16)
        grad_up = (grad_hidden * swish).astype(BF16)
        grads = (
            outer_sum(normed_two, grad_gate).astype(BF16),
            outer_sum(normed_two, grad_up).astype(BF16),
            outer_sum(grad_rows, hidden).astype(BF16),
        )
        depth = lax.axis_size("dp") // 4
        mlp_args = {
            "grad%d" % k: grad.reshape(depth, 2, 2, width // (4 * depth), -1)
            for k, grad in enumerate(grads)
        }
        own_two, give_two = own_and_give(
            mul_t(grad_gate, gate_w) + mul_t(grad_up, up_w), parts
        )
        own_out, give_out = own_and_give(mul_t(hidden, down_wt), parts)
        mlp_args.update(
            own_two_in=own_two, give_two=give_two, own_out_in=own_out, give_out=give_out
        )
    ids = jnp.where(segment >= 0, segment, 3 + places)
    done = backward(
        mlp_args,
        chunks,
        residual,
        grad_rows.reshape(parts, rows, width) if chunks else cotangent,
        tokens,
        gain_one[None, :],
        gain_two[None, :],
        attn_w,
        out_wt,
        normed_one.T,
        query.reshape(group, q_width).T,
        key.reshape(group, kv_width).T,
        value.reshape(group, kv_width).T,
        jnp.pad(attended, ((0, 0), (0, -q_width % 128))),
        (ids[:, None], ids[None, :]),
        cosine[:, 0, :].T,
        sine[:, 0, :].T,
    )
    block_out, grad_tokens = done.block_out, done.grad_tokens
    mlp_parts = [done["mlp_out%d" % k] for k in range(chunks or 3)]
    if chunks:
        mlp_parts = [
            jnp.concatenate(part, axis=1)
            for part in zip(*(jnp.split(piece, 3, axis=1) for piece in mlp_parts))
        ]
    grad_gate_w, grad_up_w, grad_down_w = mlp_parts
    attn_parts = jnp.split(done.attn_out0, cuts, axis=1) + [done.attn_out1[:, :q_width]]
    gains = jnp.sum(done.gains.reshape(2, 8, width), axis=1)
    return (
        block_out,
        grad_tokens,
        gains[0],
        attn_parts[0],
        attn_parts[1],
        attn_parts[2],
        attn_parts[3].T,
        gains[1],
        grad_gate_w,
        grad_up_w,
        grad_down_w.T,
    )


def solution(mesh):
    rows, whole = P(("dp", "mp"), None), P()
    split, turned = P("dp", "mp"), P("mp", "dp")
    return jax.shard_map(
        shards,
        mesh=mesh,
        in_specs=(
            rows, P("dp", None), whole, split, split, split, turned, whole, split, split, turned, rows,
        ),
        out_specs=(
            rows, rows, whole, split, split, split, turned, whole, split, split, turned,
        ),
        check_vma=False,
    )
```
